32 devices in a mesh: blk: 4 (over y, x), exp: 8 (over z, core).
Axes of the slice: x: 2, y: 2, z: 4, core: 2. Of those that a mesh axis runs over, the one named last changes fastest.
Arguments:
- tokens: bfloat16 [16, 1024, 768], P('exp', 'blk'), may hold values from -6 to 6
- output_grad: bfloat16 [16, 1024, 768], P('exp', 'blk'), may hold values from -6 to 6
- expert_index: int32 [4, 16, 256, 1], P('blk', 'exp'), may hold values from 0 to 7; in each aligned block of 512 rows (0 to 511, 512 to 1023, ..., all dimensions but the last counted through in order) at most 80 rows name the same one
- query_weight: bfloat16 [768, 768], replicated, may hold values from -0.21875 to 0.21875
- key_weight: bfloat16 [768, 768], replicated, may hold values from -0.21875 to 0.21875
- value_weight: bfloat16 [768, 768], replicated, may hold values from -0.21875 to 0.21875
- output_weight: bfloat16 [768, 768], replicated, may hold values from -3.5 to 3.5
- router_weight: bfloat16 [768, 8], replicated, may hold values from -0.15625 to 0.15625
- expert_in: bfloat16 [8, 768, 3072], P('exp'), may hold values from -0.21875 to 0.21875
- expert_out: bfloat16 [8, 3072, 768], P('exp'), may hold values from -0.21875 to 0.21875
- norm1_gain: float32 [768], replicated, may hold values from 0.5 to 1.5
- norm1_bias: float32 [768], replicated, may hold values from -3 to 3
- norm2_gain: float32 [768], replicated, may hold values from 0.5 to 1.5
- norm2_bias: float32 [768], replicated, may hold values from -3 to 3
Outputs:
- output: bfloat16 [16, 1024, 768], P('exp', 'blk')
- balance_loss: float32 [], replicated
- grad_tokens: bfloat16 [16, 1024, 768], P('exp', 'blk')
- grad_query: float32 [768, 768], replicated
- grad_key: float32 [768, 768], replicated
- grad_value: float32 [768, 768], replicated
- grad_output: float32 [768, 768], replicated
- grad_router: float32 [768, 8], replicated
- grad_expert_in: float32 [8, 768, 3072], P('exp', None, 'blk')
- grad_expert_out: float32 [8, 3072, 768], P('exp', 'blk')
- grad_norm1_gain: float32 [768], replicated
- grad_norm1_bias: float32 [768], replicated
- grad_norm2_gain: float32 [768], replicated
- grad_norm2_bias: float32 [768], replicated
The draws below stay inside these ranges and needn't reach their ends.
Inputs may be any that keep to these rules, and one draw needn't show every extreme that they name: `expert_index`: in each aligned block of 512 rows (the tokens of one device, in order of sequence, then position) no expert is named more than 80 times, a bound that some block reaches.
All inputs are finite; a program needn't handle non-finite values.
Results may differ from the reference program's by a relative error of at most 0.023.
Values may be sent and summed in bfloat16 or wider, within the bound.
A program may use at most 256 MiB of HBM per device.

```python
import math
import jax
import jax.numpy as jnp
import numpy as np
from jax import lax

D = 768
HEADS = 12
HEAD_DIM = 64
FF = 3072
SEQ_LEN = 1024
TOK_DEV = 512
SPAN = 256
SEQS = 2
BATCH = 16
EXPERTS = 8
CAP = 80
TOKENS = 16384
N_BLK = 4
N_EXP = 8


def block_levels(rng, extent, split, low, largest):
    loudness, own = 1.0, jax.random.fold_in(rng, 6)
    for dim, shards_of in split:
        heights = jnp.exp(jax.random.uniform(jax.random.fold_in(own, dim), (shards_of,), jnp.float32, low / len(split), largest / len(split)))
        loudness = loudness * jnp.repeat(heights, extent[dim] // shards_of).reshape([-1 if axis == dim else 1 for axis in range(len(extent))])
    return loudness


def assign_block(rng, own, number, rows, number_of, top, reach, lean):
    order = jax.random.permutation(rng, number_of)
    packed, usual = shares(number_of, rows * top, reach, lean, True), shares(number_of, rows * top, reach, lean, False)
    places = jnp.arange(number_of)

    def named(lengths, turn):
        used = int((lengths > 0).sum())
        fixed = max(1, used // 4)
        moved = fixed + (places - fixed + turn * (used - fixed)) % max(1, number_of - fixed)
        return jnp.zeros((number_of,), jnp.int32).at[order[jnp.where(places < fixed, places, moved)]].set(jnp.asarray(lengths, jnp.int32))

    lengths = jnp.where(number % 4 == 0, named(packed, number // 4), named(usual, number - number // 4 - 1))
    mixed = jax.random.permutation(jax.random.fold_in(own, 3), number_of)
    source_of, taker = mixed[0:number_of // 2 * 2:2], mixed[1:number_of // 2 * 2:2]
    slack = jnp.minimum(lengths[source_of] - 1, reach - lengths[taker]) // 2
    slack = jnp.where((source_of == order[0]) | (taker == order[0]) | (lengths[taker] == 0), 0, jnp.maximum(slack, 0))
    moved = jax.random.randint(jax.random.fold_in(own, 4), (number_of // 2,), 0, 1 << 20) % (slack + 1)
    lengths = lengths.at[source_of].add(-moved).at[taker].add(moved)
    members = jnp.searchsorted(jnp.cumsum(lengths), jnp.arange(rows * top), side="right").astype(jnp.int32)
    table = members.reshape(top, rows).T
    table = table[jax.random.permutation(jax.random.fold_in(own, 1), rows)]
    turn = jax.random.randint(jax.random.fold_in(own, 2), (rows, 1), 0, top)
    return jnp.take_along_axis(table, (jnp.arange(top)[None, :] + turn) % top, axis=1)


def shares(amount, total, reach, lean, full):
    portions = [(1 << 20) // math.isqrt(rank ** lean) + 1 for rank in range(1, amount + 1)]
    largest = reach if full else min(reach, max(-(-total // amount), total * portions[0] // sum(portions)))
    least = 1 if total - largest >= amount - 1 else 0
    given, spare = [largest] + [least] * (amount - 1), total - largest - least * (amount - 1)
    while spare > 0:
        free = [i for i in range(1, amount) if given[i] < largest] or [i for i in range(1, amount) if given[i] < reach]
        mass, remaining = sum([portions[i] for i in free]), spare
        for i in free:
            more = min(reach - given[i], max(1, remaining * portions[i] // mass), spare)
            given[i] = given[i] + more
            spare = spare - more
    return np.array(given)


def noise(own_key, dims, spread, limit, pieces=(), held_as=jnp.bfloat16):
    entries = spread * jax.random.normal(own_key, dims, jnp.float32)
    if pieces:
        entries = entries * block_levels(own_key, dims, pieces, -0.22, 0.18)
    return jnp.clip(entries, -limit, limit).astype(held_as)


def setup_inputs(seed: int = 0) -> dict:
    streams_of = jax.random.split(jax.random.key(seed), 15)
    tokens = noise(streams_of[0], (BATCH, SEQ_LEN, D), 1.0, 6.0, ((0, 8), (1, 4)))
    output_grad = noise(streams_of[1], (BATCH, SEQ_LEN, D), 1.0, 6.0, ((0, 8), (1, 4)))
    expert_index_keys = jax.random.split(jax.random.fold_in(streams_of[2], 1), N_BLK * BATCH * SPAN // TOK_DEV)
    expert_index_turns = jax.random.permutation(jax.random.fold_in(streams_of[2], 3), N_BLK * BATCH * SPAN // TOK_DEV)
    expert_index = jax.vmap(lambda own, number: assign_block(jax.random.fold_in(streams_of[2], 2), own, number, TOK_DEV, EXPERTS, 1, CAP, 1))(expert_index_keys, expert_index_turns).reshape((N_BLK, BATCH, SPAN, 1))
    query_weight = noise(streams_of[3], (D, D), D ** -0.5, 0.21875)
    key_weight = noise(streams_of[4], (D, D), D ** -0.5, 0.21875)
    value_weight = noise(streams_of[5], (D, D), D ** -0.5, 0.21875)
    output_weight = noise(streams_of[6], (D, D), (max(1, 4 * D // SEQ_LEN)) ** -0.5, 3.5)
    router_weight = noise(streams_of[7], (D, EXPERTS), (2 * D) ** -0.5, 0.15625)
    expert_in = noise(streams_of[8], (EXPERTS, D, FF), D ** -0.5, 0.21875, ((0, 8),))
    expert_out = noise(streams_of[9], (EXPERTS, FF, D), (FF // 4) ** -0.5, 0.21875, ((0, 8),))
    norm1_gain = jnp.clip(1.0 + 0.1 * jax.random.normal(streams_of[10], (D,), jnp.float32), 0.5, 1.5)
    norm1_bias = noise(streams_of[11], (D,), 0.5, 3.0, (), jnp.float32)
    norm2_gain = jnp.clip(1.0 + 0.1 * jax.random.normal(streams_of[12], (D,), jnp.float32), 0.5, 1.5)
    norm2_bias = noise(streams_of[13], (D,), 0.5, 3.0, (), jnp.float32)
    return dict(tokens=tokens, output_grad=output_grad, expert_index=expert_index, query_weight=query_weight, key_weight=key_weight, value_weight=value_weight, output_weight=output_weight, router_weight=router_weight, expert_in=expert_in, expert_out=expert_out, norm1_gain=norm1_gain, norm1_bias=norm1_bias, norm2_gain=norm2_gain, norm2_bias=norm2_bias)


HIGH = lax.Precision.HIGHEST
EPSILON = 1e-05
FLOOR_SCORE = -1e+30

@jax.custom_vjp
def low(v):
    return lax.optimization_barrier(v.astype(jnp.bfloat16)).astype(jnp.float32)

@jax.custom_vjp
def low_back(v):
    return v

def low_keep(v):
    return (low(v), None)

def low_pass(kept, grad):
    return (grad,)

def back_keep(v):
    return (v, None)

def back_low(kept, grad):
    return (low(grad),)
low.defvjp(low_keep, low_pass)
low_back.defvjp(back_keep, back_low)

def layer_norm(inputs, gain_row, bias_row):
    centered = inputs - lax.optimization_barrier(jnp.mean(inputs, axis=-1, keepdims=True))
    variance = lax.optimization_barrier(jnp.mean(centered * centered, axis=-1, keepdims=True))
    return centered * lax.rsqrt(variance + EPSILON) * gain_row + bias_row

def attend_group(group):
    queries, key_rows, value_rows = group
    raw_scores = jnp.einsum('gqhd,gkhd->ghqk', queries, key_rows, precision=HIGH) * HEAD_DIM ** (-0.5)
    scores = low_back(raw_scores)
    places = jnp.arange(SEQ_LEN, dtype=jnp.int32)
    visible = places[None, :] <= places[:, None]
    chances = jax.nn.softmax(jnp.where(visible, scores, FLOOR_SCORE), axis=-1)
    return jnp.einsum('ghqk,gkhd->gqhd', low(chances), value_rows, precision=HIGH)

def to_blocks(values):
    shaped = values.reshape(N_EXP, SEQS, N_BLK, SPAN, D)
    return shaped.transpose(2, 0, 1, 3, 4).reshape(N_BLK, N_EXP, TOK_DEV, D)

def from_blocks(values):
    shaped = values.reshape(N_BLK, N_EXP, SEQS, SPAN, D)
    return shaped.transpose(1, 2, 0, 3, 4).reshape(BATCH, SEQ_LEN, D)

def reference(tokens, output_grad, expert_index, query_weight, key_weight, value_weight, output_weight, router_weight, expert_in, expert_out, norm1_gain, norm1_bias, norm2_gain, norm2_bias):
    routing_dev = expert_index.reshape(N_BLK, N_EXP, TOK_DEV).astype(jnp.int32)
    hot_dev = (routing_dev[..., None] == jnp.arange(EXPERTS, dtype=jnp.int32)).astype(jnp.int32)
    slot_dev = lax.optimization_barrier(jnp.sum((jnp.cumsum(hot_dev, axis=2).astype(jnp.int32) - hot_dev) * hot_dev, axis=-1)).astype(jnp.int32)
    counts = lax.optimization_barrier(jnp.sum(hot_dev, axis=(0, 1, 2)))
    routing_tok = expert_index.reshape(N_BLK, N_EXP, SEQS, SPAN).transpose(1, 2, 0, 3).reshape(BATCH, SEQ_LEN)
    onehot = (routing_tok[..., None] == jnp.arange(EXPERTS, dtype=jnp.int32)).astype(jnp.float32)
    mean_load = TOKENS / EXPERTS
    load_weight = lax.optimization_barrier(jnp.sum(onehot * ((counts.astype(jnp.float32) - mean_load) / mean_load), axis=-1))
    source_rows = jnp.arange(N_EXP, dtype=jnp.int32)[:, None]

    def forward(inputs, w_query, w_key, w_value, w_output, w_router, w_in, w_out, gain_one, bias_one, gain_two, bias_two):
        normed_one = low(layer_norm(inputs, gain_one, bias_one))

        def project(matrix):
            return low(low_back(jnp.einsum('bld,de->ble', normed_one, matrix, precision=HIGH)))
        head_shape = (BATCH // SEQS, SEQS, SEQ_LEN, HEADS, HEAD_DIM)
        grouped = (project(w_query).reshape(head_shape), project(w_key).reshape(head_shape), project(w_value).reshape(head_shape))
        attended = lax.map(jax.checkpoint(attend_group), grouped)
        mixed = low(low_back(attended.reshape(BATCH, SEQ_LEN, D)))
        hidden_one = inputs + low_back(jnp.einsum('bld,de->ble', mixed, w_output, precision=HIGH))
        normed_two = low(layer_norm(hidden_one, gain_two, bias_two))
        logits = low_back(jnp.einsum('bld,de->ble', normed_two, w_router, precision=HIGH))
        gate_value = jax.nn.sigmoid(lax.optimization_barrier(jnp.sum(logits * onehot, axis=-1)))

        def expert_block(block):
            block_rows, block_routing, block_slots = block
            filled = jnp.zeros((N_EXP, EXPERTS, CAP, D), jnp.float32).at[source_rows, block_routing, block_slots].set(block_rows)
            filled = low_back(filled)
            before = low_back(jnp.einsum('secd,edf->secf', filled, w_in, precision=HIGH))
            activated = low(jax.nn.gelu(before))
            produced = low(low_back(jnp.einsum('secf,efd->secd', activated, w_out, precision=HIGH)))
            return produced[source_rows, block_routing, block_slots]
        returned = lax.map(jax.checkpoint(expert_block), (to_blocks(normed_two), routing_dev, slot_dev))
        hidden_two = hidden_one + gate_value[..., None] * from_blocks(returned)
        balance = jnp.sum(load_weight * gate_value) / TOKENS
        return (hidden_two, balance)
    floats = (tokens.astype(jnp.float32), query_weight.astype(jnp.float32), key_weight.astype(jnp.float32), value_weight.astype(jnp.float32), output_weight.astype(jnp.float32), router_weight.astype(jnp.float32), expert_in.astype(jnp.float32), expert_out.astype(jnp.float32), norm1_gain.astype(jnp.float32), norm1_bias.astype(jnp.float32), norm2_gain.astype(jnp.float32), norm2_bias.astype(jnp.float32))
    (hidden_two, balance), pullback = jax.vjp(forward, *floats)
    grads = pullback((output_grad.astype(jnp.float32), jnp.ones((), jnp.float32)))
    return (hidden_two.astype(jnp.bfloat16), balance, grads[0].astype(jnp.bfloat16), grads[1], grads[2], grads[3], grads[4], grads[5], grads[6], grads[7], grads[8], grads[9], grads[10], grads[11])
```

```python
import functools

import jax
import jax.numpy as jnp
from jax import lax
from jax.experimental import pallas as pl
from jax.experimental.pallas import tpu as pltpu
from jax.sharding import PartitionSpec as P

HEAD_DIM = 64
PAIR = 2 * HEAD_DIM
EPSILON = 1e-05
SCALE = HEAD_DIM ** (-0.5)
QUERY_ROWS = 256
ROWS = 128
FF_COLS = 256
MESH = pl.DeviceIdType.MESH
BF16, F32 = jnp.bfloat16, jnp.float32
VMEM_BYTES = 62 << 20
NT = (((1,), (1,)), ((), ()))
TN = (((0,), (0,)), ((), ()))


def dot(left, right, dims=(((1,), (0,)), ((), ()))):
    return lax.dot_general(left, right, dims, preferred_element_type=F32)


def iota(shape, dim):
    return lax.broadcasted_iota(jnp.int32, shape, dim)


def normalize(values):
    centered = values - jnp.mean(values, axis=-1, keepdims=True)
    variance = jnp.mean(centered * centered, axis=-1, keepdims=True)
    inverse = lax.rsqrt(variance + EPSILON)
    return centered * inverse, inverse


def norm_back(hat, inverse, gain, grad):
    scaled = grad * gain
    return inverse * (
        scaled
        - jnp.mean(scaled, axis=-1, keepdims=True)
        - hat * jnp.mean(scaled * hat, axis=-1, keepdims=True)
    )


def split_rows(base, size):
    return pl.ds(pl.multiple_of(base, size), size)


class Place:
    def __init__(self, cfg):
        self.__dict__.update(cfg)
        self.b = lax.axis_index("blk")
        self.e = lax.axis_index("exp")
        self.c = lax.rem(self.e, 2)
        self.pair = self.e - self.c
        self.sibling = self.pair + 1 - self.c

    def greet(self):
        bar = pltpu.get_barrier_semaphore()

        def exp_peer(k, _):
            pl.semaphore_signal(
                bar, 1, device_id=(self.b, lax.rem(self.e + k, self.ne)), device_id_type=MESH
            )

        def blk_peer(k, _):
            there = lax.rem(self.b + k, self.nb)
            pl.semaphore_signal(bar, 1, device_id=(there, self.e), device_id_type=MESH)
            pl.semaphore_signal(bar, 1, device_id=(there, self.sibling), device_id_type=MESH)

        lax.fori_loop(1, self.ne, exp_peer, None)
        lax.fori_loop(1, self.nb, blk_peer, None)
        pl.semaphore_wait(bar, self.ne - 1 + 2 * (self.nb - 1))

    def is_me(self, there):
        return there[0] * self.ne + there[1] == self.b * self.ne + self.e


def remote(src, dst, send_sem, recv_sem, there):
    return pltpu.make_async_remote_copy(
        src, dst, send_sem, recv_sem, device_id=there, device_id_type=MESH
    )


def push(me, src, dst, send_sem, recv_sem, there):
    mine = me.is_me(there)

    @pl.when(mine)
    def _():
        pltpu.make_async_copy(src, dst, recv_sem).start()

    @pl.when(jnp.logical_not(mine))
    def _():
        remote(src, dst, send_sem, recv_sem, there).start()


def push_done(me, src, dst, send_sem, recv_sem, there):
    @pl.when(jnp.logical_not(me.is_me(there)))
    def _():
        remote(src, dst, send_sem, recv_sem, there).wait_send()


def landed(dst, recv_sem):
    pltpu.make_async_copy(dst, dst, recv_sem).wait()


def exchange_start(me, src, dst, send_sem, recv_sem, size):
    def one(k, _):
        there = lax.rem(me.e + k, me.ne)
        remote(
            src.at[split_rows(there * size, size)],
            dst.at[split_rows(me.e * size, size)],
            send_sem.at[k],
            recv_sem.at[k],
            (me.b, there),
        ).start()

    own = split_rows(me.e * size, size)
    pltpu.make_async_copy(src.at[own], dst.at[own], recv_sem.at[0]).start()
    lax.fori_loop(1, me.ne, one, None)


def exchange_wait(me, src, dst, send_sem, recv_sem, size):
    own = split_rows(me.e * size, size)
    landed(dst.at[own], recv_sem.at[0])

    def one(k, _):
        source = lax.rem(me.e + me.ne - k, me.ne)
        landed(dst.at[split_rows(source * size, size)], recv_sem.at[k])

    lax.fori_loop(1, me.ne, one, None)


def exchange_sent(me, src, dst, send_sem, recv_sem, size):
    def one(k, _):
        there = lax.rem(me.e + k, me.ne)
        remote(
            src.at[split_rows(there * size, size)],
            dst.at[split_rows(me.e * size, size)],
            send_sem.at[k],
            recv_sem.at[k],
            (me.b, there),
        ).wait_send()

    lax.fori_loop(1, me.ne, one, None)


def token_slots(me, idx):
    rows = idx.shape[0]
    hot = (idx == iota((rows, 128), 1)).astype(F32)
    earlier = (iota((rows, rows), 1) < iota((rows, rows), 0)).astype(F32).astype(BF16)
    ahead = dot(earlier, hot.astype(BF16))
    slot = jnp.sum(ahead * hot, axis=1, keepdims=True)
    return idx.astype(F32) * me.cap + slot, jnp.sum(hot, axis=0, keepdims=True)


def slots_by_token(me, slot):
    rows = slot.shape[0]
    across = jnp.transpose(jnp.broadcast_to(slot, (rows, 128)))[0:1, :]
    slots = me.experts * me.cap
    return (iota((slots, rows), 0) == across.astype(jnp.int32)).astype(F32).astype(BF16)


def tokens_by_slot(me, slot):
    rows = slot.shape[0]
    slots = me.experts * me.cap
    return (iota((rows, slots), 1) == slot.astype(jnp.int32)).astype(F32).astype(BF16)


def head_masks():
    lane = iota((1, PAIR), 1)
    first = (lane < HEAD_DIM).astype(F32).astype(BF16)
    second = (lane >= HEAD_DIM).astype(F32).astype(BF16)
    return first, second


def attend_kernel(
    cfg,
    x, og, idx, gain, bias, wq, wk, wv,
    q, k, v, a, lse, o, dh, cnt,
    w, xin, o_send, lse_cols, dh_send, cnt_exp, cnt_part, cnt_blk,
    wsem, xs, xr, fs, fr, os, orr, ds, dr, cs, cr, bs, br,
):
    me = Place(cfg)
    half = me.span // 2
    columns = pl.ds(pl.multiple_of(me.c * me.half_width, 128), me.half_width)
    loads = [
        pltpu.make_async_copy(m.at[:, columns], w.at[j], wsem.at[j])
        for j, m in enumerate((wq, wk, wv))
    ]
    for load in loads:
        load.start()
    me.greet()

    def row_moves():
        for s in range(me.seqs):
            for h in range(2):
                there = (me.c * me.seqs + s, me.pair + h)
                yield (
                    x.at[pl.ds(s * me.span + h * half, half)],
                    xin.at[me.b],
                    xs.at[2 * s + h],
                    xr.at[me.b],
                    there,
                )

    for move in row_moves():
        push(me, *move)

    slot, counts = token_slots(me, idx[...])
    dh_send[...] = dot(slots_by_token(me, slot), og[...]).astype(BF16)
    exchange_start(me, dh_send, dh, ds, dr, me.cap)
    cnt_part[...] = jnp.broadcast_to(counts, cnt_part.shape)
    own = me.e
    pltpu.make_async_copy(cnt_part, cnt_exp.at[own], cr.at[0]).start()

    def count_move(j):
        return remote(
            cnt_part, cnt_exp.at[me.e], cs.at[j], cr.at[j], (me.b, lax.rem(me.e + j, me.ne))
        )

    lax.fori_loop(1, me.ne, lambda j, _: count_move(j).start(), None)

    def forward_move(j):
        rows = split_rows(j * me.span + me.c * half, half)
        return remote(a.at[rows], a.at[rows], fs.at[j], fr.at[j], (me.b, me.sibling))

    for j in range(me.nb):
        landed(xin.at[j], xr.at[j])
        hat, _ = normalize(xin[j].astype(F32))
        a[split_rows(j * me.span + me.c * half, half), :] = (
            hat * gain[...] + bias[...]
        ).astype(BF16)
        forward_move(j).start()

    landed(cnt_exp.at[me.e], cr.at[0])
    lax.fori_loop(
        1,
        me.ne,
        lambda j, _: landed(cnt_exp.at[lax.rem(me.e + me.ne - j, me.ne)], cr.at[j]),
        None,
    )
    lax.fori_loop(1, me.ne, lambda j, _: count_move(j).wait_send(), None)
    cnt_blk[me.b] = jnp.sum(cnt_exp[...], axis=0)

    def blk_move(j):
        return remote(
            cnt_blk.at[me.b],
            cnt_blk.at[me.b],
            bs.at[j],
            br.at[j],
            (lax.rem(me.b + j, me.nb), me.e),
        )

    for j in range(1, me.nb):
        blk_move(j).start()

    for load in loads:
        load.wait()
    first, second = head_masks()
    blocks = me.length // QUERY_ROWS
    spans = QUERY_ROWS // me.span
    lane = iota((1, PAIR), 1)
    visible = iota((QUERY_ROWS, QUERY_ROWS), 1) <= iota((QUERY_ROWS, QUERY_ROWS), 0)
    source = me.pair + lax.div(me.b, me.seqs)

    def o_move(j):
        return (
            o_send.at[pl.ds(j * me.span, me.span)],
            o.at[split_rows(lax.rem(me.b, me.seqs) * me.span, me.span), columns],
            os.at[j],
            orr.at[2 * lax.rem(me.b, me.seqs) + me.c],
            (j, source),
        )

    for i in range(blocks):
        for j in range(i * spans, (i + 1) * spans):
            theirs = split_rows(j * me.span + (1 - me.c) * half, half)
            landed(a.at[theirs], fr.at[j])
        here = pl.ds(i * QUERY_ROWS, QUERY_ROWS)
        rows = a[here, :]
        q[here, :] = dot(rows, w[0]).astype(BF16) * jnp.asarray(SCALE, BF16)
        k[here, :] = dot(rows, w[1]).astype(BF16)
        v[here, :] = dot(rows, w[2]).astype(BF16)

        def pair_of_heads(p, _, i=i, here=here):
            lanes = split_rows(p * PAIR, PAIR)
            queries = q[here, lanes]
            parts = [pl.ds(i * QUERY_ROWS, QUERY_ROWS)]
            if i:
                parts.append(pl.ds(0, i * QUERY_ROWS))
            done = []
            for h, mask in enumerate((first, second)):
                masked = queries * mask
                scores = [dot(masked, k[part, lanes], NT) for part in parts]
                scores[0] = jnp.where(visible, scores[0], -1e30)
                peak = functools.reduce(
                    jnp.maximum, [jnp.max(s, axis=1, keepdims=True) for s in scores]
                )
                powers = [jnp.exp(s - peak) for s in scores]
                total = sum(jnp.sum(s, axis=1, keepdims=True) for s in powers)
                mixed = sum(dot(s.astype(BF16), v[part, lanes]) for s, part in zip(powers, parts))
                done.append(mixed / total)
                lse_cols[here, :] = jnp.where(
                    lane == 2 * p + h, peak + jnp.log(total), lse_cols[here, :]
                )
            o_send[here, lanes] = jnp.where(lane < HEAD_DIM, done[0], done[1]).astype(BF16)

        lax.fori_loop(0, me.half_width // PAIR, pair_of_heads, None)
        for j in range(i * spans, (i + 1) * spans):
            push(me, *o_move(j))

    lse[...] = jnp.transpose(lse_cols[...])[0:8, :]

    for j in range(1, me.nb):
        blk_move(j).wait_send()
        landed(cnt_blk.at[lax.rem(me.b + me.nb - j, me.nb)], br.at[j])
    cnt[...] = jnp.sum(cnt_blk[...], axis=0)
    for move in row_moves():
        push_done(me, *move)
    for j in range(me.nb):
        forward_move(j).wait_send()
        push_done(me, *o_move(j))
    for s in range(me.seqs):
        for h in range(2):
            landed(
                o.at[pl.ds(s * me.span, me.span), pl.ds(h * me.half_width, me.half_width)],
                orr.at[2 * s + h],
            )
    exchange_wait(me, dh_send, dh, ds, dr, me.cap)
    exchange_sent(me, dh_send, dh, ds, dr, me.cap)


def gelu_parts(u):
    root = 0.7978845608028654
    cubic = 0.044715
    square = u * u
    t = jnp.tanh(root * u * (1.0 + cubic * square))
    value = 0.5 * u * (1.0 + t)
    slope = 0.5 * (1.0 + t) + (0.5 * root) * u * (1.0 - t * t) * (1.0 + 3.0 * cubic * square)
    return value, slope


def expert_kernel(
    cfg,
    x, o, wo, router, gain, bias, idx, dh, cnt, win_hbm, wout_hbm,
    h1, gate, mass, back, y, dwin, dwout, drouter,
    win, wout, n2, disp, took, g, du, made, dn,
    wsem, ns, nr, rs, rr,
):
    me = Place(cfg)
    loads = [
        pltpu.make_async_copy(win_hbm, win, wsem.at[0]),
        pltpu.make_async_copy(wout_hbm, wout, wsem.at[1]),
    ]
    for load in loads:
        load.start()
    me.greet()
    expert_lane = iota((ROWS, me.experts), 1)
    mass[...] = jnp.zeros_like(mass)

    def token_rows(r, _):
        here = split_rows(r * ROWS, ROWS)
        hidden = x[here, :].astype(F32) + dot(o[here, :], wo[...])
        h1[here, :] = hidden
        hat, _ = normalize(hidden)
        normed = (hat * gain[...] + bias[...]).astype(BF16)
        n2[here, :] = normed
        logits = dot(normed, router[...])
        hot = idx[here, :] == expert_lane
        value = jax.nn.sigmoid(jnp.sum(jnp.where(hot, logits, 0.0), axis=1, keepdims=True))
        gate[here, :] = value
        mass[...] += jnp.broadcast_to(
            jnp.sum(jnp.where(hot, value, 0.0), axis=0, keepdims=True), mass.shape
        )

    lax.fori_loop(0, me.rows // ROWS, token_rows, None)
    slot, _ = token_slots(me, idx[...])
    disp[...] = dot(slots_by_token(me, slot), n2[...]).astype(BF16)
    exchange_start(me, disp, took, ns, nr, me.cap)
    for load in loads:
        load.wait()
    exchange_wait(me, disp, took, ns, nr, me.cap)
    exchange_sent(me, disp, took, ns, nr, me.cap)

    slots = me.experts * me.cap
    lanes = iota((slots, me.experts), 1)
    logits = jnp.sum(jnp.where(lanes == me.e, dot(took[...], router[...]), 0.0), axis=1, keepdims=True)
    value = jax.nn.sigmoid(logits)
    disp[...] = (value * dh[...].astype(F32)).astype(BF16)

    def hidden_columns(f, _):
        here = split_rows(f * FF_COLS, FF_COLS)
        act, slope = gelu_parts(dot(took[...], win[:, here]))
        g[:, here] = act.astype(BF16)
        du[:, here] = (dot(disp[...], wout[here, :], NT) * slope).astype(BF16)

    lax.fori_loop(0, me.ff // FF_COLS, hidden_columns, None)

    def model_columns(f, _):
        here = split_rows(f * FF_COLS, FF_COLS)
        y[:, here] = dot(g[...], wout[:, here]).astype(BF16)
        made[:, here] = dot(du[...], win[here, :], NT)

    lax.fori_loop(0, me.width // FF_COLS, model_columns, None)

    load_lane = iota(cnt.shape, 1)
    load = jnp.sum(jnp.where(load_lane == me.e, cnt[...], 0.0), axis=1, keepdims=True)[0:1, :]
    weight = (load - me.mean_load) / me.mean_load
    dgate = (
        jnp.sum(dh[...].astype(F32) * y[...].astype(F32), axis=1, keepdims=True)
        + weight / me.tokens
    )
    dlogits = jnp.where(lanes == me.e, dgate * value * (1.0 - value), 0.0).astype(BF16)
    dn[...] = (made[...] + dot(dlogits, router[...], NT)).astype(BF16)
    exchange_start(me, dn, back, rs, rr, me.cap)
    drouter[...] = dot(dlogits, took[...], TN)

    def weight_columns(f, _):
        here = split_rows(f * FF_COLS, FF_COLS)
        dwin[:, here] = dot(took[...], du[:, here], TN).astype(BF16)
        dwout[here, :] = dot(g[:, here], disp[...], TN).astype(BF16)

    lax.fori_loop(0, me.ff // FF_COLS, weight_columns, None)
    exchange_wait(me, dn, back, rs, rr, me.cap)
    exchange_sent(me, dn, back, rs, rr, me.cap)


def backward_kernel(
    cfg,
    x, og, idx, h1, gate, back, y, o, q, k, v, a, lse, wo, wq, wk, wv,
    gain1, bias1, gain2, bias2,
    out, dx, dwq, dwk, dwv, dwo, norms,
    w, dh1, do_send, do, yback, dk_sum, dv_sum, dq, dk, dv, da, swap_send, swap, da_send, da_in,
    wsem, ys, yr, os, orr, ss, sr, fs, fr,
):
    me = Place(cfg)
    half = me.span // 2
    columns = pl.ds(pl.multiple_of(me.c * me.half_width, 128), me.half_width)
    loads = [
        pltpu.make_async_copy(m.at[:, columns], w.at[j], wsem.at[j])
        for j, m in enumerate((wq, wk, wv))
    ]
    for load in loads:
        load.start()
    me.greet()
    exchange_start(me, y, yback, ys, yr, me.cap)
    slot, _ = token_slots(me, idx[...])
    takes = tokens_by_slot(me, slot)
    norms[...] = jnp.zeros_like(norms)
    da[0 : me.rows, :] = dot(takes, back[...])

    def norm_rows(r, _):
        here = split_rows(r * ROWS, ROWS)
        grad = da[here, :]
        hat, inverse = normalize(h1[here, :])
        norms[2:3, :] += jnp.sum(grad * hat, axis=0, keepdims=True)
        norms[3:4, :] += jnp.sum(grad, axis=0, keepdims=True)
        total = og[here, :].astype(F32) + norm_back(hat, inverse, gain2[...], grad)
        dh1[here, :] = total
        do_send[here, :] = dot(total.astype(BF16), wo[...], NT).astype(BF16)

    lax.fori_loop(0, me.rows // ROWS, norm_rows, None)

    def o_moves():
        for s in range(me.seqs):
            for h in range(2):
                yield (
                    do_send.at[
                        pl.ds(s * me.span, me.span), pl.ds(h * me.half_width, me.half_width)
                    ],
                    do.at[split_rows(me.b * me.span, me.span)],
                    os.at[2 * s + h],
                    orr.at[me.b],
                    (me.c * me.seqs + s, me.pair + h),
                )

    for move in o_moves():
        push(me, *move)
    dwo[...] = dot(o[...], dh1[...].astype(BF16), TN)
    for j in range(me.nb):
        landed(do.at[pl.ds(j * me.span, me.span)], orr.at[j])

    first, second = head_masks()
    blocks = me.length // QUERY_ROWS
    visible = iota((QUERY_ROWS, QUERY_ROWS), 0) <= iota((QUERY_ROWS, QUERY_ROWS), 1)

    def pair_of_heads(p, _):
        lanes = split_rows(p * PAIR, PAIR)
        dk_sum[...] = jnp.zeros_like(dk_sum)
        dv_sum[...] = jnp.zeros_like(dv_sum)
        for i in range(blocks):
            here = pl.ds(i * QUERY_ROWS, QUERY_ROWS)
            queries, grads = q[here, lanes], do[here, lanes]
            parts = [here]
            if i:
                parts.append(pl.ds(0, i * QUERY_ROWS))
            dq_block = jnp.zeros((QUERY_ROWS, PAIR), F32)
            for h, mask in enumerate((first, second)):
                qm, gm = queries * mask, grads * mask
                sums = lse[pl.ds(2 * p + h, 1), here]
                scores = [dot(k[part, lanes], qm, NT) for part in parts]
                powers = [jnp.exp(s - sums) for s in scores]
                powers[0] = jnp.where(visible, powers[0], 0.0)
                weighted = [
                    s * dot(v[part, lanes], gm, NT) for s, part in zip(powers, parts)
                ]
                delta = sum(jnp.sum(t, axis=0, keepdims=True) for t in weighted)
                for s, t, part in zip(powers, weighted, parts):
                    ds = (t - s * delta).astype(BF16)
                    dv_sum[part, :] += dot(s.astype(BF16), gm)
                    dk_sum[part, :] += dot(ds, qm)
                    dq_block += dot(ds, k[part, lanes] * mask, TN)
            dq[here, lanes] = (dq_block * SCALE).astype(BF16)
        dk[:, lanes] = dk_sum[...].astype(BF16)
        dv[:, lanes] = dv_sum[...].astype(BF16)

    lax.fori_loop(0, me.half_width // PAIR, pair_of_heads, None)

    for load in loads:
        load.wait()
    da[...] = dot(dq[...], w[0], NT) + dot(dk[...], w[1], NT) + dot(dv[...], w[2], NT)
    for j in range(me.nb):
        swap_send[j] = da[split_rows(j * me.span + (1 - me.c) * half, half), :].astype(BF16)
    swap_move = remote(swap_send, swap, ss, sr, (me.b, me.sibling))
    swap_move.start()
    dwq[...] = dot(a[...], dq[...], TN)
    swap_move.wait()
    source = me.pair + lax.div(me.b, me.seqs)

    def da_move(j):
        return (
            da_send.at[j],
            da_in.at[split_rows(lax.rem(me.b, me.seqs) * me.span + me.c * half, half)],
            fs.at[j],
            fr.at[2 * lax.rem(me.b, me.seqs) + me.c],
            (j, source),
        )

    for j in range(me.nb):
        mine = da[split_rows(j * me.span + me.c * half, half), :]
        da_send[j] = (mine + swap[j].astype(F32)).astype(BF16)
        push(me, *da_move(j))
    dwk[...] = dot(a[...], dk[...], TN)
    dwv[...] = dot(a[...], dv[...], TN)

    exchange_wait(me, y, yback, ys, yr, me.cap)
    exchange_sent(me, y, yback, ys, yr, me.cap)
    da[0 : me.rows, :] = dot(takes, yback[...])

    def out_rows(r, _):
        here = split_rows(r * ROWS, ROWS)
        out[here, :] = (h1[here, :] + gate[here, :] * da[here, :]).astype(BF16)

    lax.fori_loop(0, me.rows // ROWS, out_rows, None)

    for s in range(me.seqs):
        for h in range(2):
            landed(da_in.at[pl.ds(s * me.span + h * half, half)], fr.at[2 * s + h])

    def token_rows(r, _):
        here = split_rows(r * ROWS, ROWS)
        grad = da_in[here, :].astype(F32)
        hat, inverse = normalize(x[here, :].astype(F32))
        norms[0:1, :] += jnp.sum(grad * hat, axis=0, keepdims=True)
        norms[1:2, :] += jnp.sum(grad, axis=0, keepdims=True)
        dx[here, :] = (dh1[here, :] + norm_back(hat, inverse, gain1[...], grad)).astype(BF16)

    lax.fori_loop(0, me.rows // ROWS, token_rows, None)
    for move in o_moves():
        push_done(me, *move)
    for j in range(me.nb):
        push_done(me, *da_move(j))


def in_vmem(count):
    return [pl.BlockSpec(memory_space=pltpu.VMEM)] * count


def anywhere(count):
    return [pl.BlockSpec(memory_space=pl.ANY)] * count


def call(body, cfg, number, in_specs, outs, scratch, name, cost):
    return pl.pallas_call(
        functools.partial(body, cfg),
        out_shape=[jax.ShapeDtypeStruct(shape, kind) for shape, kind in outs],
        in_specs=in_specs,
        out_specs=in_vmem(len(outs)),
        scratch_shapes=scratch,
        compiler_params=pltpu.CompilerParams(
            collective_id=number, has_side_effects=True, vmem_limit_bytes=VMEM_BYTES
        ),
        cost_estimate=pl.CostEstimate(flops=cost, bytes_accessed=1 << 24, transcendentals=1 << 22),
        name=name,
    )


def shards(
    tokens,
    output_grad,
    expert_index,
    query_weight,
    key_weight,
    value_weight,
    output_weight,
    router_weight,
    expert_in,
    expert_out,
    norm1_gain,
    norm1_bias,
    norm2_gain,
    norm2_bias,
):
    seqs, span, width = tokens.shape
    rows = seqs * span
    nb, ne = lax.axis_size("blk"), lax.axis_size("exp")
    length = span * nb
    experts = router_weight.shape[1]
    ff = expert_in.shape[2]
    cap = -(-max(2, rows * 5 // (4 * experts)) // 16) * 16
    slots = experts * cap
    token_total = rows * nb * ne
    half_width = width // 2
    cfg = dict(
        seqs=seqs, span=span, width=width, rows=rows, nb=nb, ne=ne, length=length,
        experts=experts, ff=ff, cap=cap, half_width=half_width, tokens=token_total,
        mean_load=token_total / experts,
    )
    x = tokens.reshape(rows, width)
    og = output_grad.reshape(rows, width)
    idx = expert_index.reshape(rows, 1)
    gain1, bias1 = norm1_gain.reshape(1, width), norm1_bias.reshape(1, width)
    gain2, bias2 = norm2_gain.reshape(1, width), norm2_bias.reshape(1, width)
    dma = pltpu.SemaphoreType.DMA
    vmem = pltpu.VMEM
    half = span // 2
    q, k, v, a, lse, o, dh, cnt = call(
        attend_kernel, cfg, 1,
        in_vmem(5) + anywhere(3),
        [
            ((length, half_width), BF16),
            ((length, half_width), BF16),
            ((length, half_width), BF16),
            ((length, width), BF16),
            ((8, length), F32),
            ((rows, width), BF16),
            ((slots, width), BF16),
            ((8, 128), F32),
        ],
        [
            vmem((3, width, half_width), BF16),
            vmem((nb, half, width), BF16),
            vmem((length, half_width), BF16),
            vmem((length, 128), F32),
            vmem((slots, width), BF16),
            vmem((ne, 8, 128), F32),
            vmem((8, 128), F32),
            vmem((nb, 8, 128), F32),
            dma((3,)),
            dma((2 * seqs,)), dma((nb,)),
            dma((nb,)), dma((nb,)),
            dma((nb,)), dma((2 * seqs,)),
            dma((ne,)), dma((ne,)),
            dma((ne,)), dma((ne,)),
            dma((nb,)), dma((nb,)),
        ],
        "attend", 8 << 30,
    )(x, og, idx, gain1, bias1, query_weight, key_weight, value_weight)
    h1, gate, mass, back, y, dwin, dwout, drouter = call(
        expert_kernel, cfg, 2,
        in_vmem(9) + anywhere(2),
        [
            ((rows, width), F32),
            ((rows, 1), F32),
            ((8, experts), F32),
            ((slots, width), BF16),
            ((slots, width), BF16),
            ((width, ff), BF16),
            ((ff, width), BF16),
            ((experts, width), F32),
        ],
        [
            vmem((width, ff), BF16),
            vmem((ff, width), BF16),
            vmem((rows, width), BF16),
            vmem((slots, width), BF16),
            vmem((slots, width), BF16),
            vmem((slots, ff), BF16),
            vmem((slots, ff), BF16),
            vmem((slots, width), F32),
            vmem((slots, width), BF16),
            dma((2,)),
            dma((ne,)), dma((ne,)),
            dma((ne,)), dma((ne,)),
        ],
        "experts", 20 << 30,
    )(
        x, o, output_weight, router_weight, gain2, bias2, idx, dh, cnt,
        expert_in.reshape(width, ff), expert_out.reshape(ff, width),
    )
    out, dx, dwq, dwk, dwv, dwo, norms = call(
        backward_kernel, cfg, 3,
        in_vmem(14) + anywhere(3) + in_vmem(4),
        [
            ((rows, width), BF16),
            ((rows, width), BF16),
            ((width, half_width), F32),
            ((width, half_width), F32),
            ((width, half_width), F32),
            ((width, width), F32),
            ((8, width), F32),
        ],
        [
            vmem((3, width, half_width), BF16),
            vmem((rows, width), F32),
            vmem((rows, width), BF16),
            vmem((length, half_width), BF16),
            vmem((slots, width), BF16),
            vmem((length, PAIR), F32),
            vmem((length, PAIR), F32),
            vmem((length, half_width), BF16),
            vmem((length, half_width), BF16),
            vmem((length, half_width), BF16),
            vmem((length, width), F32),
            vmem((nb, half, width), BF16),
            vmem((nb, half, width), BF16),
            vmem((nb, half, width), BF16),
            vmem((rows, width), BF16),
            dma((3,)),
            dma((ne,)), dma((ne,)),
            dma((2 * seqs,)), dma((nb,)),
            dma, dma,
            dma((nb,)), dma((2 * seqs,)),
        ],
        "backward", 20 << 30,
    )(
        x, og, idx, h1, gate, back, y, o, q, k, v, a, lse, output_weight,
        query_weight, key_weight, value_weight, gain1, bias1, gain2, bias2,
    )

    expert_in_grad = lax.psum_scatter(dwin, "blk", scatter_dimension=1, tiled=True).astype(F32)
    expert_out_grad = lax.psum_scatter(dwout, "blk", scatter_dimension=0, tiled=True).astype(F32)
    core = lax.rem(lax.axis_index("exp"), 2)
    halves = jnp.stack([dwq, dwk, dwv]).astype(BF16)
    empty = jnp.zeros_like(halves)
    full = jnp.concatenate(
        [jnp.where(core == 0, halves, empty), jnp.where(core == 0, empty, halves)], axis=2
    )
    wide, small = lax.psum(
        (
            jnp.concatenate([full, dwo.astype(BF16)[None]]),
            jnp.concatenate([norms[:4], drouter, jnp.pad(mass[:1], ((0, 0), (0, width - experts)))]),
        ),
        ("blk", "exp"),
    )
    wide = wide.astype(F32)
    load_weight = (cnt[0, :experts] - cfg["mean_load"]) / cfg["mean_load"]
    balance = jnp.sum(load_weight * small[4 + experts, :experts]) / token_total
    return (
        out.reshape(seqs, span, width),
        balance,
        dx.reshape(seqs, span, width),
        wide[0],
        wide[1],
        wide[2],
        wide[3],
        small[4 : 4 + experts].T,
        expert_in_grad[None],
        expert_out_grad[None],
        small[0],
        small[1],
        small[2],
        small[3],
    )


def solution(mesh):
    return jax.shard_map(
        shards,
        mesh=mesh,
        in_specs=(
            P("exp", "blk", None),
            P("exp", "blk", None),
            P("blk", "exp", None, None),
            P(),
            P(),
            P(),
            P(),
            P(),
            P("exp", None, None),
            P("exp", None, None),
            P(),
            P(),
            P(),
            P(),
        ),
        out_specs=(
            P("exp", "blk", None),
            P(),
            P("exp", "blk", None),
            P(),
            P(),
            P(),
            P(),
            P(),
            P("exp", None, "blk"),
            P("exp", "blk", None),
            P(),
            P(),
            P(),
            P(),
        ),
        check_vma=False,
    )
```

```python
import functools

import jax
import jax.numpy as jnp
from jax import lax
from jax.experimental import pallas as pl
from jax.experimental.pallas import tpu as pltpu
from jax.sharding import PartitionSpec as P

HEAD_DIM = 64
PAIR = 2 * HEAD_DIM
EPSILON = 1e-05
SCALE = HEAD_DIM ** (-0.5)
QUERY_ROWS = 256
ROWS = 128
FF_COLS = 256
MESH = pl.DeviceIdType.MESH
BF16, F32 = jnp.bfloat16, jnp.float32
VMEM_BYTES = 63 << 20
NT = (((1,), (1,)), ((), ()))
TN = (((0,), (0,)), ((), ()))


def dot(left, right, dims=(((1,), (0,)), ((), ()))):
    return lax.dot_general(left, right, dims, preferred_element_type=F32)


def iota(shape, dim):
    return lax.broadcasted_iota(jnp.int32, shape, dim)


def normalize(values):
    centered = values - jnp.mean(values, axis=-1, keepdims=True)
    variance = jnp.mean(centered * centered, axis=-1, keepdims=True)
    inverse = lax.rsqrt(variance + EPSILON)
    return centered * inverse, inverse


def norm_back(hat, inverse, gain, grad):
    scaled = grad * gain
    return inverse * (
        scaled
        - jnp.mean(scaled, axis=-1, keepdims=True)
        - hat * jnp.mean(scaled * hat, axis=-1, keepdims=True)
    )


def split_rows(base, size):
    return pl.ds(pl.multiple_of(base, size), size)


class Place:
    def __init__(self, cfg):
        self.__dict__.update(cfg)
        self.b = lax.axis_index("blk")
        self.e = lax.axis_index("exp")
        self.c = lax.rem(self.e, 2)
        self.pair = self.e - self.c
        self.sibling = self.pair + 1 - self.c

    def greet(self):
        bar = pltpu.get_barrier_semaphore()

        def exp_peer(k, _):
            pl.semaphore_signal(
                bar, 1, device_id=(self.b, lax.rem(self.e + k, self.ne)), device_id_type=MESH
            )

        def blk_peer(k, _):
            there = lax.rem(self.b + k, self.nb)
            pl.semaphore_signal(bar, 1, device_id=(there, self.e), device_id_type=MESH)
            pl.semaphore_signal(bar, 1, device_id=(there, self.sibling), device_id_type=MESH)

        lax.fori_loop(1, self.ne, exp_peer, None)
        lax.fori_loop(1, self.nb, blk_peer, None)
        pl.semaphore_wait(bar, self.ne - 1 + 2 * (self.nb - 1))

    def is_me(self, there):
        return there[0] * self.ne + there[1] == self.b * self.ne + self.e


def remote(src, dst, send_sem, recv_sem, there):
    return pltpu.make_async_remote_copy(
        src, dst, send_sem, recv_sem, device_id=there, device_id_type=MESH
    )


def push(me, src, dst, send_sem, recv_sem, there):
    mine = me.is_me(there)

    @pl.when(mine)
    def _():
        pltpu.make_async_copy(src, dst, recv_sem).start()

    @pl.when(jnp.logical_not(mine))
    def _():
        remote(src, dst, send_sem, recv_sem, there).start()


def push_done(me, src, dst, send_sem, recv_sem, there):
    @pl.when(jnp.logical_not(me.is_me(there)))
    def _():
        remote(src, dst, send_sem, recv_sem, there).wait_send()


def landed(dst, recv_sem):
    pltpu.make_async_copy(dst, dst, recv_sem).wait()


def exchange_start(me, src, dst, send_sem, recv_sem, size):
    def one(k, _):
        there = lax.rem(me.e + k, me.ne)
        remote(
            src.at[split_rows(there * size, size)],
            dst.at[split_rows(me.e * size, size)],
            send_sem.at[k],
            recv_sem.at[k],
            (me.b, there),
        ).start()

    own = split_rows(me.e * size, size)
    pltpu.make_async_copy(src.at[own], dst.at[own], recv_sem.at[0]).start()
    lax.fori_loop(1, me.ne, one, None)


def exchange_wait(me, src, dst, send_sem, recv_sem, size):
    own = split_rows(me.e * size, size)
    landed(dst.at[own], recv_sem.at[0])

    def one(k, _):
        source = lax.rem(me.e + me.ne - k, me.ne)
        landed(dst.at[split_rows(source * size, size)], recv_sem.at[k])

    lax.fori_loop(1, me.ne, one, None)


def exchange_sent(me, src, dst, send_sem, recv_sem, size):
    def one(k, _):
        there = lax.rem(me.e + k, me.ne)
        remote(
            src.at[split_rows(there * size, size)],
            dst.at[split_rows(me.e * size, size)],
            send_sem.at[k],
            recv_sem.at[k],
            (me.b, there),
        ).wait_send()

    lax.fori_loop(1, me.ne, one, None)


def token_slots(me, idx):
    rows = idx.shape[0]
    hot = (idx == iota((rows, 128), 1)).astype(F32)
    earlier = (iota((rows, rows), 1) < iota((rows, rows), 0)).astype(F32).astype(BF16)
    ahead = dot(earlier, hot.astype(BF16))
    slot = jnp.sum(ahead * hot, axis=1, keepdims=True)
    return idx.astype(F32) * me.cap + slot, jnp.sum(hot, axis=0, keepdims=True)


def slots_by_token(me, slot):
    rows = slot.shape[0]
    across = jnp.transpose(jnp.broadcast_to(slot, (rows, 128)))[0:1, :]
    slots = me.experts * me.cap
    return (iota((slots, rows), 0) == across.astype(jnp.int32)).astype(F32).astype(BF16)


def tokens_by_slot(me, slot):
    rows = slot.shape[0]
    slots = me.experts * me.cap
    return (iota((rows, slots), 1) == slot.astype(jnp.int32)).astype(F32).astype(BF16)


def head_masks():
    lane = iota((1, PAIR), 1)
    first = (lane < HEAD_DIM).astype(F32).astype(BF16)
    second = (lane >= HEAD_DIM).astype(F32).astype(BF16)
    return first, second


def attend_kernel(
    cfg,
    x, og, idx, gain, bias, wq, wk, wv,
    q, k, v, a, lse, o, dh, cnt,
    w, xin, o_send, lse_cols, dh_send, cnt_exp, cnt_part, cnt_blk,
    wsem, xs, xr, fs, fr, os, orr, ds, dr, cs, cr, bs, br,
):
    me = Place(cfg)
    half = me.span // 2
    columns = pl.ds(pl.multiple_of(me.c * me.half_width, 128), me.half_width)
    loads = [
        pltpu.make_async_copy(m.at[:, columns], w.at[j], wsem.at[j])
        for j, m in enumerate((wq, wk, wv))
    ]
    for load in loads:
        load.start()
    me.greet()

    def row_moves():
        for s in range(me.seqs):
            for h in range(2):
                there = (me.c * me.seqs + s, me.pair + h)
                yield (
                    x.at[pl.ds(s * me.span + h * half, half)],
                    xin.at[me.b],
                    xs.at[2 * s + h],
                    xr.at[me.b],
                    there,
                )

    for move in row_moves():
        push(me, *move)

    slot, counts = token_slots(me, idx[...])
    dh_send[...] = dot(slots_by_token(me, slot), og[...]).astype(BF16)
    exchange_start(me, dh_send, dh, ds, dr, me.cap)
    cnt_part[...] = jnp.broadcast_to(counts, cnt_part.shape)
    own = me.e
    pltpu.make_async_copy(cnt_part, cnt_exp.at[own], cr.at[0]).start()

    def count_move(j):
        return remote(
            cnt_part, cnt_exp.at[me.e], cs.at[j], cr.at[j], (me.b, lax.rem(me.e + j, me.ne))
        )

    lax.fori_loop(1, me.ne, lambda j, _: count_move(j).start(), None)

    def forward_move(j):
        rows = split_rows(j * me.span + me.c * half, half)
        return remote(a.at[rows], a.at[rows], fs.at[j], fr.at[j], (me.b, me.sibling))

    for j in range(me.nb):
        landed(xin.at[j], xr.at[j])
        hat, _ = normalize(xin[j].astype(F32))
        a[split_rows(j * me.span + me.c * half, half), :] = (
            hat * gain[...] + bias[...]
        ).astype(BF16)
        forward_move(j).start()

    landed(cnt_exp.at[me.e], cr.at[0])
    lax.fori_loop(
        1,
        me.ne,
        lambda j, _: landed(cnt_exp.at[lax.rem(me.e + me.ne - j, me.ne)], cr.at[j]),
        None,
    )
    lax.fori_loop(1, me.ne, lambda j, _: count_move(j).wait_send(), None)
    cnt_blk[me.b] = jnp.sum(cnt_exp[...], axis=0)

    def blk_move(j):
        return remote(
            cnt_blk.at[me.b],
            cnt_blk.at[me.b],
            bs.at[j],
            br.at[j],
            (lax.rem(me.b + j, me.nb), me.e),
        )

    for j in range(1, me.nb):
        blk_move(j).start()

    for load in loads:
        load.wait()
    first, second = head_masks()
    blocks = me.length // QUERY_ROWS
    spans = QUERY_ROWS // me.span
    lane = iota((1, PAIR), 1)
    visible = iota((QUERY_ROWS, QUERY_ROWS), 1) <= iota((QUERY_ROWS, QUERY_ROWS), 0)
    source = me.pair + lax.div(me.b, me.seqs)

    def o_move(j):
        return (
            o_send.at[pl.ds(j * me.span, me.span)],
            o.at[split_rows(lax.rem(me.b, me.seqs) * me.span, me.span), columns],
            os.at[j],
            orr.at[2 * lax.rem(me.b, me.seqs) + me.c],
            (j, source),
        )

    for i in range(blocks):
        for j in range(i * spans, (i + 1) * spans):
            theirs = split_rows(j * me.span + (1 - me.c) * half, half)
            landed(a.at[theirs], fr.at[j])
        here = pl.ds(i * QUERY_ROWS, QUERY_ROWS)
        rows = a[here, :]
        q[here, :] = dot(rows, w[0]).astype(BF16) * jnp.asarray(SCALE, BF16)
        k[here, :] = dot(rows, w[1]).astype(BF16)
        v[here, :] = dot(rows, w[2]).astype(BF16)

        def pair_of_heads(p, _, i=i, here=here):
            lanes = split_rows(p * PAIR, PAIR)
            queries = q[here, lanes]
            parts = [pl.ds(i * QUERY_ROWS, QUERY_ROWS)]
            if i:
                parts.append(pl.ds(0, i * QUERY_ROWS))
            done = []
            for h, mask in enumerate((first, second)):
                masked = queries * mask
                scores = [dot(masked, k[part, lanes], NT) for part in parts]
                scores[0] = jnp.where(visible, scores[0], -1e30)
                peak = functools.reduce(
                    jnp.maximum, [jnp.max(s, axis=1, keepdims=True) for s in scores]
                )
                powers = [jnp.exp(s - peak) for s in scores]
                total = sum(jnp.sum(s, axis=1, keepdims=True) for s in powers)
                mixed = sum(dot(s.astype(BF16), v[part, lanes]) for s, part in zip(powers, parts))
                done.append(mixed / total)
                lse_cols[here, :] = jnp.where(
                    lane == 2 * p + h, peak + jnp.log(total), lse_cols[here, :]
                )
            o_send[here, lanes] = jnp.where(lane < HEAD_DIM, done[0], done[1]).astype(BF16)

        lax.fori_loop(0, me.half_width // PAIR, pair_of_heads, None)
        for j in range(i * spans, (i + 1) * spans):
            push(me, *o_move(j))

    lse[...] = jnp.transpose(lse_cols[...])[0:8, :]

    for j in range(1, me.nb):
        blk_move(j).wait_send()
        landed(cnt_blk.at[lax.rem(me.b + me.nb - j, me.nb)], br.at[j])
    cnt[...] = jnp.sum(cnt_blk[...], axis=0)
    for move in row_moves():
        push_done(me, *move)
    for j in range(me.nb):
        forward_move(j).wait_send()
        push_done(me, *o_move(j))
    for s in range(me.seqs):
        for h in range(2):
            landed(
                o.at[pl.ds(s * me.span, me.span), pl.ds(h * me.half_width, me.half_width)],
                orr.at[2 * s + h],
            )
    exchange_wait(me, dh_send, dh, ds, dr, me.cap)
    exchange_sent(me, dh_send, dh, ds, dr, me.cap)


def gelu_parts(u):
    root = 0.7978845608028654
    cubic = 0.044715
    square = u * u
    t = jnp.tanh(root * u * (1.0 + cubic * square))
    value = 0.5 * u * (1.0 + t)
    slope = 0.5 * (1.0 + t) + (0.5 * root) * u * (1.0 - t * t) * (1.0 + 3.0 * cubic * square)
    return value, slope


class Refs:
    def __init__(self, names, refs):
        self.__dict__.update(zip(names, refs, strict=True))


class ExpertSums:
    def __init__(self, me, r):
        self.me, self.r = me, r
        self.hi, self.lo = lax.div(me.b, 2), lax.rem(me.b, 2)
        self.other = 1 - self.lo
        self.count = me.nb // 2
        self.size = me.ff // me.nb

    def turn(self, step):
        return lax.rem(self.hi + step, self.count)

    def span(self, hi, lo):
        return pl.ds(pl.multiple_of((2 * hi + lo) * self.size, 128), self.size)

    def in_first(self, hi):
        r = self.r
        there = (2 * self.hi + self.other, self.me.e)
        return remote(
            r.win.at[:, self.span(hi, self.other)], r.in1.at[hi], r.in1s.at[hi], r.in1r.at[hi], there
        )

    def in_second(self, step):
        r, hi = self.r, self.turn(step)
        return remote(
            r.win.at[:, self.span(hi, self.lo)],
            r.in2.at[step - 1],
            r.in2s.at[step - 1],
            r.in2r.at[step - 1],
            (2 * hi + self.lo, self.me.e),
        )

    def out_first(self, step, lo):
        r, hi = self.r, self.turn(step)
        return remote(
            r.wout.at[self.span(hi, lo)],
            r.out1.at[step - 1, lo],
            r.out1s.at[step - 1, lo],
            r.out1r.at[step - 1, lo],
            (2 * hi + self.lo, self.me.e),
        )

    def out_second(self):
        r = self.r
        return remote(
            r.wout.at[self.span(self.hi, self.other)],
            r.out2,
            r.out2s,
            r.out2r,
            (2 * self.hi + self.other, self.me.e),
        )

    def after_part(self, n):
        step = lax.div(n, 2) + 1
        lo = lax.rem(self.other + n, 2)

        @pl.when(lax.rem(n, 2) == 0)
        def _():
            self.in_first(self.turn(step)).start()

        @pl.when(step < self.count)
        def _():
            self.out_first(step, lo).start()

    def second(self):
        r = self.r
        for step in range(1, self.count):
            hi = self.turn(step)
            landed(r.in1.at[hi], r.in1r.at[hi])
            here = self.span(hi, self.lo)

            def in_rows(n, _, hi=hi, here=here):
                rows = split_rows(n * ROWS, ROWS)
                r.win[rows, here] = (
                    r.win[rows, here].astype(F32) + r.in1[hi, rows, :].astype(F32)
                ).astype(BF16)

            lax.fori_loop(0, self.me.width // ROWS, in_rows, None)
            self.in_second(step).start()
        for step in range(1, self.count):
            landed(r.out1.at[step - 1, self.other], r.out1r.at[step - 1, self.other])
        base = (2 * self.hi + self.other) * self.size

        def out_rows(n, _):
            here, rows = split_rows(base + n * ROWS, ROWS), split_rows(n * ROWS, ROWS)
            total = r.wout[here, :].astype(F32)
            for step in range(1, self.count):
                total += r.out1[step - 1, self.other, rows, :].astype(F32)
            r.wout[here, :] = total.astype(BF16)

        lax.fori_loop(0, self.size // ROWS, out_rows, None)
        self.out_second().start()

    def total_in(self, into):
        r = self.r
        landed(r.in1.at[self.hi], r.in1r.at[self.hi])
        for step in range(1, self.count):
            landed(r.in2.at[step - 1], r.in2r.at[step - 1])

        def in_rows(n, _):
            rows = split_rows(n * ROWS, ROWS)
            total = r.win[rows, self.span(self.hi, self.lo)].astype(F32)
            total += r.in1[self.hi, rows, :].astype(F32)
            for step in range(1, self.count):
                total += r.in2[step - 1, rows, :].astype(F32)
            into[rows, 0 : self.size] = total

        lax.fori_loop(0, self.me.width // ROWS, in_rows, None)

    def total_out(self, into):
        r = self.r
        for step in range(1, self.count):
            landed(r.out1.at[step - 1, self.lo], r.out1r.at[step - 1, self.lo])
        landed(r.out2, r.out2r)
        base = (2 * self.hi + self.lo) * self.size

        def out_rows(n, _):
            rows = split_rows(n * ROWS, ROWS)
            total = r.wout[split_rows(base + n * ROWS, ROWS), :].astype(F32)
            for step in range(1, self.count):
                total += r.out1[step - 1, self.lo, rows, :].astype(F32)
            into[rows, :] = total + r.out2[rows, :].astype(F32)

        lax.fori_loop(0, self.size // ROWS, out_rows, None)

    def sent(self):
        for step in range(1, self.count + 1):
            self.in_first(self.turn(step)).wait_send()
            if step < self.count:
                self.in_second(step).wait_send()
                for lo in range(2):
                    self.out_first(step, lo).wait_send()
        self.out_second().wait_send()


class SharedSum:
    def __init__(self, me, r, p, blk_first):
        self.me, self.r, self.p = me, r, p
        z = lax.div(me.e, 2)
        nz = me.ne // 2
        blk = (me.b, me.nb, lambda t: (t, me.e))
        along_z = (z, nz, lambda t: (me.b, 2 * t + me.c))
        self.first, self.second = (blk, along_z) if blk_first else (along_z, blk)
        self.outer = me.width // self.first[1]
        self.inner = self.outer // self.second[1]

    def outer_rows(self, t):
        return split_rows(t * self.outer, self.outer)

    def inner_rows(self, t, s):
        return split_rows(t * self.outer + s * self.inner, self.inner)

    def view(self, rows, core):
        me, r, p = self.me, self.r, self.p
        if p < 3:
            return r.shared.at[
                pl.ds(0, 3), rows, pl.ds(pl.multiple_of(core * me.half_width + p * PAIR, PAIR), PAIR)
            ]
        return r.shared.at[
            3, rows, pl.ds(pl.multiple_of(core * me.half_width, PAIR), me.half_width)
        ]

    def peer(self, axis, k):
        return lax.rem(axis[0] + k, axis[1])

    def source(self, axis, k):
        return lax.rem(axis[0] + axis[1] - k, axis[1])

    def move1(self, k):
        r, p = self.r, self.p
        t = self.peer(self.first, k)
        return remote(
            r.part.at[p, self.outer_rows(t)],
            r.got1.at[p, k, pl.ds(0, self.outer)],
            r.s1.at[p, k],
            r.r1.at[p, k],
            self.first[2](t),
        )

    def move2(self, k):
        r, p = self.r, self.p
        t = self.peer(self.second, k)
        return remote(
            r.got1.at[p, 0, split_rows(t * self.inner, self.inner)],
            r.got2.at[p, k],
            r.s2.at[p, k],
            r.r2.at[p, k],
            self.second[2](t),
        )

    def move3(self, k):
        r, p = self.r, self.p
        here = self.view(self.inner_rows(self.first[0], self.second[0]), self.me.c)
        return remote(
            here, here, r.s3.at[p, k], r.r3.at[p, k], self.second[2](self.peer(self.second, k))
        )

    def move4(self, k):
        r, p = self.r, self.p
        here = self.view(self.outer_rows(self.first[0]), self.me.c)
        return remote(
            here, here, r.s4.at[p, k], r.r4.at[p, k], self.first[2](self.peer(self.first, k))
        )

    def move5(self):
        r, p = self.r, self.p
        here = self.view(pl.ds(0, self.me.width), self.me.c)
        return remote(here, here, r.s5.at[p], r.r5.at[p], (self.me.b, self.me.sibling))

    def stage1(self):
        for k in range(1, self.first[1]):
            self.move1(k).start()

    def stage2(self):
        r, p = self.r, self.p
        total = r.part[p, self.outer_rows(self.first[0])].astype(F32)
        for k in range(1, self.first[1]):
            here = r.got1.at[p, k, pl.ds(0, self.outer)]
            landed(here, r.r1.at[p, k])
            total += here[...].astype(F32)
        r.got1[p, 0, 0 : self.outer, :] = total.astype(BF16)
        for k in range(1, self.second[1]):
            self.move2(k).start()

    def stage3(self):
        r, p = self.r, self.p
        total = r.got1[p, 0, split_rows(self.second[0] * self.inner, self.inner)].astype(F32)
        for k in range(1, self.second[1]):
            landed(r.got2.at[p, k], r.r2.at[p, k])
            total += r.got2[p, k].astype(F32)
        total = total.astype(BF16)
        here = self.view(self.inner_rows(self.first[0], self.second[0]), self.me.c)
        if p < 3:
            for j in range(3):
                here[j] = total[:, j * PAIR : (j + 1) * PAIR]
        else:
            here[...] = total
        for k in range(1, self.second[1]):
            self.move3(k).start()

    def stage4(self):
        for k in range(1, self.second[1]):
            rows = self.inner_rows(self.first[0], self.source(self.second, k))
            landed(self.view(rows, self.me.c), self.r.r3.at[self.p, k])
        for k in range(1, self.first[1]):
            self.move4(k).start()

    def stage5(self):
        for k in range(1, self.first[1]):
            rows = self.outer_rows(self.source(self.first, k))
            landed(self.view(rows, self.me.c), self.r.r4.at[self.p, k])
        self.move5().start()

    def end(self):
        landed(self.view(pl.ds(0, self.me.width), 1 - self.me.c), self.r.r5.at[self.p])
        for k in range(1, self.first[1]):
            self.move1(k).wait_send()
            self.move4(k).wait_send()
        for k in range(1, self.second[1]):
            self.move2(k).wait_send()
            self.move3(k).wait_send()
        self.move5().wait_send()


def layer_kernel(cfg, names, *refs):
    me = Place(cfg)
    r = Refs(names, refs)
    r.ysend, r.yback = r.g, r.du
    r.swap, r.da_in = r.took.at[pl.ds(0, me.rows)], r.back.at[pl.ds(0, me.rows)]
    half = me.span // 2
    pairs = me.half_width // PAIR
    weight_loads = [
        pltpu.make_async_copy(r.win_hbm, r.win, r.wsem.at[0]),
        pltpu.make_async_copy(r.wout_hbm, r.wout, r.wsem.at[1]),
    ]
    late = [
        pltpu.make_async_copy(src, dst, r.lsem.at[n])
        for n, (src, dst) in enumerate(
            (
                (r.og_hbm, r.og),
                (r.q_hbm, r.q),
                (r.k_hbm, r.k),
                (r.v_hbm, r.v),
                (r.a_hbm, r.a),
                (r.lse_hbm, r.lse),
            )
        )
    ]
    for p in range(pairs):
        for j, matrix in enumerate((r.wq_hbm, r.wk_hbm, r.wv_hbm)):
            src = matrix.at[:, pl.ds(pl.multiple_of(me.c * me.half_width + p * PAIR, PAIR), PAIR)]
            late.append(
                pltpu.make_async_copy(
                    src, r.w.at[p, :, pl.ds(j * PAIR, PAIR)], r.lsem.at[6 + 3 * p + j]
                )
            )
    for load in weight_loads + late:
        load.start()
    me.greet()

    expert_lane = iota((ROWS, me.experts), 1)
    r.sums[...] = jnp.zeros_like(r.sums)
    r.mass[...] = jnp.zeros_like(r.mass)

    def token_rows(n, _):
        here = split_rows(n * ROWS, ROWS)
        hidden = r.x[here, :].astype(F32) + dot(r.o[here, :], r.wo[...])
        r.h1[here, :] = hidden
        hat, _ = normalize(hidden)
        normed = (hat * r.gain2[...] + r.bias2[...]).astype(BF16)
        r.mail[here, :] = normed
        logits = dot(normed, r.router[...])
        hot = r.idx[here, :] == expert_lane
        value = jax.nn.sigmoid(jnp.sum(jnp.where(hot, logits, 0.0), axis=1, keepdims=True))
        r.gate[here, :] = value
        r.mass[...] += jnp.sum(jnp.where(hot, value, 0.0), axis=0, keepdims=True)

    lax.fori_loop(0, me.rows // ROWS, token_rows, None)
    slot, _ = token_slots(me, r.idx[...])
    r.disp[...] = dot(slots_by_token(me, slot), r.mail[...]).astype(BF16)
    exchange_start(me, r.disp, r.took, r.ns, r.nr, me.cap)
    for load in weight_loads:
        load.wait()
    exchange_wait(me, r.disp, r.took, r.ns, r.nr, me.cap)
    exchange_sent(me, r.disp, r.took, r.ns, r.nr, me.cap)

    slots = me.experts * me.cap
    lanes = iota((slots, me.experts), 1)
    logits = jnp.sum(
        jnp.where(lanes == me.e, dot(r.took[...], r.router[...]), 0.0), axis=1, keepdims=True
    )
    value = jax.nn.sigmoid(logits)
    r.disp[...] = (value * r.dh[...].astype(F32)).astype(BF16)
    r.yf[0:slots, :] = jnp.zeros((slots, me.width), F32)
    r.made[...] = jnp.zeros_like(r.made)
    sums = ExpertSums(me, r)
    slot_rows = slots // 2

    def expert_part(n, _):
        hi, lo = sums.turn(lax.div(n, 2) + 1), lax.rem(sums.other + n, 2)
        base = (2 * hi + lo) * sums.size

        def hidden_columns(f, _):
            here = pl.ds(pl.multiple_of(base + f * sums.tile, 128), sums.tile)
            there = pl.ds(pl.multiple_of(f * sums.tile, 128), sums.tile)

            def hidden_rows(n, _):
                rows = split_rows(n * slot_rows, slot_rows)
                act, slope = gelu_parts(dot(r.took[rows, :], r.win[:, here]))
                r.g[rows, there] = act.astype(BF16)
                r.du[rows, there] = (dot(r.disp[rows, :], r.wout[here, :], NT) * slope).astype(BF16)

            lax.fori_loop(0, slots // slot_rows, hidden_rows, None)

        lax.fori_loop(0, sums.size // sums.tile, hidden_columns, None)
        part = sums.span(hi, lo)

        def model_columns(f, _):
            here = split_rows(f * FF_COLS, FF_COLS)
            r.yf[0:slots, here] += dot(r.g[:, 0 : sums.size], r.wout[part, here])
            r.made[0:slots, here] += dot(r.du[:, 0 : sums.size], r.win[here, part], NT)

        lax.fori_loop(0, me.width // FF_COLS, model_columns, None)

        def weight_columns(f, _):
            here = pl.ds(pl.multiple_of(base + f * sums.tile, 128), sums.tile)
            there = pl.ds(pl.multiple_of(f * sums.tile, 128), sums.tile)
            r.win[:, here] = dot(r.took[...], r.du[:, there], TN).astype(BF16)
            r.wout[here, :] = dot(r.g[:, there], r.disp[...], TN).astype(BF16)

        lax.fori_loop(0, sums.size // sums.tile, weight_columns, None)
        sums.after_part(n)

    sums.tile = min(FF_COLS, sums.size) if sums.size % FF_COLS == 0 else PAIR
    lax.fori_loop(0, me.nb, expert_part, None)

    load_lane = iota(r.cnt.shape, 1)
    load = jnp.sum(jnp.where(load_lane == me.e, r.cnt[...], 0.0), axis=1, keepdims=True)[0:1, :]
    weight = (load - me.mean_load) / me.mean_load
    r.ysend[...] = r.yf[0:slots, :].astype(BF16)
    dgate = (
        jnp.sum(r.dh[...].astype(F32) * r.ysend[...].astype(F32), axis=1, keepdims=True)
        + weight / me.tokens
    )
    dlogits = jnp.where(lanes == me.e, dgate * value * (1.0 - value), 0.0).astype(BF16)
    r.disp[...] = (r.made[0:slots, :] + dot(dlogits, r.router[...], NT)).astype(BF16)
    exchange_start(me, r.disp, r.back, r.rs, r.rr, me.cap)
    r.sums[4 : 4 + me.experts, :] = dot(dlogits, r.took[...], TN)
    r.sums[4 + me.experts : 5 + me.experts, 0 : me.experts] = r.mass[...]
    sums.second()
    exchange_wait(me, r.disp, r.back, r.rs, r.rr, me.cap)
    exchange_start(me, r.ysend, r.yback, r.ys, r.yr, me.cap)

    for load in late:
        load.wait()
    takes = tokens_by_slot(me, slot)
    r.made[0 : me.rows, :] = dot(takes, r.back[...])

    def norm_rows(n, _):
        here = split_rows(n * ROWS, ROWS)
        grad = r.made[here, :]
        hat, inverse = normalize(r.h1[here, :])
        r.sums[2:3, :] += jnp.sum(grad * hat, axis=0, keepdims=True)
        r.sums[3:4, :] += jnp.sum(grad, axis=0, keepdims=True)
        total = r.og[here, :].astype(F32) + norm_back(hat, inverse, r.gain2[...], grad)
        r.dh1[here, :] = total
        r.mail[here, :] = dot(total.astype(BF16), r.wo[...], NT).astype(BF16)

    lax.fori_loop(0, me.rows // ROWS, norm_rows, None)

    def o_moves():
        for s in range(me.seqs):
            for h in range(2):
                yield (
                    r.mail.at[
                        pl.ds(s * me.span, me.span), pl.ds(h * me.half_width, me.half_width)
                    ],
                    r.do.at[split_rows(me.b * me.span, me.span)],
                    r.os.at[2 * s + h],
                    r.orr.at[me.b],
                    (me.c * me.seqs + s, me.pair + h),
                )

    for move in o_moves():
        push(me, *move)

    def output_columns(core):
        cols = pl.ds(pl.multiple_of(core * me.half_width, PAIR), me.half_width)
        return dot(r.o[...], r.dh1[:, cols].astype(BF16), TN)

    r.part[0] = output_columns(1 - me.c).astype(BF16)
    o_swap = remote(r.part.at[0], r.ogot, r.oss, r.osr, (me.b, me.sibling))
    o_swap.start()
    own_columns = output_columns(me.c)
    o_swap.wait()
    r.part[3] = (own_columns + r.ogot[...].astype(F32)).astype(BF16)
    pieces = [SharedSum(me, r, p, blk_first=p in (1, 2)) for p in range(4)] if me.sum_here else []
    if pieces:
        pieces[3].stage1()

    r.made[...] = jnp.zeros_like(r.made)
    for j in range(me.nb):
        landed(r.do.at[pl.ds(j * me.span, me.span)], r.orr.at[j])
    first, second = head_masks()
    blocks = me.length // QUERY_ROWS
    visible = iota((QUERY_ROWS, QUERY_ROWS), 0) <= iota((QUERY_ROWS, QUERY_ROWS), 1)

    def pair_of_heads(n, _):
        lanes = split_rows(n * PAIR, PAIR)
        r.dk_sum[...] = jnp.zeros_like(r.dk_sum)
        r.dv_sum[...] = jnp.zeros_like(r.dv_sum)
        for i in range(blocks):
            here = pl.ds(i * QUERY_ROWS, QUERY_ROWS)
            queries, grads = r.q[here, lanes], r.do[here, lanes]
            parts = [here]
            if i:
                parts.append(pl.ds(0, i * QUERY_ROWS))
            dq_block = jnp.zeros((QUERY_ROWS, PAIR), F32)
            for h, mask in enumerate((first, second)):
                qm, gm = queries * mask, grads * mask
                log_sums = r.lse[pl.ds(2 * n + h, 1), here]
                scores = [dot(r.k[part, lanes], qm, NT) for part in parts]
                powers = [jnp.exp(s - log_sums) for s in scores]
                powers[0] = jnp.where(visible, powers[0], 0.0)
                weighted = [
                    s * dot(r.v[part, lanes], gm, NT) for s, part in zip(powers, parts)
                ]
                delta = sum(jnp.sum(t, axis=0, keepdims=True) for t in weighted)
                for s, t, part in zip(powers, weighted, parts):
                    ds = (t - s * delta).astype(BF16)
                    r.dv_sum[part, :] += dot(s.astype(BF16), gm)
                    r.dk_sum[part, :] += dot(ds, qm)
                    dq_block += dot(ds, r.k[part, lanes] * mask, TN)
            r.dqkv[here, 0:PAIR] = (dq_block * SCALE).astype(BF16)
        r.dqkv[:, PAIR : 2 * PAIR] = r.dk_sum[...].astype(BF16)
        r.dqkv[:, 2 * PAIR : 3 * PAIR] = r.dv_sum[...].astype(BF16)
        r.part[n] = dot(r.a[...], r.dqkv[...], TN).astype(BF16)

        def normed_columns(f, _):
            cols = split_rows(f * FF_COLS, FF_COLS)
            r.made[:, cols] += dot(r.dqkv[...], r.w[n, cols, :], NT)

        lax.fori_loop(0, me.width // FF_COLS, normed_columns, None)
        if pieces:

            @pl.when(n == 0)
            def _():
                pieces[0].stage1()
                pieces[3].stage2()

            @pl.when(n == 1)
            def _():
                pieces[1].stage1()
                pieces[0].stage2()
                pieces[3].stage3()

            @pl.when(n == 2)
            def _():
                pieces[2].stage1()
                pieces[1].stage2()
                pieces[0].stage3()
                pieces[3].stage4()

    lax.fori_loop(0, pairs, pair_of_heads, None)

    for move in o_moves():
        push_done(me, *move)
    for j in range(me.nb):
        theirs = split_rows(j * me.span + (1 - me.c) * half, half)
        r.mail[pl.ds(j * half, half), :] = r.made[theirs, :].astype(BF16)
    swap = remote(r.mail, r.swap, r.ss, r.sr, (me.b, me.sibling))
    swap.start()
    exchange_wait(me, r.ysend, r.yback, r.ys, r.yr, me.cap)
    r.yf[0 : me.rows, :] = dot(takes, r.yback[...])

    def out_rows(n, _):
        here = split_rows(n * ROWS, ROWS)
        r.out[here, :] = (r.h1[here, :] + r.gate[here, :] * r.yf[here, :]).astype(BF16)

    lax.fori_loop(0, me.rows // ROWS, out_rows, None)
    swap.wait()
    home = me.pair + lax.div(me.b, me.seqs)

    def da_move(j):
        return (
            r.mail.at[pl.ds(j * half, half)],
            r.da_in.at[split_rows(lax.rem(me.b, me.seqs) * me.span + me.c * half, half)],
            r.fs.at[j],
            r.fr.at[2 * lax.rem(me.b, me.seqs) + me.c],
            (j, home),
        )

    for j in range(me.nb):
        mine = r.made[split_rows(j * me.span + me.c * half, half), :]
        rows = pl.ds(j * half, half)
        r.mail[rows, :] = (mine + r.swap[rows, :].astype(F32)).astype(BF16)
        push(me, *da_move(j))
    if pieces:
        pieces[2].stage2()
        pieces[1].stage3()
        pieces[0].stage4()
        pieces[3].stage5()
    for s in range(me.seqs):
        for h in range(2):
            landed(r.da_in.at[pl.ds(s * me.span + h * half, half)], r.fr.at[2 * s + h])

    def first_norm_rows(n, _):
        here = split_rows(n * ROWS, ROWS)
        grad = r.da_in[here, :].astype(F32)
        hat, inverse = normalize(r.x[here, :].astype(F32))
        r.sums[0:1, :] += jnp.sum(grad * hat, axis=0, keepdims=True)
        r.sums[1:2, :] += jnp.sum(grad, axis=0, keepdims=True)
        r.dx[here, :] = (r.dh1[here, :] + norm_back(hat, inverse, r.gain1[...], grad)).astype(
            BF16
        )

    lax.fori_loop(0, me.rows // ROWS, first_norm_rows, None)

    def sum_move(k):
        return remote(
            r.sums,
            r.sum_exp.at[me.e],
            r.es.at[k],
            r.er.at[k],
            (me.b, lax.rem(me.e + k, me.ne)),
        )

    lax.fori_loop(1, me.ne, lambda k, _: sum_move(k).start(), None)
    r.sum_exp[me.e] = r.sums[...]
    if pieces:
        pieces[2].stage3()
        pieces[1].stage4()
        pieces[0].stage5()
    lax.fori_loop(
        1,
        me.ne,
        lambda k, _: landed(r.sum_exp.at[lax.rem(me.e + me.ne - k, me.ne)], r.er.at[k]),
        None,
    )
    r.sum_blk[me.b] = jnp.sum(r.sum_exp[...], axis=0)

    def blk_move(k):
        return remote(
            r.sum_blk.at[me.b],
            r.sum_blk.at[me.b],
            r.bs.at[k],
            r.br.at[k],
            (lax.rem(me.b + k, me.nb), me.e),
        )

    for k in range(1, me.nb):
        blk_move(k).start()
    if pieces:
        pieces[2].stage4()
        pieces[1].stage5()

    size = sums.size
    sums.total_in(r.made)
    store_in = pltpu.make_async_copy(r.made.at[pl.ds(0, me.width), pl.ds(0, size)], r.dwin, r.wsem.at[0])
    store_in.start()
    sums.total_out(r.yf)
    store_out = pltpu.make_async_copy(r.yf.at[pl.ds(0, size)], r.dwout, r.wsem.at[1])
    store_out.start()
    if pieces:
        pieces[2].stage5()
    for k in range(1, me.nb):
        landed(r.sum_blk.at[lax.rem(me.b + me.nb - k, me.nb)], r.br.at[k])
    r.small[...] = jnp.sum(r.sum_blk[...], axis=0)
    lax.fori_loop(1, me.ne, lambda k, _: sum_move(k).wait_send(), None)
    for k in range(1, me.nb):
        blk_move(k).wait_send()
    exchange_sent(me, r.disp, r.back, r.rs, r.rr, me.cap)
    exchange_sent(me, r.ysend, r.yback, r.ys, r.yr, me.cap)
    for j in range(me.nb):
        push_done(me, *da_move(j))
    sums.sent()
    for piece in pieces:
        piece.end()
    store_in.wait()
    store_out.wait()


def in_vmem(count):
    return [pl.BlockSpec(memory_space=pltpu.VMEM)] * count


def anywhere(count):
    return [pl.BlockSpec(memory_space=pl.ANY)] * count


def call(body, cfg, number, in_specs, outs, scratch, name, cost):
    return pl.pallas_call(
        functools.partial(body, cfg),
        out_shape=[jax.ShapeDtypeStruct(shape, kind) for shape, kind in outs],
        in_specs=in_specs,
        out_specs=in_vmem(len(outs)),
        scratch_shapes=scratch,
        compiler_params=pltpu.CompilerParams(
            collective_id=number, has_side_effects=True, vmem_limit_bytes=VMEM_BYTES
        ),
        cost_estimate=pl.CostEstimate(flops=cost, bytes_accessed=1 << 24, transcendentals=1 << 22),
        name=name,
    )


def shards(
    tokens,
    output_grad,
    expert_index,
    query_weight,
    key_weight,
    value_weight,
    output_weight,
    router_weight,
    expert_in,
    expert_out,
    norm1_gain,
    norm1_bias,
    norm2_gain,
    norm2_bias,
):
    seqs, span, width = tokens.shape
    rows = seqs * span
    nb, ne = lax.axis_size("blk"), lax.axis_size("exp")
    length = span * nb
    experts = router_weight.shape[1]
    ff = expert_in.shape[2]
    cap = -(-max(2, rows * 5 // (4 * experts)) // 16) * 16
    slots = experts * cap
    token_total = rows * nb * ne
    half_width = width // 2
    cfg = dict(
        seqs=seqs, span=span, width=width, rows=rows, nb=nb, ne=ne, length=length,
        experts=experts, ff=ff, cap=cap, half_width=half_width, tokens=token_total,
        mean_load=token_total / experts,
    )
    x = tokens.reshape(rows, width)
    og = output_grad.reshape(rows, width)
    idx = expert_index.reshape(rows, 1)
    gain1, bias1 = norm1_gain.reshape(1, width), norm1_bias.reshape(1, width)
    gain2, bias2 = norm2_gain.reshape(1, width), norm2_bias.reshape(1, width)
    dma = pltpu.SemaphoreType.DMA
    vmem = pltpu.VMEM
    half = span // 2
    q, k, v, a, lse, o, dh, cnt = call(
        attend_kernel, cfg, 1,
        in_vmem(5) + anywhere(3),
        [
            ((length, half_width), BF16),
            ((length, half_width), BF16),
            ((length, half_width), BF16),
            ((length, width), BF16),
            ((8, length), F32),
            ((rows, width), BF16),
            ((slots, width), BF16),
            ((8, 128), F32),
        ],
        [
            vmem((3, width, half_width), BF16),
            vmem((nb, half, width), BF16),
            vmem((length, half_width), BF16),
            vmem((length, 128), F32),
            vmem((slots, width), BF16),
            vmem((ne, 8, 128), F32),
            vmem((8, 128), F32),
            vmem((nb, 8, 128), F32),
            dma((3,)),
            dma((2 * seqs,)), dma((nb,)),
            dma((nb,)), dma((nb,)),
            dma((nb,)), dma((2 * seqs,)),
            dma((ne,)), dma((ne,)),
            dma((ne,)), dma((ne,)),
            dma((nb,)), dma((nb,)),
        ],
        "attend", 8 << 30,
    )(x, og, idx, gain1, bias1, query_weight, key_weight, value_weight)
    hi = nb // 2
    size = ff // nb
    sum_rows = -(-(5 + experts) // 8) * 8
    cfg["sum_here"] = width % (8 * nb * ne) == 0
    outer = width // min(nb, ne // 2)
    inner = width // (nb * ne // 2)
    inputs = (
        ("x", x, True),
        ("o", o, True),
        ("wo", output_weight, True),
        ("router", router_weight, True),
        ("gain1", gain1, True),
        ("gain2", gain2, True),
        ("bias2", bias2, True),
        ("idx", idx, True),
        ("dh", dh, True),
        ("cnt", cnt, True),
        ("win_hbm", expert_in.reshape(width, ff), False),
        ("wout_hbm", expert_out.reshape(ff, width), False),
        ("og_hbm", og, False),
        ("q_hbm", q, False),
        ("k_hbm", k, False),
        ("v_hbm", v, False),
        ("a_hbm", a, False),
        ("lse_hbm", lse, False),
        ("wq_hbm", query_weight, False),
        ("wk_hbm", key_weight, False),
        ("wv_hbm", value_weight, False),
    )
    outputs = (
        ("out", (rows, width), BF16, True),
        ("dx", (rows, width), BF16, True),
        (
            ("shared", (4, width, width), BF16, True)
            if cfg["sum_here"]
            else ("part", (4, width, half_width), BF16, True)
        ),
        ("small", (sum_rows, width), F32, True),
        ("dwin", (width, size), F32, False),
        ("dwout", (size, width), F32, False),
    )
    scratch = dict(
        win=vmem((width, ff), BF16),
        wout=vmem((ff, width), BF16),
        og=vmem((rows, width), BF16),
        q=vmem((length, half_width), BF16),
        k=vmem((length, half_width), BF16),
        v=vmem((length, half_width), BF16),
        a=vmem((length, width), BF16),
        lse=vmem((8, length), F32),
        w=vmem((half_width // PAIR, width, 3 * PAIR), BF16),
        h1=vmem((rows, width), F32),
        gate=vmem((rows, 1), F32),
        mass=vmem((1, experts), F32),
        mail=vmem((rows, width), BF16),
        disp=vmem((slots, width), BF16),
        took=vmem((slots, width), BF16),
        g=vmem((slots, width), BF16),
        du=vmem((slots, width), BF16),
        yf=vmem((max(slots, size), width), F32),
        made=vmem((length, width), F32),
        back=vmem((slots, width), BF16),
        dh1=vmem((rows, width), F32),
        do=vmem((length, half_width), BF16),
        ogot=vmem((width, half_width), BF16),
        dk_sum=vmem((length, PAIR), F32),
        dv_sum=vmem((length, PAIR), F32),
        dqkv=vmem((length, 3 * PAIR), BF16),
        sums=vmem((sum_rows, width), F32),
        sum_exp=vmem((ne, sum_rows, width), F32),
        sum_blk=vmem((nb, sum_rows, width), F32),
        in1=vmem((hi, width, size), BF16),
        in2=vmem((hi - 1, width, size), BF16),
        out1=vmem((hi - 1, 2, size, width), BF16),
        out2=vmem((size, width), BF16),
        in1s=dma((hi,)), in1r=dma((hi,)),
        in2s=dma((hi - 1,)), in2r=dma((hi - 1,)),
        out1s=dma((hi - 1, 2)), out1r=dma((hi - 1, 2)),
        out2s=dma, out2r=dma,
        wsem=dma((2,)),
        lsem=dma((6 + 3 * (half_width // PAIR),)),
        ns=dma((ne,)), nr=dma((ne,)),
        rs=dma((ne,)), rr=dma((ne,)),
        ys=dma((ne,)), yr=dma((ne,)),
        os=dma((2 * seqs,)), orr=dma((nb,)),
        oss=dma, osr=dma,
        ss=dma, sr=dma,
        fs=dma((nb,)), fr=dma((2 * seqs,)),
        es=dma((ne,)), er=dma((ne,)),
        bs=dma((nb,)), br=dma((nb,)),
    )
    if cfg["sum_here"]:
        scratch.update(
            part=vmem((4, width, half_width), BF16),
            got1=vmem((4, max(nb, ne // 2), outer, half_width), BF16),
            got2=vmem((4, max(nb, ne // 2), inner, half_width), BF16),
            s5=dma((4,)),
            r5=dma((4,)),
        )
        for n in range(1, 5):
            scratch[f"s{n}"] = dma((4, max(nb, ne // 2)))
            scratch[f"r{n}"] = dma((4, max(nb, ne // 2)))
    names = [n for n, _, _ in inputs] + [n for n, _, _, _ in outputs] + list(scratch)
    out, dx, shared, small, dwin, dwout = pl.pallas_call(
        functools.partial(layer_kernel, cfg, names),
        out_shape=[jax.ShapeDtypeStruct(shape, kind) for _, shape, kind, _ in outputs],
        in_specs=[(in_vmem if near else anywhere)(1)[0] for _, _, near in inputs],
        out_specs=[(in_vmem if near else anywhere)(1)[0] for _, _, _, near in outputs],
        scratch_shapes=list(scratch.values()),
        compiler_params=pltpu.CompilerParams(
            collective_id=2, has_side_effects=True, vmem_limit_bytes=VMEM_BYTES
        ),
        cost_estimate=pl.CostEstimate(
            flops=30 << 30, bytes_accessed=1 << 25, transcendentals=1 << 23
        ),
        name="layer",
    )(*[value for _, value, _ in inputs])
    if not cfg["sum_here"]:
        own = shared.reshape(4, width, half_width)
        own = jnp.concatenate(
            [
                own[:3].reshape(3, width, 3, PAIR).transpose(2, 1, 0, 3).reshape(3, width, half_width),
                own[3:],
            ]
        )
        core, empty = lax.rem(lax.axis_index("exp"), 2), jnp.zeros_like(own)
        shared = lax.psum(
            jnp.concatenate(
                [jnp.where(core == 0, own, empty), jnp.where(core == 0, empty, own)], axis=2
            ),
            ("blk", "exp"),
        )
    wide = shared.astype(F32)
    load_weight = (cnt[0, :experts] - cfg["mean_load"]) / cfg["mean_load"]
    balance = jnp.sum(load_weight * small[4 + experts, :experts]) / token_total
    return (
        out.reshape(seqs, span, width),
        balance,
        dx.reshape(seqs, span, width),
        wide[0],
        wide[1],
        wide[2],
        wide[3],
        small[4 : 4 + experts].T,
        dwin[None],
        dwout[None],
        small[0],
        small[1],
        small[2],
        small[3],
    )


def solution(mesh):
    return jax.shard_map(
        shards,
        mesh=mesh,
        in_specs=(
            P("exp", "blk", None),
            P("exp", "blk", None),
            P("blk", "exp", None, None),
            P(),
            P(),
            P(),
            P(),
            P(),
            P("exp", None, None),
            P("exp", None, None),
            P(),
            P(),
            P(),
            P(),
        ),
        out_specs=(
            P("exp", "blk", None),
            P(),
            P("exp", "blk", None),
            P(),
            P(),
            P(),
            P(),
            P(),
            P("exp", None, "blk"),
            P("exp", "blk", None),
            P(),
            P(),
            P(),
            P(),
        ),
        check_vma=False,
    )
```

```python
import functools

import jax
import jax.numpy as jnp
from jax import lax
from jax.experimental import pallas as pl
from jax.experimental.pallas import tpu as pltpu
from jax.sharding import PartitionSpec as P

HEAD_DIM = 64
PAIR = 2 * HEAD_DIM
EPSILON = 1e-05
SCALE = HEAD_DIM ** (-0.5)
QUERY_ROWS = 256
ROWS = 128
FF_COLS = 256
MESH = pl.DeviceIdType.MESH
BF16, F32 = jnp.bfloat16, jnp.float32
VMEM_BYTES = 255 << 18
NT = (((1,), (1,)), ((), ()))
TN = (((0,), (0,)), ((), ()))


def dot(left, right, dims=(((1,), (0,)), ((), ()))):
    return lax.dot_general(left, right, dims, preferred_element_type=F32)


def iota(shape, dim):
    return lax.broadcasted_iota(jnp.int32, shape, dim)


def normalize(values):
    centered = values - jnp.mean(values, axis=-1, keepdims=True)
    variance = jnp.mean(centered * centered, axis=-1, keepdims=True)
    inverse = lax.rsqrt(variance + EPSILON)
    return centered * inverse, inverse


def norm_back(hat, inverse, gain, grad):
    scaled = grad * gain
    return inverse * (
        scaled
        - jnp.mean(scaled, axis=-1, keepdims=True)
        - hat * jnp.mean(scaled * hat, axis=-1, keepdims=True)
    )


def split_rows(base, size):
    return pl.ds(pl.multiple_of(base, size), size)


class Place:
    def __init__(self, cfg):
        self.__dict__.update(cfg)
        self.b = lax.axis_index("blk")
        self.e = lax.axis_index("exp")
        self.c = lax.rem(self.e, 2)
        self.pair = self.e - self.c
        self.sibling = self.pair + 1 - self.c

    def greet(self):
        bar = pltpu.get_barrier_semaphore()

        def exp_peer(k, _):
            pl.semaphore_signal(
                bar, 1, device_id=(self.b, lax.rem(self.e + k, self.ne)), device_id_type=MESH
            )

        def blk_peer(k, _):
            there = lax.rem(self.b + k, self.nb)
            pl.semaphore_signal(bar, 1, device_id=(there, self.e), device_id_type=MESH)
            pl.semaphore_signal(bar, 1, device_id=(there, self.sibling), device_id_type=MESH)

        lax.fori_loop(1, self.ne, exp_peer, None)
        lax.fori_loop(1, self.nb, blk_peer, None)
        pl.semaphore_wait(bar, self.ne - 1 + 2 * (self.nb - 1))

    def is_me(self, there):
        return there[0] * self.ne + there[1] == self.b * self.ne + self.e


def remote(src, dst, send_sem, recv_sem, there):
    return pltpu.make_async_remote_copy(
        src, dst, send_sem, recv_sem, device_id=there, device_id_type=MESH
    )


def push(me, src, dst, send_sem, recv_sem, there):
    mine = me.is_me(there)

    @pl.when(mine)
    def _():
        pltpu.make_async_copy(src, dst, recv_sem).start()

    @pl.when(jnp.logical_not(mine))
    def _():
        remote(src, dst, send_sem, recv_sem, there).start()


def push_done(me, src, dst, send_sem, recv_sem, there):
    @pl.when(jnp.logical_not(me.is_me(there)))
    def _():
        remote(src, dst, send_sem, recv_sem, there).wait_send()


def landed(dst, recv_sem):
    pltpu.make_async_copy(dst, dst, recv_sem).wait()


def exchange_start(me, src, dst, send_sem, recv_sem, size):
    def one(k, _):
        there = lax.rem(me.e + k, me.ne)
        remote(
            src.at[split_rows(there * size, size)],
            dst.at[split_rows(me.e * size, size)],
            send_sem.at[k],
            recv_sem.at[k],
            (me.b, there),
        ).start()

    own = split_rows(me.e * size, size)
    pltpu.make_async_copy(src.at[own], dst.at[own], recv_sem.at[0]).start()
    lax.fori_loop(1, me.ne, one, None)


def exchange_wait(me, src, dst, send_sem, recv_sem, size):
    own = split_rows(me.e * size, size)
    landed(dst.at[own], recv_sem.at[0])

    def one(k, _):
        source = lax.rem(me.e + me.ne - k, me.ne)
        landed(dst.at[split_rows(source * size, size)], recv_sem.at[k])

    lax.fori_loop(1, me.ne, one, None)


def exchange_sent(me, src, dst, send_sem, recv_sem, size):
    def one(k, _):
        there = lax.rem(me.e + k, me.ne)
        remote(
            src.at[split_rows(there * size, size)],
            dst.at[split_rows(me.e * size, size)],
            send_sem.at[k],
            recv_sem.at[k],
            (me.b, there),
        ).wait_send()

    lax.fori_loop(1, me.ne, one, None)


def token_slots(me, idx):
    rows = idx.shape[1]
    hot = (iota((128, rows), 0) == idx).astype(F32)
    earlier = (iota((rows, rows), 0) < iota((rows, rows), 1)).astype(F32).astype(BF16)
    ahead = dot(hot.astype(BF16), earlier)
    slot = jnp.sum(ahead * hot, axis=0, keepdims=True).astype(jnp.int32) + idx * me.cap
    return slot, jnp.sum(hot, axis=1, keepdims=True)[0 : me.experts]


def slots_by_token(me, slot):
    shape = (me.experts * me.cap, slot.shape[1])
    return (iota(shape, 0) == slot).astype(F32).astype(BF16)


def head_masks():
    lane = iota((1, PAIR), 1)
    first = (lane < HEAD_DIM).astype(F32).astype(BF16)
    second = (lane >= HEAD_DIM).astype(F32).astype(BF16)
    return first, second


def gelu_parts(u):
    root = 0.7978845608028654
    cubic = 0.044715
    square = u * u
    t = jnp.tanh(root * u * (1.0 + cubic * square))
    value = 0.5 * u * (1.0 + t)
    slope = 0.5 * (1.0 + t) + (0.5 * root) * u * (1.0 - t * t) * (1.0 + 3.0 * cubic * square)
    return value, slope


class Refs:
    def __init__(self, names, refs):
        self.__dict__.update(zip(names, refs, strict=True))


class ExpertSums:
    def __init__(self, me, r):
        self.me, self.r = me, r
        self.hi, self.lo = lax.div(me.b, 2), lax.rem(me.b, 2)
        self.other = 1 - self.lo
        self.count = me.nb // 2
        self.size = me.ff // me.nb

    def turn(self, step):
        return lax.rem(self.hi + step, self.count)

    def span(self, hi, lo):
        return pl.ds(pl.multiple_of((2 * hi + lo) * self.size, 128), self.size)

    def in_first(self, hi):
        r = self.r
        there = (2 * self.hi + self.other, self.me.e)
        return remote(
            r.win.at[:, self.span(hi, self.other)], r.in1.at[hi], r.in1s.at[hi], r.in1r.at[hi], there
        )

    def in_second(self, step):
        r, hi = self.r, self.turn(step)
        return remote(
            r.win.at[:, self.span(hi, self.lo)],
            r.in2.at[step - 1],
            r.in2s.at[step - 1],
            r.in2r.at[step - 1],
            (2 * hi + self.lo, self.me.e),
        )

    def out_first(self, step, lo):
        r, hi = self.r, self.turn(step)
        return remote(
            r.wout.at[self.span(hi, lo)],
            r.out1.at[step - 1, lo],
            r.out1s.at[step - 1, lo],
            r.out1r.at[step - 1, lo],
            (2 * hi + self.lo, self.me.e),
        )

    def out_second(self):
        r = self.r
        return remote(
            r.wout.at[self.span(self.hi, self.other)],
            r.out2,
            r.out2s,
            r.out2r,
            (2 * self.hi + self.other, self.me.e),
        )

    def after_part(self, n):
        step = lax.div(n, 2) + 1
        lo = lax.rem(self.other + n, 2)

        @pl.when(lax.rem(n, 2) == 0)
        def _():
            self.in_first(self.turn(step)).start()

        @pl.when(step < self.count)
        def _():
            self.out_first(step, lo).start()

    def second_add(self):
        r = self.r
        for step in range(1, self.count):
            hi = self.turn(step)
            landed(r.in1.at[hi], r.in1r.at[hi])
            here = self.span(hi, self.lo)

            def in_rows(n, _, hi=hi, here=here):
                rows = split_rows(n * ROWS, ROWS)
                r.win[rows, here] = (
                    r.win[rows, here].astype(F32) + r.in1[hi, rows, :].astype(F32)
                ).astype(BF16)

            lax.fori_loop(0, self.me.width // ROWS, in_rows, None)
        for step in range(1, self.count):
            landed(r.out1.at[step - 1, self.other], r.out1r.at[step - 1, self.other])
        base = (2 * self.hi + self.other) * self.size

        def out_rows(n, _):
            here, rows = split_rows(base + n * ROWS, ROWS), split_rows(n * ROWS, ROWS)
            total = r.wout[here, :].astype(F32)
            for step in range(1, self.count):
                total += r.out1[step - 1, self.other, rows, :].astype(F32)
            r.wout[here, :] = total.astype(BF16)

        lax.fori_loop(0, self.size // ROWS, out_rows, None)

    def second_send(self):
        for step in range(1, self.count):
            self.in_second(step).start()
        self.out_second().start()

    def total_in(self, into):
        r = self.r
        landed(r.in1.at[self.hi], r.in1r.at[self.hi])
        for step in range(1, self.count):
            landed(r.in2.at[step - 1], r.in2r.at[step - 1])

        def in_rows(n, _):
            rows = split_rows(n * ROWS, ROWS)
            total = r.win[rows, self.span(self.hi, self.lo)].astype(F32)
            total += r.in1[self.hi, rows, :].astype(F32)
            for step in range(1, self.count):
                total += r.in2[step - 1, rows, :].astype(F32)
            into[rows, 0 : self.size] = total

        lax.fori_loop(0, self.me.width // ROWS, in_rows, None)

    def total_out(self, into):
        r = self.r
        for step in range(1, self.count):
            landed(r.out1.at[step - 1, self.lo], r.out1r.at[step - 1, self.lo])
        landed(r.out2, r.out2r)
        base = (2 * self.hi + self.lo) * self.size

        def out_rows(n, _):
            rows = split_rows(n * ROWS, ROWS)
            total = r.wout[split_rows(base + n * ROWS, ROWS), :].astype(F32)
            for step in range(1, self.count):
                total += r.out1[step - 1, self.lo, rows, :].astype(F32)
            into[rows, :] = total + r.out2[rows, :].astype(F32)

        lax.fori_loop(0, self.size // ROWS, out_rows, None)

    def sent(self):
        for step in range(1, self.count + 1):
            self.in_first(self.turn(step)).wait_send()
            if step < self.count:
                self.in_second(step).wait_send()
                for lo in range(2):
                    self.out_first(step, lo).wait_send()
        self.out_second().wait_send()


class SharedSum:
    def __init__(self, me, r, p, blk_first):
        self.me, self.r, self.p = me, r, p
        z = lax.div(me.e, 2)
        nz = me.ne // 2
        blk = (me.b, me.nb, lambda t: (t, me.e))
        along_z = (z, nz, lambda t: (me.b, 2 * t + me.c))
        self.first, self.second = (blk, along_z) if blk_first else (along_z, blk)
        self.outer = me.width // self.first[1]
        self.inner = self.outer // self.second[1]

    def outer_rows(self, t):
        return split_rows(t * self.outer, self.outer)

    def inner_rows(self, t, s):
        return split_rows(t * self.outer + s * self.inner, self.inner)

    def view(self, rows, core):
        me, r, p = self.me, self.r, self.p
        if p < 3:
            return r.shared.at[
                pl.ds(0, 3), rows, pl.ds(pl.multiple_of(core * me.half_width + p * PAIR, PAIR), PAIR)
            ]
        return r.shared.at[
            3, rows, pl.ds(pl.multiple_of(core * me.half_width, PAIR), me.half_width)
        ]

    def peer(self, axis, k):
        return lax.rem(axis[0] + k, axis[1])

    def source(self, axis, k):
        return lax.rem(axis[0] + axis[1] - k, axis[1])

    def move1(self, k):
        r, p = self.r, self.p
        t = self.peer(self.first, k)
        return remote(
            r.part.at[p, self.outer_rows(t)],
            r.got1.at[p, k, pl.ds(0, self.outer)],
            r.s1.at[p, k],
            r.r1.at[p, k],
            self.first[2](t),
        )

    def move2(self, k):
        r, p = self.r, self.p
        t = self.peer(self.second, k)
        return remote(
            r.got1.at[p, 0, split_rows(t * self.inner, self.inner)],
            r.got2.at[p, k],
            r.s2.at[p, k],
            r.r2.at[p, k],
            self.second[2](t),
        )

    def move3(self, k):
        r, p = self.r, self.p
        here = self.view(self.inner_rows(self.first[0], self.second[0]), self.me.c)
        return remote(
            here, here, r.s3.at[p, k], r.r3.at[p, k], self.second[2](self.peer(self.second, k))
        )

    def move4(self, k):
        r, p = self.r, self.p
        here = self.view(self.outer_rows(self.first[0]), self.me.c)
        return remote(
            here, here, r.s4.at[p, k], r.r4.at[p, k], self.first[2](self.peer(self.first, k))
        )

    def move5(self):
        r, p = self.r, self.p
        here = self.view(pl.ds(0, self.me.width), self.me.c)
        return remote(here, here, r.s5.at[p], r.r5.at[p], (self.me.b, self.me.sibling))

    def stage1(self):
        for k in range(1, self.first[1]):
            self.move1(k).start()

    def stage2(self):
        r, p = self.r, self.p
        total = r.part[p, self.outer_rows(self.first[0])].astype(F32)
        for k in range(1, self.first[1]):
            here = r.got1.at[p, k, pl.ds(0, self.outer)]
            landed(here, r.r1.at[p, k])
            total += here[...].astype(F32)
        r.got1[p, 0, 0 : self.outer, :] = total.astype(BF16)
        for k in range(1, self.second[1]):
            self.move2(k).start()

    def stage3(self):
        r, p = self.r, self.p
        total = r.got1[p, 0, split_rows(self.second[0] * self.inner, self.inner)].astype(F32)
        for k in range(1, self.second[1]):
            landed(r.got2.at[p, k], r.r2.at[p, k])
            total += r.got2[p, k].astype(F32)
        total = total.astype(BF16)
        here = self.view(self.inner_rows(self.first[0], self.second[0]), self.me.c)
        if p < 3:
            for j in range(3):
                here[j] = total[:, j * PAIR : (j + 1) * PAIR]
        else:
            here[...] = total
        for k in range(1, self.second[1]):
            self.move3(k).start()

    def stage4(self):
        for k in range(1, self.second[1]):
            rows = self.inner_rows(self.first[0], self.source(self.second, k))
            landed(self.view(rows, self.me.c), self.r.r3.at[self.p, k])
        for k in range(1, self.first[1]):
            self.move4(k).start()

    def stage5(self):
        for k in range(1, self.first[1]):
            rows = self.outer_rows(self.source(self.first, k))
            landed(self.view(rows, self.me.c), self.r.r4.at[self.p, k])
        self.move5().start()

    def end(self):
        landed(self.view(pl.ds(0, self.me.width), 1 - self.me.c), self.r.r5.at[self.p])
        for k in range(1, self.first[1]):
            self.move1(k).wait_send()
            self.move4(k).wait_send()
        for k in range(1, self.second[1]):
            self.move2(k).wait_send()
            self.move3(k).wait_send()
        self.move5().wait_send()


class AllSum:
    def __init__(self, me, own, by_exp, by_blk, sems):
        self.me, self.own, self.by_exp, self.by_blk = me, own, by_exp, by_blk
        self.es, self.er, self.bs, self.br = sems

    def exp_move(self, k):
        me = self.me
        there = (me.b, lax.rem(me.e + k, me.ne))
        return remote(self.own, self.by_exp.at[me.e], self.es.at[k], self.er.at[k], there)

    def blk_move(self, k):
        me = self.me
        here = self.by_blk.at[me.b]
        there = (lax.rem(me.b + k, me.nb), me.e)
        return remote(here, here, self.bs.at[k], self.br.at[k], there)

    def start(self):
        lax.fori_loop(1, self.me.ne, lambda k, _: self.exp_move(k).start(), None)
        self.by_exp[self.me.e] = self.own[...]

    def middle(self):
        me = self.me

        def arrived(k, _):
            landed(self.by_exp.at[lax.rem(me.e + me.ne - k, me.ne)], self.er.at[k])

        lax.fori_loop(1, me.ne, arrived, None)
        self.by_blk[me.b] = jnp.sum(self.by_exp[...], axis=0)
        for k in range(1, me.nb):
            self.blk_move(k).start()

    def total(self):
        me = self.me
        for k in range(1, me.nb):
            landed(self.by_blk.at[lax.rem(me.b + me.nb - k, me.nb)], self.br.at[k])
        return jnp.sum(self.by_blk[...], axis=0)

    def sent(self):
        lax.fori_loop(1, self.me.ne, lambda k, _: self.exp_move(k).wait_send(), None)
        for k in range(1, self.me.nb):
            self.blk_move(k).wait_send()


def layer_kernel(cfg, names, *refs):
    me = Place(cfg)
    r = Refs(names, refs)
    half = me.span // 2
    pairs = me.half_width // PAIR
    blocks = me.length // QUERY_ROWS
    slots = me.experts * me.cap
    r.ysend, r.yback = r.g, r.du
    r.swap, r.da_in = r.took.at[pl.ds(0, me.rows)], r.back.at[pl.ds(0, me.rows)]
    r.xin, r.o_send, r.lse_cols, r.dh_send = r.mail, r.g, r.dk_sum, r.disp
    gain1, bias1, gain2, bias2 = (
        v[...].reshape(1, me.width) for v in (r.gain1, r.bias1, r.gain2, r.bias2)
    )
    loads = {}
    for name in ("x", "og", "wo", "win", "wout"):
        loads[name] = pltpu.make_async_copy(
            getattr(r, name + "_hbm"), getattr(r, name), r.lsem.at[len(loads)]
        )
    for p in range(pairs):
        for j, matrix in enumerate((r.wq_hbm, r.wk_hbm, r.wv_hbm)):
            src = matrix.at[:, pl.ds(pl.multiple_of(me.c * me.half_width + p * PAIR, PAIR), PAIR)]
            loads["w", p, j] = pltpu.make_async_copy(
                src, r.w.at[p, :, pl.ds(j * PAIR, PAIR)], r.lsem.at[len(loads)]
            )
    for load in loads.values():
        load.start()
    me.greet()

    def row_moves():
        for s in range(me.seqs):
            for h in range(2):
                yield (
                    r.x_hbm.at[pl.ds(s * me.span + h * half, half)],
                    r.xin.at[split_rows(me.b * half, half)],
                    r.xs.at[2 * s + h],
                    r.xr.at[me.b],
                    (me.c * me.seqs + s, me.pair + h),
                )

    for move in row_moves():
        push(me, *move)

    slot, counts = token_slots(me, r.idx[...])
    r.cnt[...] = jnp.broadcast_to(counts, r.cnt.shape)
    count_sum = AllSum(me, r.cnt, r.cnt_exp, r.cnt_blk, (r.ces, r.cer, r.cbs, r.cbr))
    count_sum.start()
    r.idx_col[...] = jnp.transpose(
        jnp.broadcast_to(r.idx[...].astype(F32), (128, me.rows))
    )
    loads["og"].wait()
    r.dh_send[...] = dot(slots_by_token(me, slot), r.og[...]).astype(BF16)
    exchange_start(me, r.dh_send, r.dh, r.ds, r.dr, me.cap)

    def forward_move(j):
        rows = split_rows(j * me.span + me.c * half, half)
        return remote(r.a.at[rows], r.a.at[rows], r.fws.at[j], r.fwr.at[j], (me.b, me.sibling))

    for j in range(me.nb):
        landed(r.xin.at[pl.ds(j * half, half)], r.xr.at[j])
        hat, _ = normalize(r.xin[pl.ds(j * half, half), :].astype(F32))
        r.a[split_rows(j * me.span + me.c * half, half), :] = (hat * gain1 + bias1).astype(BF16)
        forward_move(j).start()

    for p in range(pairs):
        for j in range(3):
            loads["w", p, j].wait()
    first, second = head_masks()
    spans = QUERY_ROWS // me.span
    lane = iota((1, PAIR), 1)
    visible = iota((QUERY_ROWS, QUERY_ROWS), 1) <= iota((QUERY_ROWS, QUERY_ROWS), 0)
    home = me.pair + lax.div(me.b, me.seqs)
    columns = pl.ds(pl.multiple_of(me.c * me.half_width, PAIR), me.half_width)

    def o_move(j):
        return (
            r.o_send.at[
                pl.ds(j * me.span % me.rows, me.span),
                pl.ds(j * me.span // me.rows * me.half_width, me.half_width),
            ],
            r.o.at[split_rows(lax.rem(me.b, me.seqs) * me.span, me.span), columns],
            r.os.at[j],
            r.osr.at[2 * lax.rem(me.b, me.seqs) + me.c],
            (j, home),
        )

    for i in range(blocks):
        for j in range(i * spans, (i + 1) * spans):
            theirs = split_rows(j * me.span + (1 - me.c) * half, half)
            landed(r.a.at[theirs], r.fwr.at[j])
        here = pl.ds(i * QUERY_ROWS, QUERY_ROWS)

        def pair_of_heads(p, _, i=i, here=here):
            lanes = split_rows(p * PAIR, PAIR)
            qkv = dot(r.a[here, :], r.w[p]).astype(BF16)
            queries = qkv[:, 0:PAIR] * jnp.asarray(SCALE, BF16)
            r.q[here, lanes] = queries
            r.k[here, lanes] = qkv[:, PAIR : 2 * PAIR]
            r.v[here, lanes] = qkv[:, 2 * PAIR : 3 * PAIR]
            parts = [pl.ds(i * QUERY_ROWS, QUERY_ROWS)]
            if i:
                parts.append(pl.ds(0, i * QUERY_ROWS))
            done = []
            for h, mask in enumerate((first, second)):
                masked = queries * mask
                scores = [dot(masked, r.k[part, lanes], NT) for part in parts]
                scores[0] = jnp.where(visible, scores[0], -1e30)
                peak = functools.reduce(
                    jnp.maximum, [jnp.max(s, axis=1, keepdims=True) for s in scores]
                )
                powers = [jnp.exp(s - peak) for s in scores]
                total = sum(jnp.sum(s, axis=1, keepdims=True) for s in powers)
                mixed = sum(
                    dot(s.astype(BF16), r.v[part, lanes]) for s, part in zip(powers, parts)
                )
                done.append(mixed / total)
                r.lse_cols[here, :] = jnp.where(
                    lane == 2 * p + h, peak + jnp.log(total), r.lse_cols[here, :]
                )
            base = i * QUERY_ROWS // me.rows * me.half_width
            r.o_send[
                pl.ds(i * QUERY_ROWS % me.rows, QUERY_ROWS),
                pl.ds(pl.multiple_of(base + p * PAIR, PAIR), PAIR),
            ] = jnp.where(lane < HEAD_DIM, done[0], done[1]).astype(BF16)

        lax.fori_loop(0, pairs, pair_of_heads, None)
        for j in range(i * spans, (i + 1) * spans):
            push(me, *o_move(j))
        if i == 0:
            count_sum.middle()
    r.lse[...] = jnp.transpose(r.lse_cols[...])[0:8, :]
    for j in range(me.nb):
        forward_move(j).wait_send()
        push_done(me, *o_move(j))
    for move in row_moves():
        push_done(me, *move)
    for name in ("x", "wo"):
        loads[name].wait()
    exchange_wait(me, r.dh_send, r.dh, r.ds, r.dr, me.cap)
    exchange_sent(me, r.dh_send, r.dh, r.ds, r.dr, me.cap)

    expert_lane = iota((ROWS, me.experts), 1)
    r.sums[...] = jnp.zeros_like(r.sums)
    r.mass[...] = jnp.zeros_like(r.mass)
    for s in range(me.seqs):
        for h in range(2):
            landed(
                r.o.at[pl.ds(s * me.span, me.span), pl.ds(h * me.half_width, me.half_width)],
                r.osr.at[2 * s + h],
            )

    def token_rows(n, _):
        here = split_rows(n * ROWS, ROWS)
        hidden = r.x[here, :].astype(F32) + dot(r.o[here, :], r.wo[...])
        r.h1[here, :] = hidden
        hat, _ = normalize(hidden)
        normed = (hat * gain2 + bias2).astype(BF16)
        r.mail[here, :] = normed
        logits = dot(normed, r.router[...], NT)
        hot = r.idx_col[here, 0 : me.experts].astype(jnp.int32) == expert_lane
        value = jax.nn.sigmoid(jnp.sum(jnp.where(hot, logits, 0.0), axis=1, keepdims=True))
        r.gate[here, :] = value
        r.mass[...] += jnp.sum(jnp.where(hot, value, 0.0), axis=0, keepdims=True)

    lax.fori_loop(0, me.rows // ROWS, token_rows, None)
    takes = slots_by_token(me, slot)
    r.disp[...] = dot(takes, r.mail[...]).astype(BF16)
    exchange_start(me, r.disp, r.took, r.ns, r.nr, me.cap)
    loads["win"].wait()
    loads["wout"].wait()
    exchange_wait(me, r.disp, r.took, r.ns, r.nr, me.cap)
    exchange_sent(me, r.disp, r.took, r.ns, r.nr, me.cap)

    lanes = iota((slots, me.experts), 1)
    logits = jnp.sum(
        jnp.where(lanes == me.e, dot(r.took[...], r.router[...], NT), 0.0), axis=1, keepdims=True
    )
    value = jax.nn.sigmoid(logits)
    r.disp[...] = (value * r.dh[...].astype(F32)).astype(BF16)
    r.yf[0:slots, :] = jnp.zeros((slots, me.width), F32)
    r.made[...] = jnp.zeros_like(r.made)
    sums = ExpertSums(me, r)
    slot_rows = slots // 2

    def expert_part(n, _):
        hi, lo = sums.turn(lax.div(n, 2) + 1), lax.rem(sums.other + n, 2)
        base = (2 * hi + lo) * sums.size

        def hidden_columns(f, _):
            here = pl.ds(pl.multiple_of(base + f * sums.tile, 128), sums.tile)
            there = pl.ds(pl.multiple_of(f * sums.tile, 128), sums.tile)

            def hidden_rows(n, _):
                rows = split_rows(n * slot_rows, slot_rows)
                act, slope = gelu_parts(dot(r.took[rows, :], r.win[:, here]))
                r.g[rows, there] = act.astype(BF16)
                r.du[rows, there] = (dot(r.disp[rows, :], r.wout[here, :], NT) * slope).astype(BF16)

            lax.fori_loop(0, slots // slot_rows, hidden_rows, None)

        lax.fori_loop(0, sums.size // sums.tile, hidden_columns, None)
        part = sums.span(hi, lo)

        def model_columns(f, _):
            here = split_rows(f * FF_COLS, FF_COLS)
            r.yf[0:slots, here] += dot(r.g[:, 0 : sums.size], r.wout[part, here])
            r.made[0:slots, here] += dot(r.du[:, 0 : sums.size], r.win[here, part], NT)

        lax.fori_loop(0, me.width // FF_COLS, model_columns, None)

        def weight_columns(f, _):
            here = pl.ds(pl.multiple_of(base + f * sums.tile, 128), sums.tile)
            there = pl.ds(pl.multiple_of(f * sums.tile, 128), sums.tile)
            r.win[:, here] = dot(r.took[...], r.du[:, there], TN).astype(BF16)
            r.wout[here, :] = dot(r.g[:, there], r.disp[...], TN).astype(BF16)

        lax.fori_loop(0, sums.size // sums.tile, weight_columns, None)
        sums.after_part(n)

    sums.tile = min(FF_COLS, sums.size) if sums.size % FF_COLS == 0 else PAIR
    lax.fori_loop(0, me.nb, expert_part, None)

    weights = (count_sum.total() - me.mean_load) / me.mean_load
    weight = jnp.sum(jnp.where(iota(weights.shape, 0) == me.e, weights, 0.0), axis=0, keepdims=True)
    weight = weight[:, 0:1]
    r.ysend[...] = r.yf[0:slots, :].astype(BF16)
    dgate = (
        jnp.sum(r.dh[...].astype(F32) * r.ysend[...].astype(F32), axis=1, keepdims=True)
        + weight / me.tokens
    )
    dlogits = jnp.where(lanes == me.e, dgate * value * (1.0 - value), 0.0).astype(BF16)
    r.disp[...] = (r.made[0:slots, :] + dot(dlogits, r.router[...])).astype(BF16)
    exchange_start(me, r.disp, r.back, r.rs, r.rr, me.cap)
    r.sums[2 : 2 + me.experts, :] = dot(dlogits, r.took[...], TN)
    r.sums[2 + me.experts : 3 + me.experts, 0 : me.experts] = r.mass[...]
    sums.second_add()
    exchange_wait(me, r.disp, r.back, r.rs, r.rr, me.cap)

    r.made[0 : me.rows, :] = dot(takes, r.back[...], TN)

    def norm_rows(n, _):
        here = split_rows(n * ROWS, ROWS)
        grad = r.made[here, :]
        hat, inverse = normalize(r.h1[here, :])
        r.sums[0:1, :] += jnp.sum(grad * hat, axis=0, keepdims=True)
        r.sums[1:2, :] += jnp.sum(grad, axis=0, keepdims=True)
        total = r.og[here, :].astype(F32) + norm_back(hat, inverse, gain2, grad)
        r.dh1[here, :] = total
        r.mail[here, :] = dot(total.astype(BF16), r.wo[...], NT).astype(BF16)

    def do_moves(s):
        for h in range(2):
            yield (
                r.mail.at[pl.ds(s * me.span, me.span), pl.ds(h * me.half_width, me.half_width)],
                r.do.at[split_rows(me.b * me.span, me.span)],
                r.dos.at[2 * s + h],
                r.dor.at[me.b],
                (me.c * me.seqs + s, me.pair + h),
            )

    steps = me.span // ROWS
    for s in range(me.seqs):
        lax.fori_loop(s * steps, (s + 1) * steps, norm_rows, None)
        for move in do_moves(s):
            push(me, *move)
    sums.second_send()
    early = AllSum(me, r.sums, r.sum_exp, r.sum_blk, (r.es, r.er, r.bs, r.br))
    early.start()
    exchange_start(me, r.ysend, r.yback, r.ys, r.yr, me.cap)

    def output_columns(core):
        cols = pl.ds(pl.multiple_of(core * me.half_width, PAIR), me.half_width)
        return dot(r.o[...], r.dh1[:, cols].astype(BF16), TN)

    r.part[0] = output_columns(1 - me.c).astype(BF16)
    o_swap = remote(r.part.at[0], r.ogot, r.ows, r.owr, (me.b, me.sibling))
    o_swap.start()
    own_columns = output_columns(me.c)
    o_swap.wait()
    r.part[3] = (own_columns + r.ogot[...].astype(F32)).astype(BF16)
    pieces = [SharedSum(me, r, p, blk_first=p in (1, 2)) for p in range(4)] if me.sum_here else []
    if pieces:
        pieces[3].stage1()

    r.made[...] = jnp.zeros_like(r.made)
    for j in range(me.nb):
        landed(r.do.at[pl.ds(j * me.span, me.span)], r.dor.at[j])
    visible = iota((QUERY_ROWS, QUERY_ROWS), 0) <= iota((QUERY_ROWS, QUERY_ROWS), 1)

    def pair_back(n, _):
        lanes = split_rows(n * PAIR, PAIR)
        r.dk_sum[...] = jnp.zeros_like(r.dk_sum)
        r.dv_sum[...] = jnp.zeros_like(r.dv_sum)
        for i in range(blocks):
            here = pl.ds(i * QUERY_ROWS, QUERY_ROWS)
            queries, grads = r.q[here, lanes], r.do[here, lanes]
            parts = [here]
            if i:
                parts.append(pl.ds(0, i * QUERY_ROWS))
            dq_block = jnp.zeros((QUERY_ROWS, PAIR), F32)
            for h, mask in enumerate((first, second)):
                qm, gm = queries * mask, grads * mask
                log_sums = r.lse[pl.ds(2 * n + h, 1), here]
                scores = [dot(r.k[part, lanes], qm, NT) for part in parts]
                powers = [jnp.exp(s - log_sums) for s in scores]
                powers[0] = jnp.where(visible, powers[0], 0.0)
                weighted = [
                    s * dot(r.v[part, lanes], gm, NT) for s, part in zip(powers, parts)
                ]
                delta = sum(jnp.sum(t, axis=0, keepdims=True) for t in weighted)
                for s, t, part in zip(powers, weighted, parts):
                    ds = (t - s * delta).astype(BF16)
                    r.dv_sum[part, :] += dot(s.astype(BF16), gm)
                    r.dk_sum[part, :] += dot(ds, qm)
                    dq_block += dot(ds, r.k[part, lanes] * mask, TN)
            r.dqkv[here, 0:PAIR] = (dq_block * SCALE).astype(BF16)
        r.dqkv[:, PAIR : 2 * PAIR] = r.dk_sum[...].astype(BF16)
        r.dqkv[:, 2 * PAIR : 3 * PAIR] = r.dv_sum[...].astype(BF16)
        r.part[n] = dot(r.a[...], r.dqkv[...], TN).astype(BF16)

        def normed_columns(f, _):
            cols = split_rows(f * FF_COLS, FF_COLS)
            r.made[:, cols] += dot(r.dqkv[...], r.w[n, cols, :], NT)

        lax.fori_loop(0, me.width // FF_COLS, normed_columns, None)
        if pieces:

            @pl.when(n == 0)
            def _():
                pieces[0].stage1()
                pieces[3].stage2()

            @pl.when(n == 1)
            def _():
                pieces[1].stage1()
                pieces[0].stage2()
                pieces[3].stage3()

            @pl.when(n == 2)
            def _():
                pieces[2].stage1()
                pieces[1].stage2()
                pieces[0].stage3()
                pieces[3].stage4()

    lax.fori_loop(0, pairs, pair_back, None)
    early.middle()

    for s in range(me.seqs):
        for move in do_moves(s):
            push_done(me, *move)
    for j in range(me.nb):
        theirs = split_rows(j * me.span + (1 - me.c) * half, half)
        r.mail[pl.ds(j * half, half), :] = r.made[theirs, :].astype(BF16)
    swap = remote(r.mail, r.swap, r.ss, r.sr, (me.b, me.sibling))
    swap.start()
    exchange_wait(me, r.ysend, r.yback, r.ys, r.yr, me.cap)
    r.yf[0 : me.rows, :] = dot(takes, r.yback[...], TN)

    def out_rows(n, _):
        here = split_rows(n * ROWS, ROWS)
        r.out[here, :] = (r.h1[here, :] + r.gate[here, :] * r.yf[here, :]).astype(BF16)

    lax.fori_loop(0, me.rows // ROWS, out_rows, None)
    swap.wait()
    def da_move(j):
        return (
            r.mail.at[pl.ds(j * half, half)],
            r.da_in.at[split_rows(lax.rem(me.b, me.seqs) * me.span + me.c * half, half)],
            r.fs.at[j],
            r.fr.at[2 * lax.rem(me.b, me.seqs) + me.c],
            (j, home),
        )

    for j in range(me.nb):
        mine = r.made[split_rows(j * me.span + me.c * half, half), :]
        rows = pl.ds(j * half, half)
        r.mail[rows, :] = (mine + r.swap[rows, :].astype(F32)).astype(BF16)
        push(me, *da_move(j))
    if pieces:
        pieces[2].stage2()
        pieces[1].stage3()
        pieces[0].stage4()
        pieces[3].stage5()
    for s in range(me.seqs):
        for h in range(2):
            landed(r.da_in.at[pl.ds(s * me.span + h * half, half)], r.fr.at[2 * s + h])

    r.late[...] = jnp.zeros_like(r.late)
    tiles = me.width // FF_COLS

    def first_norm_rows(n, _):
        here = split_rows(n * ROWS, ROWS)
        grad = r.da_in[here, :].astype(F32)
        hat, inverse = normalize(r.x[here, :].astype(F32))
        gain_part = jnp.sum(grad * hat, axis=0, keepdims=True)
        bias_part = jnp.sum(grad, axis=0, keepdims=True)
        for j in range(tiles):
            cols = slice(j * FF_COLS, (j + 1) * FF_COLS)
            r.late[j : j + 1, :] += gain_part[:, cols]
            r.late[tiles + j : tiles + j + 1, :] += bias_part[:, cols]
        r.dx[here, :] = (r.dh1[here, :] + norm_back(hat, inverse, gain1, grad)).astype(BF16)

    lax.fori_loop(0, me.rows // ROWS, first_norm_rows, None)
    late = AllSum(me, r.late, r.late_exp, r.late_blk, (r.les, r.ler, r.lbs, r.lbr))
    late.start()
    if pieces:
        pieces[2].stage3()
        pieces[1].stage4()
        pieces[0].stage5()
    late.middle()
    if pieces:
        pieces[2].stage4()
        pieces[1].stage5()

    size = sums.size
    sums.total_in(r.made)
    store_in = pltpu.make_async_copy(
        r.made.at[pl.ds(0, me.width), pl.ds(0, size)], r.dwin, r.fsem.at[0]
    )
    store_in.start()
    sums.total_out(r.yf)
    store_out = pltpu.make_async_copy(r.yf.at[pl.ds(0, size)], r.dwout, r.fsem.at[1])
    store_out.start()
    if pieces:
        pieces[2].stage5()
    early_total = early.total()
    late_total = late.total()
    r.small[0 : r.sums.shape[0], :] = early_total
    for j in range(tiles):
        cols = slice(j * FF_COLS, (j + 1) * FF_COLS)
        r.small[me.experts + 4 : me.experts + 5, cols] = late_total[j : j + 1, :]
        r.small[me.experts + 5 : me.experts + 6, cols] = late_total[tiles + j : tiles + j + 1, :]
    own_weight = jnp.transpose(jnp.broadcast_to(weights, (weights.shape[0], 128)))[0:1, :]
    mass = early_total[2 + me.experts : 3 + me.experts, 0 : me.experts]
    r.small[me.experts + 3 : me.experts + 4, 0:1] = (
        jnp.sum(own_weight[:, 0 : me.experts] * mass, axis=1, keepdims=True) / me.tokens
    )
    for each in (count_sum, early, late):
        each.sent()
    exchange_sent(me, r.disp, r.back, r.rs, r.rr, me.cap)
    exchange_sent(me, r.ysend, r.yback, r.ys, r.yr, me.cap)
    for j in range(me.nb):
        push_done(me, *da_move(j))
    sums.sent()
    stores = [store_in, store_out]
    for piece in pieces:
        piece.end()
    if pieces:
        targets = [(r.shared.at[j], out) for j, out in enumerate((r.gq, r.gk, r.gv, r.go))]
    else:
        targets = [(r.part, r.own_part)]
    for n, (src, dst) in enumerate(targets):
        store = pltpu.make_async_copy(src, dst, r.fsem.at[2 + n])
        store.start()
        stores.append(store)
    for store in stores:
        store.wait()


def in_vmem(count):
    return [pl.BlockSpec(memory_space=pltpu.VMEM)] * count


def anywhere(count):
    return [pl.BlockSpec(memory_space=pl.ANY)] * count


def shards(
    tokens,
    output_grad,
    expert_index,
    query_weight,
    key_weight,
    value_weight,
    output_weight,
    router_weight,
    expert_in,
    expert_out,
    norm1_gain,
    norm1_bias,
    norm2_gain,
    norm2_bias,
):
    seqs, span, width = tokens.shape
    rows = seqs * span
    nb, ne = lax.axis_size("blk"), lax.axis_size("exp")
    length = span * nb
    experts = router_weight.shape[1]
    ff = expert_in.shape[2]
    cap = -(-max(2, rows * 5 // (4 * experts)) // 16) * 16
    slots = experts * cap
    token_total = rows * nb * ne
    half_width = width // 2
    cfg = dict(
        seqs=seqs, span=span, width=width, rows=rows, nb=nb, ne=ne, length=length,
        experts=experts, ff=ff, cap=cap, half_width=half_width, tokens=token_total,
        mean_load=token_total / experts,
    )
    dma = pltpu.SemaphoreType.DMA
    vmem = pltpu.VMEM
    hi = nb // 2
    size = ff // nb
    sum_rows = -(-(3 + experts) // 8) * 8
    cfg["sum_here"] = width % (8 * nb * ne) == 0
    outer = width // min(nb, ne // 2)
    inner = width // (nb * ne // 2)
    inputs = (
        ("idx", expert_index.reshape(1, rows), True),
        ("router", router_weight.T, True),
        ("gain1", norm1_gain, True),
        ("bias1", norm1_bias, True),
        ("gain2", norm2_gain, True),
        ("bias2", norm2_bias, True),
        ("x_hbm", tokens.reshape(rows, width), False),
        ("og_hbm", output_grad.reshape(rows, width), False),
        ("wo_hbm", output_weight, False),
        ("win_hbm", expert_in.reshape(width, ff), False),
        ("wout_hbm", expert_out.reshape(ff, width), False),
        ("wq_hbm", query_weight, False),
        ("wk_hbm", key_weight, False),
        ("wv_hbm", value_weight, False),
    )
    small_rows = -(-(6 + experts) // 8) * 8
    outputs = [
        ("out", (rows, width), BF16, True),
        ("dx", (rows, width), BF16, True),
        ("small", (small_rows, width), F32, True),
        ("dwin", (width, size), F32, False),
        ("dwout", (size, width), F32, False),
    ]
    if cfg["sum_here"]:
        outputs += [(n, (width, width), BF16, False) for n in ("gq", "gk", "gv", "go")]
    else:
        outputs.append(("own_part", (4, width, half_width), BF16, False))
    scratch = dict(
        win=vmem((width, ff), BF16),
        wout=vmem((ff, width), BF16),
        x=vmem((rows, width), BF16),
        og=vmem((rows, width), BF16),
        o=vmem((rows, width), BF16),
        wo=vmem((width, width), BF16),
        dh=vmem((slots, width), BF16),
        idx_col=vmem((rows, 128), F32),
        cnt=vmem((experts, 128), F32),
        cnt_exp=vmem((ne, experts, 128), F32),
        cnt_blk=vmem((nb, experts, 128), F32),
        q=vmem((length, half_width), BF16),
        k=vmem((length, half_width), BF16),
        v=vmem((length, half_width), BF16),
        a=vmem((length, width), BF16),
        lse=vmem((8, length), F32),
        w=vmem((half_width // PAIR, width, 3 * PAIR), BF16),
        h1=vmem((rows, width), F32),
        gate=vmem((rows, 1), F32),
        mass=vmem((1, experts), F32),
        mail=vmem((rows, width), BF16),
        disp=vmem((slots, width), BF16),
        took=vmem((slots, width), BF16),
        g=vmem((slots, width), BF16),
        du=vmem((slots, width), BF16),
        yf=vmem((max(slots, size), width), F32),
        made=vmem((length, width), F32),
        back=vmem((slots, width), BF16),
        dh1=vmem((rows, width), F32),
        do=vmem((length, half_width), BF16),
        ogot=vmem((width, half_width), BF16),
        dk_sum=vmem((length, PAIR), F32),
        dv_sum=vmem((length, PAIR), F32),
        dqkv=vmem((length, 3 * PAIR), BF16),
        sums=vmem((sum_rows, width), F32),
        sum_exp=vmem((ne, sum_rows, width), F32),
        sum_blk=vmem((nb, sum_rows, width), F32),
        late=vmem((8, FF_COLS), F32),
        late_exp=vmem((ne, 8, FF_COLS), F32),
        late_blk=vmem((nb, 8, FF_COLS), F32),
        part=vmem((4, width, half_width), BF16),
        in1=vmem((hi, width, size), BF16),
        in2=vmem((hi - 1, width, size), BF16),
        out1=vmem((hi - 1, 2, size, width), BF16),
        out2=vmem((size, width), BF16),
        in1s=dma((hi,)), in1r=dma((hi,)),
        in2s=dma((hi - 1,)), in2r=dma((hi - 1,)),
        out1s=dma((hi - 1, 2)), out1r=dma((hi - 1, 2)),
        out2s=dma, out2r=dma,
        lsem=dma((5 + 3 * (half_width // PAIR),)),
        fsem=dma((6,)),
        xs=dma((2 * seqs,)), xr=dma((nb,)),
        fws=dma((nb,)), fwr=dma((nb,)),
        os=dma((nb,)), osr=dma((2 * seqs,)),
        ds=dma((ne,)), dr=dma((ne,)),
        ces=dma((ne,)), cer=dma((ne,)), cbs=dma((nb,)), cbr=dma((nb,)),
        ns=dma((ne,)), nr=dma((ne,)),
        rs=dma((ne,)), rr=dma((ne,)),
        ys=dma((ne,)), yr=dma((ne,)),
        dos=dma((2 * seqs,)), dor=dma((nb,)),
        ows=dma, owr=dma,
        ss=dma, sr=dma,
        fs=dma((nb,)), fr=dma((2 * seqs,)),
        es=dma((ne,)), er=dma((ne,)), bs=dma((nb,)), br=dma((nb,)),
        les=dma((ne,)), ler=dma((ne,)), lbs=dma((nb,)), lbr=dma((nb,)),
    )
    if cfg["sum_here"]:
        scratch.update(
            shared=vmem((4, width, width), BF16),
            got1=vmem((4, max(nb, ne // 2), outer, half_width), BF16),
            got2=vmem((4, max(nb, ne // 2), inner, half_width), BF16),
            s5=dma((4,)),
            r5=dma((4,)),
        )
        for n in range(1, 5):
            scratch[f"s{n}"] = dma((4, max(nb, ne // 2)))
            scratch[f"r{n}"] = dma((4, max(nb, ne // 2)))
    names = [n for n, _, _ in inputs] + [n for n, _, _, _ in outputs] + list(scratch)
    out, dx, small, dwin, dwout, *wide = pl.pallas_call(
        functools.partial(layer_kernel, cfg, names),
        out_shape=[jax.ShapeDtypeStruct(shape, kind) for _, shape, kind, _ in outputs],
        in_specs=[(in_vmem if near else anywhere)(1)[0] for _, _, near in inputs],
        out_specs=[(in_vmem if near else anywhere)(1)[0] for _, _, _, near in outputs],
        scratch_shapes=list(scratch.values()),
        compiler_params=pltpu.CompilerParams(
            collective_id=1, has_side_effects=True, vmem_limit_bytes=VMEM_BYTES
        ),
        cost_estimate=pl.CostEstimate(
            flops=30 << 30, bytes_accessed=1 << 25, transcendentals=1 << 23
        ),
        name="layer",
    )(*[value for _, value, _ in inputs])
    if not cfg["sum_here"]:
        own = wide[0]
        own = jnp.concatenate(
            [
                own[:3].reshape(3, width, 3, PAIR).transpose(2, 1, 0, 3).reshape(3, width, half_width),
                own[3:],
            ]
        )
        core, empty = lax.rem(lax.axis_index("exp"), 2), jnp.zeros_like(own)
        wide = lax.psum(
            jnp.concatenate(
                [jnp.where(core == 0, own, empty), jnp.where(core == 0, empty, own)], axis=2
            ),
            ("blk", "exp"),
        )
    wide = [wide[n].astype(F32) for n in range(4)]
    return (
        out.reshape(seqs, span, width),
        small[experts + 3, 0],
        dx.reshape(seqs, span, width),
        *wide,
        small[2 : 2 + experts].T,
        dwin[None],
        dwout[None],
        small[experts + 4],
        small[experts + 5],
        small[0],
        small[1],
    )


def solution(mesh):
    return jax.shard_map(
        shards,
        mesh=mesh,
        in_specs=(
            P("exp", "blk", None),
            P("exp", "blk", None),
            P("blk", "exp", None, None),
            P(),
            P(),
            P(),
            P(),
            P(),
            P("exp", None, None),
            P("exp", None, None),
            P(),
            P(),
            P(),
            P(),
        ),
        out_specs=(
            P("exp", "blk", None),
            P(),
            P("exp", "blk", None),
            P(),
            P(),
            P(),
            P(),
            P(),
            P("exp", None, "blk"),
            P("exp", "blk", None),
            P(),
            P(),
            P(),
            P(),
        ),
        check_vma=False,
    )
```

```python
import functools

import jax
import jax.numpy as jnp
from jax import lax
from jax.experimental import pallas as pl
from jax.experimental.pallas import tpu as pltpu
from jax.sharding import PartitionSpec as P

HEAD_DIM = 64
PAIR = 2 * HEAD_DIM
EPSILON = 1e-05
SCALE = HEAD_DIM ** (-0.5)
QUERY_ROWS = 256
ROWS = 128
FF_COLS = 256
MESH = pl.DeviceIdType.MESH
BF16, F32 = jnp.bfloat16, jnp.float32
BLK_FIRST = (0, 1, 2)
PLAN = {
    "start": ((3, 1),),
    0: ((0, 1),),
    1: ((1, 1),),
    2: ((2, 1), (3, 2), (0, 2)),
    "rows sent": ((1, 2), (2, 2), (3, 3), (0, 3)),
    "rows done": ((1, 3), (2, 3), (3, 4), (0, 4)),
    "late": ((1, 4), (2, 4), (3, 5), (0, 5)),
    "last": ((1, 5), (2, 5)),
}
VMEM_BYTES = 255 << 18
NT = (((1,), (1,)), ((), ()))
TN = (((0,), (0,)), ((), ()))


def dot(left, right, dims=(((1,), (0,)), ((), ()))):
    return lax.dot_general(left, right, dims, preferred_element_type=F32)


def iota(shape, dim):
    return lax.broadcasted_iota(jnp.int32, shape, dim)


def normalize(values):
    centered = values - jnp.mean(values, axis=-1, keepdims=True)
    variance = jnp.mean(centered * centered, axis=-1, keepdims=True)
    inverse = lax.rsqrt(variance + EPSILON)
    return centered * inverse, inverse


def norm_back(hat, inverse, gain, grad):
    scaled = grad * gain
    return inverse * (
        scaled
        - jnp.mean(scaled, axis=-1, keepdims=True)
        - hat * jnp.mean(scaled * hat, axis=-1, keepdims=True)
    )


def split_rows(base, size):
    return pl.ds(pl.multiple_of(base, size), size)


class Place:
    def __init__(self, cfg):
        self.__dict__.update(cfg)
        self.b = lax.axis_index("blk")
        self.e = lax.axis_index("exp")
        self.c = lax.rem(self.e, 2)
        self.pair = self.e - self.c
        self.sibling = self.pair + 1 - self.c

    def greet(self):
        bar = pltpu.get_barrier_semaphore()

        def exp_peer(k, _):
            pl.semaphore_signal(
                bar, 1, device_id=(self.b, lax.rem(self.e + k, self.ne)), device_id_type=MESH
            )

        def blk_peer(k, _):
            there = lax.rem(self.b + k, self.nb)
            pl.semaphore_signal(bar, 1, device_id=(there, self.e), device_id_type=MESH)
            pl.semaphore_signal(bar, 1, device_id=(there, self.sibling), device_id_type=MESH)

        lax.fori_loop(1, self.ne, exp_peer, None)
        lax.fori_loop(1, self.nb, blk_peer, None)
        pl.semaphore_wait(bar, self.ne - 1 + 2 * (self.nb - 1))

    def is_me(self, there):
        return there[0] * self.ne + there[1] == self.b * self.ne + self.e


def remote(src, dst, send_sem, recv_sem, there):
    return pltpu.make_async_remote_copy(
        src, dst, send_sem, recv_sem, device_id=there, device_id_type=MESH
    )


def push(me, src, dst, send_sem, recv_sem, there):
    mine = me.is_me(there)

    @pl.when(mine)
    def _():
        pltpu.make_async_copy(src, dst, recv_sem).start()

    @pl.when(jnp.logical_not(mine))
    def _():
        remote(src, dst, send_sem, recv_sem, there).start()


def push_done(me, src, dst, send_sem, recv_sem, there):
    @pl.when(jnp.logical_not(me.is_me(there)))
    def _():
        remote(src, dst, send_sem, recv_sem, there).wait_send()


def landed(dst, recv_sem):
    pltpu.make_async_copy(dst, dst, recv_sem).wait()


def exchange_start(me, src, dst, send_sem, recv_sem, size):
    def one(k, _):
        there = lax.rem(me.e + k, me.ne)
        remote(
            src.at[split_rows(there * size, size)],
            dst.at[split_rows(me.e * size, size)],
            send_sem.at[k],
            recv_sem.at[k],
            (me.b, there),
        ).start()

    own = split_rows(me.e * size, size)
    pltpu.make_async_copy(src.at[own], dst.at[own], recv_sem.at[0]).start()
    lax.fori_loop(1, me.ne, one, None)


def exchange_wait(me, src, dst, send_sem, recv_sem, size):
    own = split_rows(me.e * size, size)
    landed(dst.at[own], recv_sem.at[0])

    def one(k, _):
        source = lax.rem(me.e + me.ne - k, me.ne)
        landed(dst.at[split_rows(source * size, size)], recv_sem.at[k])

    lax.fori_loop(1, me.ne, one, None)


def exchange_sent(me, src, dst, send_sem, recv_sem, size):
    def one(k, _):
        there = lax.rem(me.e + k, me.ne)
        remote(
            src.at[split_rows(there * size, size)],
            dst.at[split_rows(me.e * size, size)],
            send_sem.at[k],
            recv_sem.at[k],
            (me.b, there),
        ).wait_send()

    lax.fori_loop(1, me.ne, one, None)


def token_slots(me, idx):
    rows = idx.shape[1]
    hot = (iota((128, rows), 0) == idx).astype(F32)
    earlier = (iota((rows, rows), 0) < iota((rows, rows), 1)).astype(F32).astype(BF16)
    ahead = dot(hot.astype(BF16), earlier)
    slot = jnp.sum(ahead * hot, axis=0, keepdims=True).astype(jnp.int32) + idx * me.cap
    return slot, jnp.sum(hot, axis=1, keepdims=True)[0 : me.experts]


def slots_by_token(me, slot):
    shape = (me.experts * me.cap, slot.shape[1])
    return (iota(shape, 0) == slot).astype(F32).astype(BF16)


def head_masks():
    lane = iota((1, PAIR), 1)
    first = (lane < HEAD_DIM).astype(F32).astype(BF16)
    second = (lane >= HEAD_DIM).astype(F32).astype(BF16)
    return first, second


def gelu_parts(u):
    root = 0.7978845608028654
    cubic = 0.044715
    square = u * u
    t = jnp.tanh(root * u * (1.0 + cubic * square))
    value = 0.5 * u * (1.0 + t)
    slope = 0.5 * (1.0 + t) + (0.5 * root) * u * (1.0 - t * t) * (1.0 + 3.0 * cubic * square)
    return value, slope


class Refs:
    def __init__(self, names, refs):
        self.__dict__.update(zip(names, refs, strict=True))


class ExpertSums:
    def __init__(self, me, r):
        self.me, self.r = me, r
        self.hi, self.lo = lax.div(me.b, 2), lax.rem(me.b, 2)
        self.other = 1 - self.lo
        self.count = me.nb // 2
        self.size = me.ff // me.nb

    def turn(self, step):
        return lax.rem(self.hi + step, self.count)

    def span(self, hi, lo):
        return pl.ds(pl.multiple_of((2 * hi + lo) * self.size, 128), self.size)

    def in_first(self, hi):
        r = self.r
        there = (2 * self.hi + self.other, self.me.e)
        return remote(
            r.win.at[:, self.span(hi, self.other)], r.in1.at[hi], r.in1s.at[hi], r.in1r.at[hi], there
        )

    def in_second(self, step):
        r, hi = self.r, self.turn(step)
        return remote(
            r.win.at[:, self.span(hi, self.lo)],
            r.in2.at[step - 1],
            r.in2s.at[step - 1],
            r.in2r.at[step - 1],
            (2 * hi + self.lo, self.me.e),
        )

    def out_first(self, step, lo):
        r, hi = self.r, self.turn(step)
        return remote(
            r.wout.at[self.span(hi, lo)],
            r.out1.at[step - 1, lo],
            r.out1s.at[step - 1, lo],
            r.out1r.at[step - 1, lo],
            (2 * hi + self.lo, self.me.e),
        )

    def out_second(self):
        r = self.r
        return remote(
            r.wout.at[self.span(self.hi, self.other)],
            r.out2,
            r.out2s,
            r.out2r,
            (2 * self.hi + self.other, self.me.e),
        )

    def after_part(self, n):
        step = lax.div(n, 2) + 1
        lo = lax.rem(self.other + n, 2)

        @pl.when(lax.rem(n, 2) == 0)
        def _():
            self.in_first(self.turn(step)).start()

        @pl.when(step < self.count)
        def _():
            self.out_first(step, lo).start()

    def second_add(self):
        r = self.r
        for step in range(1, self.count):
            hi = self.turn(step)
            landed(r.in1.at[hi], r.in1r.at[hi])
            here = self.span(hi, self.lo)

            def in_rows(n, _, hi=hi, here=here):
                rows = split_rows(n * ROWS, ROWS)
                r.win[rows, here] = (
                    r.win[rows, here].astype(F32) + r.in1[hi, rows, :].astype(F32)
                ).astype(BF16)

            lax.fori_loop(0, self.me.width // ROWS, in_rows, None)
        for step in range(1, self.count):
            landed(r.out1.at[step - 1, self.other], r.out1r.at[step - 1, self.other])
        base = (2 * self.hi + self.other) * self.size

        def out_rows(n, _):
            here, rows = split_rows(base + n * ROWS, ROWS), split_rows(n * ROWS, ROWS)
            total = r.wout[here, :].astype(F32)
            for step in range(1, self.count):
                total += r.out1[step - 1, self.other, rows, :].astype(F32)
            r.wout[here, :] = total.astype(BF16)

        lax.fori_loop(0, self.size // ROWS, out_rows, None)

    def second_send(self):
        for step in range(1, self.count):
            self.in_second(step).start()
        self.out_second().start()

    def total_in(self, into):
        r = self.r
        landed(r.in1.at[self.hi], r.in1r.at[self.hi])
        for step in range(1, self.count):
            landed(r.in2.at[step - 1], r.in2r.at[step - 1])

        def in_rows(n, _):
            rows = split_rows(n * ROWS, ROWS)
            total = r.win[rows, self.span(self.hi, self.lo)].astype(F32)
            total += r.in1[self.hi, rows, :].astype(F32)
            for step in range(1, self.count):
                total += r.in2[step - 1, rows, :].astype(F32)
            into[rows, 0 : self.size] = total

        lax.fori_loop(0, self.me.width // ROWS, in_rows, None)

    def total_out(self, into):
        r = self.r
        for step in range(1, self.count):
            landed(r.out1.at[step - 1, self.lo], r.out1r.at[step - 1, self.lo])
        landed(r.out2, r.out2r)
        base = (2 * self.hi + self.lo) * self.size

        def out_rows(n, _):
            rows = split_rows(n * ROWS, ROWS)
            total = r.wout[split_rows(base + n * ROWS, ROWS), :].astype(F32)
            for step in range(1, self.count):
                total += r.out1[step - 1, self.lo, rows, :].astype(F32)
            into[rows, :] = total + r.out2[rows, :].astype(F32)

        lax.fori_loop(0, self.size // ROWS, out_rows, None)

    def sent(self):
        for step in range(1, self.count + 1):
            self.in_first(self.turn(step)).wait_send()
            if step < self.count:
                self.in_second(step).wait_send()
                for lo in range(2):
                    self.out_first(step, lo).wait_send()
        self.out_second().wait_send()


class SharedSum:
    def __init__(self, me, r, p, blk_first):
        self.me, self.r, self.p = me, r, p
        z = lax.div(me.e, 2)
        nz = me.ne // 2
        blk = (me.b, me.nb, lambda t: (t, me.e))
        along_z = (z, nz, lambda t: (me.b, 2 * t + me.c))
        self.first, self.second = (blk, along_z) if blk_first else (along_z, blk)
        self.outer = me.width // self.first[1]
        self.inner = self.outer // self.second[1]

    def outer_rows(self, t):
        return split_rows(t * self.outer, self.outer)

    def inner_rows(self, t, s):
        return split_rows(t * self.outer + s * self.inner, self.inner)

    def view(self, rows, core):
        me, r, p = self.me, self.r, self.p
        if p < 3:
            return r.shared.at[
                pl.ds(0, 3), rows, pl.ds(pl.multiple_of(core * me.half_width + p * PAIR, PAIR), PAIR)
            ]
        return r.shared.at[
            3, rows, pl.ds(pl.multiple_of(core * me.half_width, PAIR), me.half_width)
        ]

    def peer(self, axis, k):
        return lax.rem(axis[0] + k, axis[1])

    def source(self, axis, k):
        return lax.rem(axis[0] + axis[1] - k, axis[1])

    def move1(self, k):
        r, p = self.r, self.p
        t = self.peer(self.first, k)
        return remote(
            r.part.at[p, self.outer_rows(t)],
            r.got1.at[p, k, pl.ds(0, self.outer)],
            r.s1.at[p, k],
            r.r1.at[p, k],
            self.first[2](t),
        )

    def move2(self, k):
        r, p = self.r, self.p
        t = self.peer(self.second, k)
        return remote(
            r.got1.at[p, 0, split_rows(t * self.inner, self.inner)],
            r.got2.at[p, k],
            r.s2.at[p, k],
            r.r2.at[p, k],
            self.second[2](t),
        )

    def move3(self, k):
        r, p = self.r, self.p
        here = self.view(self.inner_rows(self.first[0], self.second[0]), self.me.c)
        return remote(
            here, here, r.s3.at[p, k], r.r3.at[p, k], self.second[2](self.peer(self.second, k))
        )

    def move4(self, k):
        r, p = self.r, self.p
        here = self.view(self.outer_rows(self.first[0]), self.me.c)
        return remote(
            here, here, r.s4.at[p, k], r.r4.at[p, k], self.first[2](self.peer(self.first, k))
        )

    def move5(self):
        r, p = self.r, self.p
        here = self.view(pl.ds(0, self.me.width), self.me.c)
        return remote(here, here, r.s5.at[p], r.r5.at[p], (self.me.b, self.me.sibling))

    def stage1(self):
        for k in range(1, self.first[1]):
            self.move1(k).start()

    def stage2(self):
        r, p = self.r, self.p
        total = r.part[p, self.outer_rows(self.first[0])].astype(F32)
        for k in range(1, self.first[1]):
            here = r.got1.at[p, k, pl.ds(0, self.outer)]
            landed(here, r.r1.at[p, k])
            total += here[...].astype(F32)
        r.got1[p, 0, 0 : self.outer, :] = total.astype(BF16)
        for k in range(1, self.second[1]):
            self.move2(k).start()

    def stage3(self):
        r, p = self.r, self.p
        total = r.got1[p, 0, split_rows(self.second[0] * self.inner, self.inner)].astype(F32)
        for k in range(1, self.second[1]):
            landed(r.got2.at[p, k], r.r2.at[p, k])
            total += r.got2[p, k].astype(F32)
        total = total.astype(BF16)
        here = self.view(self.inner_rows(self.first[0], self.second[0]), self.me.c)
        if p < 3:
            for j in range(3):
                here[j] = total[:, j * PAIR : (j + 1) * PAIR]
        else:
            here[...] = total
        for k in range(1, self.second[1]):
            self.move3(k).start()

    def stage4(self):
        for k in range(1, self.second[1]):
            rows = self.inner_rows(self.first[0], self.source(self.second, k))
            landed(self.view(rows, self.me.c), self.r.r3.at[self.p, k])
        for k in range(1, self.first[1]):
            self.move4(k).start()

    def stage5(self):
        for k in range(1, self.first[1]):
            rows = self.outer_rows(self.source(self.first, k))
            landed(self.view(rows, self.me.c), self.r.r4.at[self.p, k])
        self.move5().start()

    def end(self):
        landed(self.view(pl.ds(0, self.me.width), 1 - self.me.c), self.r.r5.at[self.p])
        for k in range(1, self.first[1]):
            self.move1(k).wait_send()
            self.move4(k).wait_send()
        for k in range(1, self.second[1]):
            self.move2(k).wait_send()
            self.move3(k).wait_send()
        self.move5().wait_send()


class AllSum:
    def __init__(self, me, own, by_exp, by_blk, sems):
        self.me, self.own, self.by_exp, self.by_blk = me, own, by_exp, by_blk
        self.es, self.er, self.bs, self.br = sems

    def exp_move(self, k):
        me = self.me
        there = (me.b, lax.rem(me.e + k, me.ne))
        return remote(self.own, self.by_exp.at[me.e], self.es.at[k], self.er.at[k], there)

    def blk_move(self, k):
        me = self.me
        here = self.by_blk.at[me.b]
        there = (lax.rem(me.b + k, me.nb), me.e)
        return remote(here, here, self.bs.at[k], self.br.at[k], there)

    def start(self):
        lax.fori_loop(1, self.me.ne, lambda k, _: self.exp_move(k).start(), None)
        self.by_exp[self.me.e] = self.own[...]

    def middle(self):
        me = self.me

        def arrived(k, _):
            landed(self.by_exp.at[lax.rem(me.e + me.ne - k, me.ne)], self.er.at[k])

        lax.fori_loop(1, me.ne, arrived, None)
        self.by_blk[me.b] = jnp.sum(self.by_exp[...], axis=0)
        for k in range(1, me.nb):
            self.blk_move(k).start()

    def total(self):
        me = self.me
        for k in range(1, me.nb):
            landed(self.by_blk.at[lax.rem(me.b + me.nb - k, me.nb)], self.br.at[k])
        return jnp.sum(self.by_blk[...], axis=0)

    def sent(self):
        lax.fori_loop(1, self.me.ne, lambda k, _: self.exp_move(k).wait_send(), None)
        for k in range(1, self.me.nb):
            self.blk_move(k).wait_send()


def layer_kernel(cfg, names, *refs):
    me = Place(cfg)
    r = Refs(names, refs)
    half = me.span // 2
    pairs = me.half_width // PAIR
    blocks = me.length // QUERY_ROWS
    slots = me.experts * me.cap
    roomy = slots * me.width <= 1 << 19
    model_tile = me.width if roomy else FF_COLS
    r.ysend, r.yback = r.g, r.du
    r.swap, r.da_in = r.took.at[pl.ds(0, me.rows)], r.back.at[pl.ds(0, me.rows)]
    r.xin, r.o_send, r.lse_cols, r.dh_send = r.mail, r.g, r.dk_sum, r.disp
    gain1, bias1, gain2, bias2 = (
        v[...].reshape(1, me.width) for v in (r.gain1, r.bias1, r.gain2, r.bias2)
    )
    loads = {}
    for name in ("x", "og", "wo", "win", "wout"):
        loads[name] = pltpu.make_async_copy(
            getattr(r, name + "_hbm"), getattr(r, name), r.lsem.at[len(loads)]
        )
    for p in range(pairs):
        for j, matrix in enumerate((r.wq_hbm, r.wk_hbm, r.wv_hbm)):
            src = matrix.at[:, pl.ds(pl.multiple_of(me.c * me.half_width + p * PAIR, PAIR), PAIR)]
            loads["w", p, j] = pltpu.make_async_copy(
                src, r.w.at[p, :, pl.ds(j * PAIR, PAIR)], r.lsem.at[len(loads)]
            )
    for load in loads.values():
        load.start()
    me.greet()

    def row_moves():
        for s in range(me.seqs):
            for h in range(2):
                yield (
                    r.x_hbm.at[pl.ds(s * me.span + h * half, half)],
                    r.xin.at[split_rows(me.b * half, half)],
                    r.xs.at[2 * s + h],
                    r.xr.at[me.b],
                    (me.c * me.seqs + s, me.pair + h),
                )

    for move in row_moves():
        push(me, *move)

    slot, counts = token_slots(me, r.idx[...])
    r.cnt[...] = jnp.broadcast_to(counts, r.cnt.shape)
    count_sum = AllSum(me, r.cnt, r.cnt_exp, r.cnt_blk, (r.ces, r.cer, r.cbs, r.cbr))
    count_sum.start()
    r.idx_col[...] = jnp.transpose(
        jnp.broadcast_to(r.idx[...].astype(F32), (128, me.rows))
    )
    loads["og"].wait()
    r.dh_send[...] = dot(slots_by_token(me, slot), r.og[...]).astype(BF16)
    exchange_start(me, r.dh_send, r.dh, r.ds, r.dr, me.cap)

    def forward_move(j):
        rows = split_rows(j * me.span + me.c * half, half)
        return remote(r.a.at[rows], r.a.at[rows], r.fws.at[j], r.fwr.at[j], (me.b, me.sibling))

    for j in range(me.nb):
        landed(r.xin.at[pl.ds(j * half, half)], r.xr.at[j])
        hat, _ = normalize(r.xin[pl.ds(j * half, half), :].astype(F32))
        r.a[split_rows(j * me.span + me.c * half, half), :] = (hat * gain1 + bias1).astype(BF16)
        forward_move(j).start()

    for p in range(pairs):
        for j in range(3):
            loads["w", p, j].wait()
    first, second = head_masks()
    spans = QUERY_ROWS // me.span
    lane = iota((1, PAIR), 1)
    visible = iota((QUERY_ROWS, QUERY_ROWS), 1) <= iota((QUERY_ROWS, QUERY_ROWS), 0)
    home = me.pair + lax.div(me.b, me.seqs)
    columns = pl.ds(pl.multiple_of(me.c * me.half_width, PAIR), me.half_width)

    def o_move(j):
        return (
            r.o_send.at[
                pl.ds(j * me.span % me.rows, me.span),
                pl.ds(j * me.span // me.rows * me.half_width, me.half_width),
            ],
            r.o.at[split_rows(lax.rem(me.b, me.seqs) * me.span, me.span), columns],
            r.os.at[j],
            r.osr.at[2 * lax.rem(me.b, me.seqs) + me.c],
            (j, home),
        )

    for i in range(blocks):
        for j in range(i * spans, (i + 1) * spans):
            theirs = split_rows(j * me.span + (1 - me.c) * half, half)
            landed(r.a.at[theirs], r.fwr.at[j])
        here = pl.ds(i * QUERY_ROWS, QUERY_ROWS)

        def pair_of_heads(p, _, i=i, here=here):
            lanes = split_rows(p * PAIR, PAIR)
            qkv = dot(r.a[here, :], r.w[p]).astype(BF16)
            queries = qkv[:, 0:PAIR] * jnp.asarray(SCALE, BF16)
            r.q[here, lanes] = queries
            r.k[here, lanes] = qkv[:, PAIR : 2 * PAIR]
            r.v[here, lanes] = qkv[:, 2 * PAIR : 3 * PAIR]
            parts = [pl.ds(i * QUERY_ROWS, QUERY_ROWS)]
            if i:
                parts.append(pl.ds(0, i * QUERY_ROWS))
            done = []
            for h, mask in enumerate((first, second)):
                masked = queries * mask
                scores = [dot(masked, r.k[part, lanes], NT) for part in parts]
                scores[0] = jnp.where(visible, scores[0], -1e30)
                peak = functools.reduce(
                    jnp.maximum, [jnp.max(s, axis=1, keepdims=True) for s in scores]
                )
                powers = [jnp.exp(s - peak) for s in scores]
                total = sum(jnp.sum(s, axis=1, keepdims=True) for s in powers)
                mixed = sum(
                    dot(s.astype(BF16), r.v[part, lanes]) for s, part in zip(powers, parts)
                )
                done.append(mixed / total)
                r.lse_cols[here, :] = jnp.where(
                    lane == 2 * p + h, peak + jnp.log(total), r.lse_cols[here, :]
                )
            base = i * QUERY_ROWS // me.rows * me.half_width
            r.o_send[
                pl.ds(i * QUERY_ROWS % me.rows, QUERY_ROWS),
                pl.ds(pl.multiple_of(base + p * PAIR, PAIR), PAIR),
            ] = jnp.where(lane < HEAD_DIM, done[0], done[1]).astype(BF16)

        lax.fori_loop(0, pairs, pair_of_heads, None)
        for j in range(i * spans, (i + 1) * spans):
            push(me, *o_move(j))
        if i == 0:
            count_sum.middle()
    r.lse[...] = jnp.transpose(r.lse_cols[...])[0:8, :]
    for j in range(me.nb):
        forward_move(j).wait_send()
        push_done(me, *o_move(j))
    for move in row_moves():
        push_done(me, *move)
    for name in ("x", "wo"):
        loads[name].wait()
    exchange_wait(me, r.dh_send, r.dh, r.ds, r.dr, me.cap)
    exchange_sent(me, r.dh_send, r.dh, r.ds, r.dr, me.cap)

    expert_lane = iota((ROWS, me.experts), 1)
    r.sums[...] = jnp.zeros_like(r.sums)
    r.mass[...] = jnp.zeros_like(r.mass)
    for s in range(me.seqs):
        for h in range(2):
            landed(
                r.o.at[pl.ds(s * me.span, me.span), pl.ds(h * me.half_width, me.half_width)],
                r.osr.at[2 * s + h],
            )

    def token_rows(n, _):
        here = split_rows(n * ROWS, ROWS)
        hidden = r.x[here, :].astype(F32) + dot(r.o[here, :], r.wo[...])
        r.h1[here, :] = hidden
        hat, _ = normalize(hidden)
        normed = (hat * gain2 + bias2).astype(BF16)
        r.mail[here, :] = normed
        logits = dot(normed, r.router[...], NT)
        hot = r.idx_col[here, 0 : me.experts].astype(jnp.int32) == expert_lane
        value = jax.nn.sigmoid(jnp.sum(jnp.where(hot, logits, 0.0), axis=1, keepdims=True))
        r.gate[here, :] = value
        r.mass[...] += jnp.sum(jnp.where(hot, value, 0.0), axis=0, keepdims=True)

    lax.fori_loop(0, me.rows // ROWS, token_rows, None)
    takes = slots_by_token(me, slot)
    r.disp[...] = dot(takes, r.mail[...]).astype(BF16)
    exchange_start(me, r.disp, r.took, r.ns, r.nr, me.cap)
    loads["win"].wait()
    loads["wout"].wait()
    exchange_wait(me, r.disp, r.took, r.ns, r.nr, me.cap)
    exchange_sent(me, r.disp, r.took, r.ns, r.nr, me.cap)

    lanes = iota((slots, me.experts), 1)
    logits = jnp.sum(
        jnp.where(lanes == me.e, dot(r.took[...], r.router[...], NT), 0.0), axis=1, keepdims=True
    )
    value = jax.nn.sigmoid(logits)
    r.disp[...] = (value * r.dh[...].astype(F32)).astype(BF16)
    r.yf[0:slots, :] = jnp.zeros((slots, me.width), F32)
    r.made[...] = jnp.zeros_like(r.made)
    sums = ExpertSums(me, r)
    slot_rows = slots if roomy else slots // 4

    def expert_part(n, _):
        hi, lo = sums.turn(lax.div(n, 2) + 1), lax.rem(sums.other + n, 2)
        base = (2 * hi + lo) * sums.size

        def hidden_columns(f, _):
            here = pl.ds(pl.multiple_of(base + f * sums.tile, 128), sums.tile)
            there = pl.ds(pl.multiple_of(f * sums.tile, 128), sums.tile)

            def hidden_rows(n, _):
                rows = split_rows(n * slot_rows, slot_rows)
                act, slope = gelu_parts(dot(r.took[rows, :], r.win[:, here]))
                r.g[rows, there] = act.astype(BF16)
                r.du[rows, there] = (dot(r.disp[rows, :], r.wout[here, :], NT) * slope).astype(BF16)

            lax.fori_loop(0, slots // slot_rows, hidden_rows, None)

        lax.fori_loop(0, sums.size // sums.tile, hidden_columns, None)
        part = sums.span(hi, lo)


        def model_columns(f, _):
            here = split_rows(f * model_tile, model_tile)
            r.yf[0:slots, here] += dot(r.g[:, 0 : sums.size], r.wout[part, here])
            r.made[0:slots, here] += dot(r.du[:, 0 : sums.size], r.win[here, part], NT)

        lax.fori_loop(0, me.width // model_tile, model_columns, None)

        def weight_columns(f, _):
            here = pl.ds(pl.multiple_of(base + f * sums.tile, 128), sums.tile)
            there = pl.ds(pl.multiple_of(f * sums.tile, 128), sums.tile)
            r.win[:, here] = dot(r.took[...], r.du[:, there], TN).astype(BF16)
            r.wout[here, :] = dot(r.g[:, there], r.disp[...], TN).astype(BF16)

        lax.fori_loop(0, sums.size // sums.tile, weight_columns, None)
        sums.after_part(n)

    sums.tile = sums.size
    lax.fori_loop(0, me.nb, expert_part, None)

    weights = (count_sum.total() - me.mean_load) / me.mean_load
    weight = jnp.sum(jnp.where(iota(weights.shape, 0) == me.e, weights, 0.0), axis=0, keepdims=True)
    weight = weight[:, 0:1]
    r.ysend[...] = r.yf[0:slots, :].astype(BF16)
    dgate = (
        jnp.sum(r.dh[...].astype(F32) * r.ysend[...].astype(F32), axis=1, keepdims=True)
        + weight / me.tokens
    )
    dlogits = jnp.where(lanes == me.e, dgate * value * (1.0 - value), 0.0).astype(BF16)
    r.disp[...] = (r.made[0:slots, :] + dot(dlogits, r.router[...])).astype(BF16)
    exchange_start(me, r.disp, r.back, r.rs, r.rr, me.cap)
    r.sums[2 : 2 + me.experts, :] = dot(dlogits, r.took[...], TN)
    r.sums[2 + me.experts : 3 + me.experts, 0 : me.experts] = r.mass[...]
    sums.second_add()
    exchange_wait(me, r.disp, r.back, r.rs, r.rr, me.cap)

    r.made[0 : me.rows, :] = dot(takes, r.back[...], TN)

    def norm_rows(n, _):
        here = split_rows(n * ROWS, ROWS)
        grad = r.made[here, :]
        hat, inverse = normalize(r.h1[here, :])
        r.sums[0:1, :] += jnp.sum(grad * hat, axis=0, keepdims=True)
        r.sums[1:2, :] += jnp.sum(grad, axis=0, keepdims=True)
        total = r.og[here, :].astype(F32) + norm_back(hat, inverse, gain2, grad)
        r.dh1[here, :] = total
        r.mail[here, :] = dot(total.astype(BF16), r.wo[...], NT).astype(BF16)

    def do_moves(s):
        for h in range(2):
            yield (
                r.mail.at[pl.ds(s * me.span, me.span), pl.ds(h * me.half_width, me.half_width)],
                r.do.at[split_rows(me.b * me.span, me.span)],
                r.dos.at[2 * s + h],
                r.dor.at[me.b],
                (me.c * me.seqs + s, me.pair + h),
            )

    steps = me.span // ROWS
    for s in range(me.seqs):
        lax.fori_loop(s * steps, (s + 1) * steps, norm_rows, None)
        for move in do_moves(s):
            push(me, *move)
    sums.second_send()
    early = AllSum(me, r.sums, r.sum_exp, r.sum_blk, (r.es, r.er, r.bs, r.br))
    early.start()
    exchange_start(me, r.ysend, r.yback, r.ys, r.yr, me.cap)

    def output_columns(core):
        cols = pl.ds(pl.multiple_of(core * me.half_width, PAIR), me.half_width)
        return dot(r.o[...], r.dh1[:, cols].astype(BF16), TN)

    r.part[0] = output_columns(1 - me.c).astype(BF16)
    o_swap = remote(r.part.at[0], r.ogot, r.ows, r.owr, (me.b, me.sibling))
    o_swap.start()
    own_columns = output_columns(me.c)
    o_swap.wait()
    r.part[3] = (own_columns + r.ogot[...].astype(F32)).astype(BF16)
    pieces = [SharedSum(me, r, p, p in BLK_FIRST) for p in range(4)] if me.sum_here else []

    def advance(point):
        for p, stage in PLAN.get(point, ()) if pieces else ():
            getattr(pieces[p], f"stage{stage}")()

    advance("start")

    r.made[...] = jnp.zeros_like(r.made)
    for j in range(me.nb):
        landed(r.do.at[pl.ds(j * me.span, me.span)], r.dor.at[j])
    visible = iota((QUERY_ROWS, QUERY_ROWS), 0) <= iota((QUERY_ROWS, QUERY_ROWS), 1)

    def pair_back(n, _):
        lanes = split_rows(n * PAIR, PAIR)
        r.dk_sum[...] = jnp.zeros_like(r.dk_sum)
        r.dv_sum[...] = jnp.zeros_like(r.dv_sum)
        for i in range(blocks):
            here = pl.ds(i * QUERY_ROWS, QUERY_ROWS)
            queries, grads = r.q[here, lanes], r.do[here, lanes]
            parts = [here]
            if i:
                parts.append(pl.ds(0, i * QUERY_ROWS))
            dq_block = jnp.zeros((QUERY_ROWS, PAIR), F32)
            for h, mask in enumerate((first, second)):
                qm, gm = queries * mask, grads * mask
                log_sums = r.lse[pl.ds(2 * n + h, 1), here]
                scores = [dot(r.k[part, lanes], qm, NT) for part in parts]
                powers = [jnp.exp(s - log_sums) for s in scores]
                powers[0] = jnp.where(visible, powers[0], 0.0)
                weighted = [
                    s * dot(r.v[part, lanes], gm, NT) for s, part in zip(powers, parts)
                ]
                delta = sum(jnp.sum(t, axis=0, keepdims=True) for t in weighted)
                for s, t, part in zip(powers, weighted, parts):
                    ds = (t - s * delta).astype(BF16)
                    r.dv_sum[part, :] += dot(s.astype(BF16), gm)
                    r.dk_sum[part, :] += dot(ds, qm)
                    dq_block += dot(ds, r.k[part, lanes] * mask, TN)
            r.dqkv[here, 0:PAIR] = (dq_block * SCALE).astype(BF16)
        r.dqkv[:, PAIR : 2 * PAIR] = r.dk_sum[...].astype(BF16)
        r.dqkv[:, 2 * PAIR : 3 * PAIR] = r.dv_sum[...].astype(BF16)
        r.part[n] = dot(r.a[...], r.dqkv[...], TN).astype(BF16)

        def normed_columns(f, _):
            cols = split_rows(f * model_tile, model_tile)
            r.made[:, cols] += dot(r.dqkv[...], r.w[n, cols, :], NT)

        lax.fori_loop(0, me.width // model_tile, normed_columns, None)
        for done in range(pairs):

            @pl.when(n == done)
            def _(done=done):
                advance(done)

    lax.fori_loop(0, pairs, pair_back, None)
    early.middle()

    for s in range(me.seqs):
        for move in do_moves(s):
            push_done(me, *move)
    for j in range(me.nb):
        theirs = split_rows(j * me.span + (1 - me.c) * half, half)
        r.mail[pl.ds(j * half, half), :] = r.made[theirs, :].astype(BF16)
    swap = remote(r.mail, r.swap, r.ss, r.sr, (me.b, me.sibling))
    swap.start()
    exchange_wait(me, r.ysend, r.yback, r.ys, r.yr, me.cap)
    r.yf[0 : me.rows, :] = dot(takes, r.yback[...], TN)

    def out_rows(n, _):
        here = split_rows(n * ROWS, ROWS)
        r.out[here, :] = (r.h1[here, :] + r.gate[here, :] * r.yf[here, :]).astype(BF16)

    lax.fori_loop(0, me.rows // ROWS, out_rows, None)
    swap.wait()
    def da_move(j):
        return (
            r.mail.at[pl.ds(j * half, half)],
            r.da_in.at[split_rows(lax.rem(me.b, me.seqs) * me.span + me.c * half, half)],
            r.fs.at[j],
            r.fr.at[2 * lax.rem(me.b, me.seqs) + me.c],
            (j, home),
        )

    for j in range(me.nb):
        mine = r.made[split_rows(j * me.span + me.c * half, half), :]
        rows = pl.ds(j * half, half)
        r.mail[rows, :] = (mine + r.swap[rows, :].astype(F32)).astype(BF16)
        push(me, *da_move(j))
    advance("rows sent")
    for s in range(me.seqs):
        for h in range(2):
            landed(r.da_in.at[pl.ds(s * me.span + h * half, half)], r.fr.at[2 * s + h])

    r.late[...] = jnp.zeros_like(r.late)
    tiles = me.width // FF_COLS

    def first_norm_rows(n, _):
        here = split_rows(n * ROWS, ROWS)
        grad = r.da_in[here, :].astype(F32)
        hat, inverse = normalize(r.x[here, :].astype(F32))
        gain_part = jnp.sum(grad * hat, axis=0, keepdims=True)
        bias_part = jnp.sum(grad, axis=0, keepdims=True)
        for j in range(tiles):
            cols = slice(j * FF_COLS, (j + 1) * FF_COLS)
            r.late[j : j + 1, :] += gain_part[:, cols]
            r.late[tiles + j : tiles + j + 1, :] += bias_part[:, cols]
        r.dx[here, :] = (r.dh1[here, :] + norm_back(hat, inverse, gain1, grad)).astype(BF16)

    lax.fori_loop(0, me.rows // ROWS, first_norm_rows, None)
    late = AllSum(me, r.late, r.late_exp, r.late_blk, (r.les, r.ler, r.lbs, r.lbr))
    late.start()
    advance("rows done")
    late.middle()
    advance("late")

    size = sums.size
    sums.total_in(r.made)
    store_in = pltpu.make_async_copy(
        r.made.at[pl.ds(0, me.width), pl.ds(0, size)], r.dwin, r.fsem.at[0]
    )
    store_in.start()
    sums.total_out(r.yf)
    store_out = pltpu.make_async_copy(r.yf.at[pl.ds(0, size)], r.dwout, r.fsem.at[1])
    store_out.start()
    advance("last")
    early_total = early.total()
    late_total = late.total()
    r.small[0 : r.sums.shape[0], :] = early_total
    for j in range(tiles):
        cols = slice(j * FF_COLS, (j + 1) * FF_COLS)
        r.small[me.experts + 4 : me.experts + 5, cols] = late_total[j : j + 1, :]
        r.small[me.experts + 5 : me.experts + 6, cols] = late_total[tiles + j : tiles + j + 1, :]
    own_weight = jnp.transpose(jnp.broadcast_to(weights, (weights.shape[0], 128)))[0:1, :]
    mass = early_total[2 + me.experts : 3 + me.experts, 0 : me.experts]
    r.small[me.experts + 3 : me.experts + 4, 0:1] = (
        jnp.sum(own_weight[:, 0 : me.experts] * mass, axis=1, keepdims=True) / me.tokens
    )
    for each in (count_sum, early, late):
        each.sent()
    exchange_sent(me, r.disp, r.back, r.rs, r.rr, me.cap)
    exchange_sent(me, r.ysend, r.yback, r.ys, r.yr, me.cap)
    for j in range(me.nb):
        push_done(me, *da_move(j))
    sums.sent()
    stores = [store_in, store_out]
    for piece in pieces:
        piece.end()
    if pieces:
        targets = [(r.shared.at[j], out) for j, out in enumerate((r.gq, r.gk, r.gv, r.go))]
    else:
        targets = [(r.part, r.own_part)]
    for n, (src, dst) in enumerate(targets):
        store = pltpu.make_async_copy(src, dst, r.fsem.at[2 + n])
        store.start()
        stores.append(store)
    for store in stores:
        store.wait()


def in_vmem(count):
    return [pl.BlockSpec(memory_space=pltpu.VMEM)] * count


def anywhere(count):
    return [pl.BlockSpec(memory_space=pl.ANY)] * count


def shards(
    tokens,
    output_grad,
    expert_index,
    query_weight,
    key_weight,
    value_weight,
    output_weight,
    router_weight,
    expert_in,
    expert_out,
    norm1_gain,
    norm1_bias,
    norm2_gain,
    norm2_bias,
):
    seqs, span, width = tokens.shape
    rows = seqs * span
    nb, ne = lax.axis_size("blk"), lax.axis_size("exp")
    length = span * nb
    experts = router_weight.shape[1]
    ff = expert_in.shape[2]
    cap = -(-max(2, rows * 5 // (4 * experts)) // 16) * 16
    slots = experts * cap
    token_total = rows * nb * ne
    half_width = width // 2
    cfg = dict(
        seqs=seqs, span=span, width=width, rows=rows, nb=nb, ne=ne, length=length,
        experts=experts, ff=ff, cap=cap, half_width=half_width, tokens=token_total,
        mean_load=token_total / experts,
    )
    dma = pltpu.SemaphoreType.DMA
    vmem = pltpu.VMEM
    hi = nb // 2
    size = ff // nb
    sum_rows = -(-(3 + experts) // 8) * 8
    cfg["sum_here"] = width % (8 * nb * ne) == 0
    outer = width // min(nb, ne // 2)
    inner = width // (nb * ne // 2)
    inputs = (
        ("idx", expert_index.reshape(1, rows), True),
        ("router", router_weight.T, True),
        ("gain1", norm1_gain, True),
        ("bias1", norm1_bias, True),
        ("gain2", norm2_gain, True),
        ("bias2", norm2_bias, True),
        ("x_hbm", tokens.reshape(rows, width), False),
        ("og_hbm", output_grad.reshape(rows, width), False),
        ("wo_hbm", output_weight, False),
        ("win_hbm", expert_in.reshape(width, ff), False),
        ("wout_hbm", expert_out.reshape(ff, width), False),
        ("wq_hbm", query_weight, False),
        ("wk_hbm", key_weight, False),
        ("wv_hbm", value_weight, False),
    )
    small_rows = -(-(6 + experts) // 8) * 8
    outputs = [
        ("out", (rows, width), BF16, True),
        ("dx", (rows, width), BF16, True),
        ("small", (small_rows, width), F32, True),
        ("dwin", (width, size), F32, False),
        ("dwout", (size, width), F32, False),
    ]
    if cfg["sum_here"]:
        outputs += [(n, (width, width), BF16, False) for n in ("gq", "gk", "gv", "go")]
    else:
        outputs.append(("own_part", (4, width, half_width), BF16, False))
    scratch = dict(
        win=vmem((width, ff), BF16),
        wout=vmem((ff, width), BF16),
        x=vmem((rows, width), BF16),
        og=vmem((rows, width), BF16),
        o=vmem((rows, width), BF16),
        wo=vmem((width, width), BF16),
        dh=vmem((slots, width), BF16),
        idx_col=vmem((rows, 128), F32),
        cnt=vmem((experts, 128), F32),
        cnt_exp=vmem((ne, experts, 128), F32),
        cnt_blk=vmem((nb, experts, 128), F32),
        q=vmem((length, half_width), BF16),
        k=vmem((length, half_width), BF16),
        v=vmem((length, half_width), BF16),
        a=vmem((length, width), BF16),
        lse=vmem((8, length), F32),
        w=vmem((half_width // PAIR, width, 3 * PAIR), BF16),
        h1=vmem((rows, width), F32),
        gate=vmem((rows, 1), F32),
        mass=vmem((1, experts), F32),
        mail=vmem((rows, width), BF16),
        disp=vmem((slots, width), BF16),
        took=vmem((slots, width), BF16),
        g=vmem((slots, width), BF16),
        du=vmem((slots, width), BF16),
        yf=vmem((max(slots, size), width), F32),
        made=vmem((length, width), F32),
        back=vmem((slots, width), BF16),
        dh1=vmem((rows, width), F32),
        do=vmem((length, half_width), BF16),
        ogot=vmem((width, half_width), BF16),
        dk_sum=vmem((length, PAIR), F32),
        dv_sum=vmem((length, PAIR), F32),
        dqkv=vmem((length, 3 * PAIR), BF16),
        sums=vmem((sum_rows, width), F32),
        sum_exp=vmem((ne, sum_rows, width), F32),
        sum_blk=vmem((nb, sum_rows, width), F32),
        late=vmem((8, FF_COLS), F32),
        late_exp=vmem((ne, 8, FF_COLS), F32),
        late_blk=vmem((nb, 8, FF_COLS), F32),
        part=vmem((4, width, half_width), BF16),
        in1=vmem((hi, width, size), BF16),
        in2=vmem((hi - 1, width, size), BF16),
        out1=vmem((hi - 1, 2, size, width), BF16),
        out2=vmem((size, width), BF16),
        in1s=dma((hi,)), in1r=dma((hi,)),
        in2s=dma((hi - 1,)), in2r=dma((hi - 1,)),
        out1s=dma((hi - 1, 2)), out1r=dma((hi - 1, 2)),
        out2s=dma, out2r=dma,
        lsem=dma((5 + 3 * (half_width // PAIR),)),
        fsem=dma((6,)),
        xs=dma((2 * seqs,)), xr=dma((nb,)),
        fws=dma((nb,)), fwr=dma((nb,)),
        os=dma((nb,)), osr=dma((2 * seqs,)),
        ds=dma((ne,)), dr=dma((ne,)),
        ces=dma((ne,)), cer=dma((ne,)), cbs=dma((nb,)), cbr=dma((nb,)),
        ns=dma((ne,)), nr=dma((ne,)),
        rs=dma((ne,)), rr=dma((ne,)),
        ys=dma((ne,)), yr=dma((ne,)),
        dos=dma((2 * seqs,)), dor=dma((nb,)),
        ows=dma, owr=dma,
        ss=dma, sr=dma,
        fs=dma((nb,)), fr=dma((2 * seqs,)),
        es=dma((ne,)), er=dma((ne,)), bs=dma((nb,)), br=dma((nb,)),
        les=dma((ne,)), ler=dma((ne,)), lbs=dma((nb,)), lbr=dma((nb,)),
    )
    if cfg["sum_here"]:
        scratch.update(
            shared=vmem((4, width, width), BF16),
            got1=vmem((4, max(nb, ne // 2), outer, half_width), BF16),
            got2=vmem((4, max(nb, ne // 2), inner, half_width), BF16),
            s5=dma((4,)),
            r5=dma((4,)),
        )
        for n in range(1, 5):
            scratch[f"s{n}"] = dma((4, max(nb, ne // 2)))
            scratch[f"r{n}"] = dma((4, max(nb, ne // 2)))
    names = [n for n, _, _ in inputs] + [n for n, _, _, _ in outputs] + list(scratch)
    out, dx, small, dwin, dwout, *wide = pl.pallas_call(
        functools.partial(layer_kernel, cfg, names),
        out_shape=[jax.ShapeDtypeStruct(shape, kind) for _, shape, kind, _ in outputs],
        in_specs=[(in_vmem if near else anywhere)(1)[0] for _, _, near in inputs],
        out_specs=[(in_vmem if near else anywhere)(1)[0] for _, _, _, near in outputs],
        scratch_shapes=list(scratch.values()),
        compiler_params=pltpu.CompilerParams(
            collective_id=1, has_side_effects=True, vmem_limit_bytes=VMEM_BYTES
        ),
        cost_estimate=pl.CostEstimate(
            flops=30 << 30, bytes_accessed=1 << 25, transcendentals=1 << 23
        ),
        name="layer",
    )(*[value for _, value, _ in inputs])
    if not cfg["sum_here"]:
        own = wide[0]
        own = jnp.concatenate(
            [
                own[:3].reshape(3, width, 3, PAIR).transpose(2, 1, 0, 3).reshape(3, width, half_width),
                own[3:],
            ]
        )
        core, empty = lax.rem(lax.axis_index("exp"), 2), jnp.zeros_like(own)
        wide = lax.psum(
            jnp.concatenate(
                [jnp.where(core == 0, own, empty), jnp.where(core == 0, empty, own)], axis=2
            ),
            ("blk", "exp"),
        )
    wide = [wide[n].astype(F32) for n in range(4)]
    return (
        out.reshape(seqs, span, width),
        small[experts + 3, 0],
        dx.reshape(seqs, span, width),
        *wide,
        small[2 : 2 + experts].T,
        dwin[None],
        dwout[None],
        small[experts + 4],
        small[experts + 5],
        small[0],
        small[1],
    )


def solution(mesh):
    return jax.shard_map(
        shards,
        mesh=mesh,
        in_specs=(
            P("exp", "blk", None),
            P("exp", "blk", None),
            P("blk", "exp", None, None),
            P(),
            P(),
            P(),
            P(),
            P(),
            P("exp", None, None),
            P("exp", None, None),
            P(),
            P(),
            P(),
            P(),
        ),
        out_specs=(
            P("exp", "blk", None),
            P(),
            P("exp", "blk", None),
            P(),
            P(),
            P(),
            P(),
            P(),
            P("exp", None, "blk"),
            P("exp", "blk", None),
            P(),
            P(),
            P(),
            P(),
        ),
        check_vma=False,
    )
```

```python
import functools

import jax
import jax.numpy as jnp
from jax import lax
from jax.experimental import pallas as pl
from jax.experimental.pallas import tpu as pltpu
from jax.sharding import PartitionSpec as P

HEAD_DIM = 64
PAIR = 2 * HEAD_DIM
EPSILON = 1e-05
SCALE = HEAD_DIM ** (-0.5)
QUERY_ROWS = 256
ROWS = 128
FF_COLS = 256
MESH = pl.DeviceIdType.MESH
BF16, F32 = jnp.bfloat16, jnp.float32
BLK_FIRST = (0, 1, 2)
PLAN = {
    "start": ((3, 1),),
    0: ((0, 1),),
    1: ((1, 1),),
    2: ((2, 1), (0, 2)),
    "rows sent": ((1, 2), (2, 2), (0, 3), (3, 2), (1, 3), (0, 4), (2, 3), (3, 3)),
    "rows done": ((1, 4), (2, 4), (3, 4)),
    "late": ((0, 5), (1, 5)),
    "last": ((2, 5), (3, 5)),
}
VMEM_BYTES = 255 << 18
NT = (((1,), (1,)), ((), ()))
TN = (((0,), (0,)), ((), ()))


def dot(left, right, dims=(((1,), (0,)), ((), ()))):
    return lax.dot_general(left, right, dims, preferred_element_type=F32)


def iota(shape, dim):
    return lax.broadcasted_iota(jnp.int32, shape, dim)


def normalize(values):
    centered = values - jnp.mean(values, axis=-1, keepdims=True)
    variance = jnp.mean(centered * centered, axis=-1, keepdims=True)
    inverse = lax.rsqrt(variance + EPSILON)
    return centered * inverse, inverse


def norm_back(hat, inverse, gain, grad):
    scaled = grad * gain
    return inverse * (
        scaled
        - jnp.mean(scaled, axis=-1, keepdims=True)
        - hat * jnp.mean(scaled * hat, axis=-1, keepdims=True)
    )


def split_rows(base, size):
    return pl.ds(pl.multiple_of(base, size), size)


class Place:
    def __init__(self, cfg):
        self.__dict__.update(cfg)
        self.b = lax.axis_index("blk")
        self.e = lax.axis_index("exp")
        self.c = lax.rem(self.e, 2)
        self.pair = self.e - self.c
        self.sibling = self.pair + 1 - self.c

    def greet(self):
        bar = pltpu.get_barrier_semaphore()

        def exp_peer(k, _):
            pl.semaphore_signal(
                bar, 1, device_id=(self.b, lax.rem(self.e + k, self.ne)), device_id_type=MESH
            )

        def blk_peer(k, _):
            there = lax.rem(self.b + k, self.nb)
            pl.semaphore_signal(bar, 1, device_id=(there, self.e), device_id_type=MESH)
            pl.semaphore_signal(bar, 1, device_id=(there, self.sibling), device_id_type=MESH)

        lax.fori_loop(1, self.ne, exp_peer, None)
        lax.fori_loop(1, self.nb, blk_peer, None)
        pl.semaphore_wait(bar, self.ne - 1 + 2 * (self.nb - 1))

    def is_me(self, there):
        return there[0] * self.ne + there[1] == self.b * self.ne + self.e


def remote(src, dst, send_sem, recv_sem, there):
    return pltpu.make_async_remote_copy(
        src, dst, send_sem, recv_sem, device_id=there, device_id_type=MESH
    )


def push(me, src, dst, send_sem, recv_sem, there):
    mine = me.is_me(there)

    @pl.when(mine)
    def _():
        pltpu.make_async_copy(src, dst, recv_sem).start()

    @pl.when(jnp.logical_not(mine))
    def _():
        remote(src, dst, send_sem, recv_sem, there).start()


def push_done(me, src, dst, send_sem, recv_sem, there):
    @pl.when(jnp.logical_not(me.is_me(there)))
    def _():
        remote(src, dst, send_sem, recv_sem, there).wait_send()


def landed(dst, recv_sem):
    pltpu.make_async_copy(dst, dst, recv_sem).wait()


def exp_peer(me, k, sign):
    near = me.ne // 2
    place = lax.rem(me.e, near)
    base = lax.rem(me.e - place + near * lax.div(k, near), me.ne)
    return base + lax.rem(place + near + sign * lax.rem(k, near), near)


def turned(me, k):
    return lax.rem(k + me.ne // 2, me.ne)


def exchange_move(me, src, dst, send_sem, recv_sem, size, k):
    there = exp_peer(me, k, 1)
    return remote(
        src.at[split_rows(there * size, size)],
        dst.at[split_rows(me.e * size, size)],
        send_sem.at[k],
        recv_sem.at[k],
        (me.b, there),
    )


def exchange_start(me, src, dst, send_sem, recv_sem, size, ahead=None):
    own = split_rows(me.e * size, size)

    def one(k, _):
        if ahead:
            k = turned(me, k)
            ahead(k, split_rows(exp_peer(me, k, 1) * size, size))
        exchange_move(me, src, dst, send_sem, recv_sem, size, k).start()

    if ahead:
        lax.fori_loop(0, me.ne // 2, one, None)
        ahead(0, own)
    pltpu.make_async_copy(src.at[own], dst.at[own], recv_sem.at[0]).start()
    lax.fori_loop(me.ne // 2 + 1 if ahead else 1, me.ne, one, None)


def exchange_wait(me, src, dst, send_sem, recv_sem, size):
    own = split_rows(me.e * size, size)
    landed(dst.at[own], recv_sem.at[0])

    def one(k, _):
        rows = split_rows(exp_peer(me, k, -1) * size, size)
        landed(dst.at[rows], recv_sem.at[k])

    lax.fori_loop(1, me.ne, one, None)


def exchange_sent(me, src, dst, send_sem, recv_sem, size):
    def one(k, _):
        exchange_move(me, src, dst, send_sem, recv_sem, size, k).wait_send()

    lax.fori_loop(1, me.ne, one, None)


def token_slots(me, idx):
    rows = idx.shape[1]
    hot = (iota((128, rows), 0) == idx).astype(F32)
    earlier = (iota((rows, rows), 0) < iota((rows, rows), 1)).astype(F32).astype(BF16)
    ahead = dot(hot.astype(BF16), earlier)
    slot = jnp.sum(ahead * hot, axis=0, keepdims=True).astype(jnp.int32) + idx * me.cap
    return slot, jnp.sum(hot, axis=1, keepdims=True)[0 : me.experts]


def slots_by_token(me, slot):
    shape = (me.experts * me.cap, slot.shape[1])
    return (iota(shape, 0) == slot).astype(F32).astype(BF16)


def head_masks():
    lane = iota((1, PAIR), 1)
    first = (lane < HEAD_DIM).astype(F32).astype(BF16)
    second = (lane >= HEAD_DIM).astype(F32).astype(BF16)
    return first, second


def gelu_parts(u):
    root = 0.7978845608028654
    cubic = 0.044715
    square = u * u
    t = jnp.tanh(root * u * (1.0 + cubic * square))
    value = 0.5 * u * (1.0 + t)
    slope = 0.5 * (1.0 + t) + (0.5 * root) * u * (1.0 - t * t) * (1.0 + 3.0 * cubic * square)
    return value, slope


class Refs:
    def __init__(self, names, refs):
        self.__dict__.update(zip(names, refs, strict=True))


class ExpertSums:
    def __init__(self, me, r):
        self.me, self.r = me, r
        self.hi, self.lo = lax.div(me.b, 2), lax.rem(me.b, 2)
        self.other = 1 - self.lo
        self.count = me.nb // 2
        self.size = me.ff // me.nb

    def turn(self, step):
        return lax.rem(self.hi + step, self.count)

    def span(self, hi, lo):
        return pl.ds(pl.multiple_of((2 * hi + lo) * self.size, 128), self.size)

    def in_first(self, hi):
        r = self.r
        there = (2 * self.hi + self.other, self.me.e)
        return remote(
            r.win.at[:, self.span(hi, self.other)], r.in1.at[hi], r.in1s.at[hi], r.in1r.at[hi], there
        )

    def in_second(self, step):
        r, hi = self.r, self.turn(step)
        return remote(
            r.win.at[:, self.span(hi, self.lo)],
            r.in2.at[step - 1],
            r.in2s.at[step - 1],
            r.in2r.at[step - 1],
            (2 * hi + self.lo, self.me.e),
        )

    def out_first(self, step, lo):
        r, hi = self.r, self.turn(step)
        return remote(
            r.wout.at[self.span(hi, lo)],
            r.out1.at[step - 1, lo],
            r.out1s.at[step - 1, lo],
            r.out1r.at[step - 1, lo],
            (2 * hi + self.lo, self.me.e),
        )

    def out_second(self):
        r = self.r
        return remote(
            r.wout.at[self.span(self.hi, self.other)],
            r.out2,
            r.out2s,
            r.out2r,
            (2 * self.hi + self.other, self.me.e),
        )

    def after_part(self, n):
        step = lax.div(n, 2) + 1
        lo = lax.rem(self.other + n, 2)

        @pl.when(lax.rem(n, 2) == 0)
        def _():
            self.in_first(self.turn(step)).start()

        @pl.when(step < self.count)
        def _():
            self.out_first(step, lo).start()

    def second_add(self):
        r = self.r
        for step in range(1, self.count):
            hi = self.turn(step)
            landed(r.in1.at[hi], r.in1r.at[hi])
            here = self.span(hi, self.lo)

            def in_rows(n, _, hi=hi, here=here):
                rows = split_rows(n * ROWS, ROWS)
                r.win[rows, here] = (
                    r.win[rows, here].astype(F32) + r.in1[hi, rows, :].astype(F32)
                ).astype(BF16)

            lax.fori_loop(0, self.me.width // ROWS, in_rows, None)
        for step in range(1, self.count):
            landed(r.out1.at[step - 1, self.other], r.out1r.at[step - 1, self.other])
        base = (2 * self.hi + self.other) * self.size

        def out_rows(n, _):
            here, rows = split_rows(base + n * ROWS, ROWS), split_rows(n * ROWS, ROWS)
            total = r.wout[here, :].astype(F32)
            for step in range(1, self.count):
                total += r.out1[step - 1, self.other, rows, :].astype(F32)
            r.wout[here, :] = total.astype(BF16)

        lax.fori_loop(0, self.size // ROWS, out_rows, None)

    def second_send(self):
        for step in range(1, self.count):
            self.in_second(step).start()
        self.out_second().start()

    def total_in(self, into):
        r = self.r
        landed(r.in1.at[self.hi], r.in1r.at[self.hi])
        for step in range(1, self.count):
            landed(r.in2.at[step - 1], r.in2r.at[step - 1])

        def in_rows(n, _):
            rows = split_rows(n * ROWS, ROWS)
            total = r.win[rows, self.span(self.hi, self.lo)].astype(F32)
            total += r.in1[self.hi, rows, :].astype(F32)
            for step in range(1, self.count):
                total += r.in2[step - 1, rows, :].astype(F32)
            into[rows, 0 : self.size] = total

        lax.fori_loop(0, self.me.width // ROWS, in_rows, None)

    def total_out(self, into):
        r = self.r
        for step in range(1, self.count):
            landed(r.out1.at[step - 1, self.lo], r.out1r.at[step - 1, self.lo])
        landed(r.out2, r.out2r)
        base = (2 * self.hi + self.lo) * self.size

        def out_rows(n, _):
            rows = split_rows(n * ROWS, ROWS)
            total = r.wout[split_rows(base + n * ROWS, ROWS), :].astype(F32)
            for step in range(1, self.count):
                total += r.out1[step - 1, self.lo, rows, :].astype(F32)
            into[rows, :] = total + r.out2[rows, :].astype(F32)

        lax.fori_loop(0, self.size // ROWS, out_rows, None)

    def sent(self):
        for step in range(1, self.count + 1):
            self.in_first(self.turn(step)).wait_send()
            if step < self.count:
                self.in_second(step).wait_send()
                for lo in range(2):
                    self.out_first(step, lo).wait_send()
        self.out_second().wait_send()


class PairSums:
    def __init__(self, me, r):
        self.me, self.r = me, r
        self.hi, self.lo = lax.div(me.b, 2), lax.rem(me.b, 2)
        self.count = me.nb // 2
        self.size = me.ff // me.nb
        self.partner = (2 * self.hi + 1 - self.lo, me.e)

    def turn(self, step):
        return lax.rem(self.hi + step, self.count)

    def place(self, hi):
        return split_rows(hi * self.size, self.size)

    def owner(self, step):
        return (2 * self.turn(step) + self.lo, self.me.e)

    def in_move(self, step):
        r, k = self.r, step - 1
        src = r.win.at[:, self.place(self.turn(step))]
        return remote(src, r.in_got.at[k], r.ins.at[k], r.inr.at[k], self.owner(step))

    def out_move(self, step):
        r, k = self.r, step - 1
        src = r.wout.at[self.place(self.turn(step))]
        return remote(src, r.out_got.at[k], r.outs.at[k], r.outr.at[k], self.owner(step))

    def second_send(self):
        for step in range(1, self.count):
            self.out_move(step).start()

    def total_in(self, into):
        r = self.r
        for step in range(1, self.count):
            landed(r.in_got.at[step - 1], r.inr.at[step - 1])

        def in_rows(n, _):
            rows = split_rows(n * ROWS, ROWS)
            total = r.win[rows, self.place(self.hi)].astype(F32)
            for step in range(1, self.count):
                total += r.in_got[step - 1, rows, :].astype(F32)
            into[rows, 0 : self.size] = total

        lax.fori_loop(0, self.me.width // ROWS, in_rows, None)

    def total_out(self, into):
        r = self.r
        for step in range(1, self.count):
            landed(r.out_got.at[step - 1], r.outr.at[step - 1])

        def out_rows(n, _):
            rows = split_rows(n * ROWS, ROWS)
            total = r.wout[split_rows(self.hi * self.size + n * ROWS, ROWS), :].astype(F32)
            for step in range(1, self.count):
                total += r.out_got[step - 1, rows, :].astype(F32)
            into[rows, :] = total

        lax.fori_loop(0, self.size // ROWS, out_rows, None)

    def sent(self):
        for step in range(1, self.count):
            self.in_move(step).wait_send()
            self.out_move(step).wait_send()


class SharedSum:
    def __init__(self, me, r, p, blk_first):
        self.me, self.r, self.p = me, r, p
        z = lax.div(me.e, 2)
        nz = me.ne // 2
        blk = (me.b, me.nb, lambda t: (t, me.e))
        along_z = (z, nz, lambda t: (me.b, 2 * t + me.c))
        self.first, self.second = (blk, along_z) if blk_first else (along_z, blk)
        self.outer = me.width // self.first[1]
        self.inner = self.outer // self.second[1]

    def outer_rows(self, t):
        return split_rows(t * self.outer, self.outer)

    def inner_rows(self, t, s):
        return split_rows(t * self.outer + s * self.inner, self.inner)

    def view(self, rows, core):
        me, r, p = self.me, self.r, self.p
        if p < 3:
            return r.shared.at[
                pl.ds(0, 3), rows, pl.ds(pl.multiple_of(core * me.half_width + p * PAIR, PAIR), PAIR)
            ]
        return r.shared.at[
            3, rows, pl.ds(pl.multiple_of(core * me.half_width, PAIR), me.half_width)
        ]

    def peer(self, axis, k):
        return lax.rem(axis[0] + k, axis[1])

    def source(self, axis, k):
        return lax.rem(axis[0] + axis[1] - k, axis[1])

    def move1(self, k):
        r, p = self.r, self.p
        t = self.peer(self.first, k)
        return remote(
            r.part.at[p, self.outer_rows(t)],
            r.got1.at[p, k, pl.ds(0, self.outer)],
            r.s1.at[p, k],
            r.r1.at[p, k],
            self.first[2](t),
        )

    def move2(self, k):
        r, p = self.r, self.p
        t = self.peer(self.second, k)
        return remote(
            r.got1.at[p, 0, split_rows(t * self.inner, self.inner)],
            r.got2.at[p, k],
            r.s2.at[p, k],
            r.r2.at[p, k],
            self.second[2](t),
        )

    def move3(self, k):
        r, p = self.r, self.p
        here = self.view(self.inner_rows(self.first[0], self.second[0]), self.me.c)
        return remote(
            here, here, r.s3.at[p, k], r.r3.at[p, k], self.second[2](self.peer(self.second, k))
        )

    def move4(self, k):
        r, p = self.r, self.p
        here = self.view(self.outer_rows(self.first[0]), self.me.c)
        return remote(
            here, here, r.s4.at[p, k], r.r4.at[p, k], self.first[2](self.peer(self.first, k))
        )

    def move5(self):
        r, p = self.r, self.p
        here = self.view(pl.ds(0, self.me.width), self.me.c)
        return remote(here, here, r.s5.at[p], r.r5.at[p], (self.me.b, self.me.sibling))

    def stage1(self):
        for k in range(1, self.first[1]):
            self.move1(k).start()

    def stage2(self):
        r, p = self.r, self.p
        total = r.part[p, self.outer_rows(self.first[0])].astype(F32)
        for k in range(1, self.first[1]):
            here = r.got1.at[p, k, pl.ds(0, self.outer)]
            landed(here, r.r1.at[p, k])
            total += here[...].astype(F32)
        r.got1[p, 0, 0 : self.outer, :] = total.astype(BF16)
        for k in range(1, self.second[1]):
            self.move2(k).start()

    def stage3(self):
        r, p = self.r, self.p
        total = r.got1[p, 0, split_rows(self.second[0] * self.inner, self.inner)].astype(F32)
        for k in range(1, self.second[1]):
            landed(r.got2.at[p, k], r.r2.at[p, k])
            total += r.got2[p, k].astype(F32)
        total = total.astype(BF16)
        here = self.view(self.inner_rows(self.first[0], self.second[0]), self.me.c)
        if p < 3:
            for j in range(3):
                here[j] = total[:, j * PAIR : (j + 1) * PAIR]
        else:
            here[...] = total
        for k in range(1, self.second[1]):
            self.move3(k).start()

    def stage4(self):
        for k in range(1, self.second[1]):
            rows = self.inner_rows(self.first[0], self.source(self.second, k))
            landed(self.view(rows, self.me.c), self.r.r3.at[self.p, k])
        for k in range(1, self.first[1]):
            self.move4(k).start()

    def stage5(self):
        for k in range(1, self.first[1]):
            rows = self.outer_rows(self.source(self.first, k))
            landed(self.view(rows, self.me.c), self.r.r4.at[self.p, k])
        self.move5().start()

    def end(self):
        landed(self.view(pl.ds(0, self.me.width), 1 - self.me.c), self.r.r5.at[self.p])
        for k in range(1, self.first[1]):
            self.move1(k).wait_send()
            self.move4(k).wait_send()
        for k in range(1, self.second[1]):
            self.move2(k).wait_send()
            self.move3(k).wait_send()
        self.move5().wait_send()


class AllSum:
    def __init__(self, me, own, by_exp, by_blk, sems):
        self.me, self.own, self.by_exp, self.by_blk = me, own, by_exp, by_blk
        self.es, self.er, self.bs, self.br = sems

    def exp_move(self, k):
        me = self.me
        there = (me.b, lax.rem(me.e + k, me.ne))
        return remote(self.own, self.by_exp.at[me.e], self.es.at[k], self.er.at[k], there)

    def blk_move(self, k):
        me = self.me
        here = self.by_blk.at[me.b]
        there = (lax.rem(me.b + k, me.nb), me.e)
        return remote(here, here, self.bs.at[k], self.br.at[k], there)

    def start(self):
        lax.fori_loop(1, self.me.ne, lambda k, _: self.exp_move(k).start(), None)
        self.by_exp[self.me.e] = self.own[...]

    def middle(self):
        me = self.me

        def arrived(k, _):
            landed(self.by_exp.at[lax.rem(me.e + me.ne - k, me.ne)], self.er.at[k])

        lax.fori_loop(1, me.ne, arrived, None)
        self.by_blk[me.b] = jnp.sum(self.by_exp[...], axis=0)
        for k in range(1, me.nb):
            self.blk_move(k).start()

    def total(self):
        me = self.me
        for k in range(1, me.nb):
            landed(self.by_blk.at[lax.rem(me.b + me.nb - k, me.nb)], self.br.at[k])
        return jnp.sum(self.by_blk[...], axis=0)

    def sent(self):
        lax.fori_loop(1, self.me.ne, lambda k, _: self.exp_move(k).wait_send(), None)
        for k in range(1, self.me.nb):
            self.blk_move(k).wait_send()


def layer_kernel(cfg, names, *refs):
    me = Place(cfg)
    r = Refs(names, refs)
    half = me.span // 2
    pairs = me.half_width // PAIR
    blocks = me.length // QUERY_ROWS
    slots = me.experts * me.cap
    roomy = slots * me.width <= 1 << 19
    model_tile = me.width if roomy else FF_COLS
    early_g = r.g.at[0] if me.paired else r.g
    r.ysend, r.yback = early_g, r.dh2 if me.paired else r.du
    r.swap, r.da_in = r.took.at[pl.ds(0, me.rows)], r.back.at[pl.ds(0, me.rows)]
    r.xin, r.o_send, r.lse_cols, r.dh_send = r.mail, early_g, r.dk_sum, r.disp
    gain1, bias1, gain2, bias2 = (
        v[...].reshape(1, me.width) for v in (r.gain1, r.bias1, r.gain2, r.bias2)
    )
    loads = {}
    sums = PairSums(me, r) if me.paired else ExpertSums(me, r)
    whole = ("x", "og", "wo") if me.paired else ("x", "og", "wo", "win", "wout")
    for name in whole:
        loads[name] = pltpu.make_async_copy(
            getattr(r, name + "_hbm"), getattr(r, name), r.lsem.at[len(loads)]
        )
    for p in range(pairs):
        for j, matrix in enumerate((r.wq_hbm, r.wk_hbm, r.wv_hbm)):
            src = matrix.at[:, pl.ds(pl.multiple_of(me.c * me.half_width + p * PAIR, PAIR), PAIR)]
            loads["w", p, j] = pltpu.make_async_copy(
                src, r.w.at[p, :, pl.ds(j * PAIR, PAIR)], r.lsem.at[len(loads)]
            )
    for h in range(sums.count) if me.paired else ():
        part = pl.ds(pl.multiple_of((2 * h + sums.lo) * sums.size, 128), sums.size)
        place = pl.ds(h * sums.size, sums.size)
        loads["win", h] = pltpu.make_async_copy(
            r.win_hbm.at[:, part], r.win.at[:, place], r.lsem.at[len(loads)]
        )
        loads["wout", h] = pltpu.make_async_copy(
            r.wout_hbm.at[part], r.wout.at[place], r.lsem.at[len(loads)]
        )
    for load in loads.values():
        load.start()
    me.greet()

    def row_moves():
        for s in range(me.seqs):
            for h in range(2):
                yield (
                    r.x_hbm.at[pl.ds(s * me.span + h * half, half)],
                    r.xin.at[split_rows(me.b * half, half)],
                    r.xs.at[2 * s + h],
                    r.xr.at[me.b],
                    (me.c * me.seqs + s, me.pair + h),
                )

    for move in row_moves():
        push(me, *move)

    slot, counts = token_slots(me, r.idx[...])
    r.cnt[...] = jnp.broadcast_to(counts, r.cnt.shape)
    count_sum = AllSum(me, r.cnt, r.cnt_exp, r.cnt_blk, (r.ces, r.cer, r.cbs, r.cbr))
    count_sum.start()
    r.idx_col[...] = jnp.transpose(
        jnp.broadcast_to(r.idx[...].astype(F32), (128, me.rows))
    )
    loads["og"].wait()
    r.dh_send[...] = dot(slots_by_token(me, slot), r.og[...]).astype(BF16)
    exchange_start(me, r.dh_send, r.dh, r.ds, r.dr, me.cap)

    def forward_move(j):
        rows = split_rows(j * me.span + me.c * half, half)
        return remote(r.a.at[rows], r.a.at[rows], r.fws.at[j], r.fwr.at[j], (me.b, me.sibling))

    for j in range(me.nb):
        landed(r.xin.at[pl.ds(j * half, half)], r.xr.at[j])
        hat, _ = normalize(r.xin[pl.ds(j * half, half), :].astype(F32))
        r.a[split_rows(j * me.span + me.c * half, half), :] = (hat * gain1 + bias1).astype(BF16)
        forward_move(j).start()

    for p in range(pairs):
        for j in range(3):
            loads["w", p, j].wait()
    first, second = head_masks()
    spans = QUERY_ROWS // me.span
    lane = iota((1, PAIR), 1)
    visible = iota((QUERY_ROWS, QUERY_ROWS), 1) <= iota((QUERY_ROWS, QUERY_ROWS), 0)
    home = me.pair + lax.div(me.b, me.seqs)
    columns = pl.ds(pl.multiple_of(me.c * me.half_width, PAIR), me.half_width)

    def o_move(j):
        return (
            r.o_send.at[
                pl.ds(j * me.span % me.rows, me.span),
                pl.ds(j * me.span // me.rows * me.half_width, me.half_width),
            ],
            r.o.at[split_rows(lax.rem(me.b, me.seqs) * me.span, me.span), columns],
            r.os.at[j],
            r.osr.at[2 * lax.rem(me.b, me.seqs) + me.c],
            (j, home),
        )

    def dh_slot(k):
        return split_rows(exp_peer(me, jnp.int32(k), -1) * me.cap, me.cap)

    def dh_move(k):
        rows = dh_slot(k)
        return remote(r.dh.at[rows], r.dh2.at[rows], r.d2s.at[k], r.d2r.at[k], sums.partner)

    def dh_arrived(k):
        landed(r.dh.at[dh_slot(k)], r.dr.at[k])
        if me.paired:
            dh_move(k).start()

    for i in range(blocks):
        for j in range(i * spans, (i + 1) * spans):
            theirs = split_rows(j * me.span + (1 - me.c) * half, half)
            landed(r.a.at[theirs], r.fwr.at[j])
        here = pl.ds(i * QUERY_ROWS, QUERY_ROWS)

        def pair_of_heads(p, _, i=i, here=here):
            lanes = split_rows(p * PAIR, PAIR)
            qkv = dot(r.a[here, :], r.w[p]).astype(BF16)
            queries = qkv[:, 0:PAIR] * jnp.asarray(SCALE, BF16)
            r.q[here, lanes] = queries
            r.k[here, lanes] = qkv[:, PAIR : 2 * PAIR]
            r.v[here, lanes] = qkv[:, 2 * PAIR : 3 * PAIR]
            parts = [pl.ds(i * QUERY_ROWS, QUERY_ROWS)]
            if i:
                parts.append(pl.ds(0, i * QUERY_ROWS))
            done = []
            for h, mask in enumerate((first, second)):
                masked = queries * mask
                scores = [dot(masked, r.k[part, lanes], NT) for part in parts]
                scores[0] = jnp.where(visible, scores[0], -1e30)
                peak = functools.reduce(
                    jnp.maximum, [jnp.max(s, axis=1, keepdims=True) for s in scores]
                )
                powers = [jnp.exp(s - peak) for s in scores]
                total = sum(jnp.sum(s, axis=1, keepdims=True) for s in powers)
                mixed = sum(
                    dot(s.astype(BF16), r.v[part, lanes]) for s, part in zip(powers, parts)
                )
                done.append(mixed / total)
                r.lse_cols[here, :] = jnp.where(
                    lane == 2 * p + h, peak + jnp.log(total), r.lse_cols[here, :]
                )
            base = i * QUERY_ROWS // me.rows * me.half_width
            r.o_send[
                pl.ds(i * QUERY_ROWS % me.rows, QUERY_ROWS),
                pl.ds(pl.multiple_of(base + p * PAIR, PAIR), PAIR),
            ] = jnp.where(lane < HEAD_DIM, done[0], done[1]).astype(BF16)

        lax.fori_loop(0, pairs, pair_of_heads, None)
        for j in range(i * spans, (i + 1) * spans):
            push(me, *o_move(j))
        if i == 0:
            count_sum.middle()
        for k in range(me.ne):
            if (i == blocks - 1) if not me.paired else (max(0, k + 1 - me.ne // 2) == i):
                dh_arrived(k)
    for k in range(me.ne // 2 + blocks - 1, me.ne) if me.paired else ():
        dh_arrived(k)
    r.lse[...] = jnp.transpose(r.lse_cols[...])[0:8, :]
    for j in range(me.nb):
        forward_move(j).wait_send()
        push_done(me, *o_move(j))
    for move in row_moves():
        push_done(me, *move)
    for name in ("x", "wo"):
        loads[name].wait()
    exchange_sent(me, r.dh_send, r.dh, r.ds, r.dr, me.cap)

    expert_lane = iota((ROWS, me.experts), 1)
    r.sums[...] = jnp.zeros_like(r.sums)
    r.mass[...] = jnp.zeros_like(r.mass)
    for s in range(me.seqs):
        for h in range(2):
            landed(
                r.o.at[pl.ds(s * me.span, me.span), pl.ds(h * me.half_width, me.half_width)],
                r.osr.at[2 * s + h],
            )

    def token_rows(n, _):
        here = split_rows(n * ROWS, ROWS)
        hidden = r.x[here, :].astype(F32) + dot(r.o[here, :], r.wo[...])
        r.h1[here, :] = hidden
        hat, _ = normalize(hidden)
        normed = (hat * gain2 + bias2).astype(BF16)
        r.mail[here, :] = normed
        logits = dot(normed, r.router[...], NT)
        hot = r.idx_col[here, 0 : me.experts].astype(jnp.int32) == expert_lane
        value = jax.nn.sigmoid(jnp.sum(jnp.where(hot, logits, 0.0), axis=1, keepdims=True))
        r.gate[here, :] = value
        r.mass[...] += jnp.sum(jnp.where(hot, value, 0.0), axis=0, keepdims=True)

    lax.fori_loop(0, me.rows // ROWS, token_rows, None)
    takes = slots_by_token(me, slot)
    r.disp[...] = dot(takes, r.mail[...]).astype(BF16)
    exchange_start(me, r.disp, r.took, r.ns, r.nr, me.cap)
    for key, load in loads.items():
        if key in ("win", "wout") or key[0] in ("win", "wout"):
            load.wait()

    def took_move(k, rows):
        return remote(r.took.at[rows], r.took2.at[rows], r.t2s.at[k], r.t2r.at[k], sums.partner)

    if not me.paired:
        exchange_wait(me, r.disp, r.took, r.ns, r.nr, me.cap)
        exchange_sent(me, r.disp, r.took, r.ns, r.nr, me.cap)

    lanes = iota((slots, me.experts), 1)

    def gate_of(rows, lanes):
        logits = dot(rows, r.router[...], NT)
        picked = jnp.sum(jnp.where(lanes == me.e, logits, 0.0), axis=1, keepdims=True)
        return jax.nn.sigmoid(picked)

    if not me.paired:
        value = gate_of(r.took[...], lanes)
        r.disp[...] = (value * r.dh[...].astype(F32)).astype(BF16)
        r.yf[0:slots, :] = jnp.zeros((slots, me.width), F32)
        r.made[...] = jnp.zeros_like(r.made)
    slot_rows = slots if roomy else slots // 4

    def expert_part(n, _):
        hi, lo = sums.turn(lax.div(n, 2) + 1), lax.rem(sums.other + n, 2)
        base = (2 * hi + lo) * sums.size

        def hidden_columns(f, _):
            here = pl.ds(pl.multiple_of(base + f * sums.tile, 128), sums.tile)
            there = pl.ds(pl.multiple_of(f * sums.tile, 128), sums.tile)

            def hidden_rows(n, _):
                rows = split_rows(n * slot_rows, slot_rows)
                act, slope = gelu_parts(dot(r.took[rows, :], r.win[:, here]))
                r.g[rows, there] = act.astype(BF16)
                r.du[rows, there] = (dot(r.disp[rows, :], r.wout[here, :], NT) * slope).astype(BF16)

            lax.fori_loop(0, slots // slot_rows, hidden_rows, None)

        lax.fori_loop(0, sums.size // sums.tile, hidden_columns, None)
        part = sums.span(hi, lo)


        def model_columns(f, _):
            here = split_rows(f * model_tile, model_tile)
            r.yf[0:slots, here] += dot(r.g[:, 0 : sums.size], r.wout[part, here])
            r.made[0:slots, here] += dot(r.du[:, 0 : sums.size], r.win[here, part], NT)

        lax.fori_loop(0, me.width // model_tile, model_columns, None)

        def weight_columns(f, _):
            here = pl.ds(pl.multiple_of(base + f * sums.tile, 128), sums.tile)
            there = pl.ds(pl.multiple_of(f * sums.tile, 128), sums.tile)
            r.win[:, here] = dot(r.took[...], r.du[:, there], TN).astype(BF16)
            r.wout[here, :] = dot(r.g[:, there], r.disp[...], TN).astype(BF16)

        lax.fori_loop(0, sums.size // sums.tile, weight_columns, None)
        sums.after_part(n)

    near = me.ne // 2
    half_slots = near * me.cap
    half_lanes = iota((half_slots, me.experts), 1)

    def products(took, dh, dy, act, back, rows):
        gates = gate_of(took[rows, :], half_lanes)
        dy[rows, :] = (gates * dh[rows, :].astype(F32)).astype(BF16)
        for h in range(sums.count):
            place = pl.ds(h * sums.size, sums.size)
            value, slope = gelu_parts(dot(took[rows, :], r.win[:, place]))
            act.at[h][rows, :] = value.astype(BF16)
            back.at[h][rows, :] = (dot(dy[rows, :], r.wout[place, :], NT) * slope).astype(BF16)
        places = [pl.ds(h * sums.size, sums.size) for h in range(sums.count)]
        made_y = sum(dot(act.at[h][rows, :], r.wout[place, :]) for h, place in enumerate(places))
        made_dn = sum(
            dot(back.at[h][rows, :], r.win[:, place], NT) for h, place in enumerate(places)
        )
        return gates, made_y, made_dn

    def dgate_rows(dh, y):
        return jnp.sum(dh.astype(F32) * y, axis=1, keepdims=True)

    def dn_move(k, rows):
        return remote(r.dn2.at[rows], r.dn_got.at[rows], r.g2s.at[k], r.g2r.at[k], sums.partner)

    def slot_rows_of(k):
        return split_rows(exp_peer(me, k, 1) * me.cap, me.cap)

    if me.paired:
        act2 = r.shared.at[pl.ds(0, sums.count), pl.ds(0, slots)]
        back2 = r.shared.at[pl.ds(sums.count, sums.count), pl.ds(0, slots)]

        def half_rows(n, _):
            def pass_on(k, _):
                rows = split_rows(exp_peer(me, k, -1) * me.cap, me.cap)
                landed(r.took.at[rows], r.nr.at[k])
                took_move(k, rows).start()

            def arrived(k, _):
                rows = split_rows(exp_peer(me, k, -1) * me.cap, me.cap)
                landed(r.dh2.at[rows], r.d2r.at[k])
                landed(r.took2.at[rows], r.t2r.at[k])

            lax.fori_loop(n * near, (n + 1) * near, pass_on, None)
            base = lax.rem(me.e - lax.rem(me.e, near) + n * near, me.ne)
            rows = pl.ds(pl.multiple_of(base * me.cap, half_slots), half_slots)
            gates, made_y, made_dn = products(r.took, r.dh, r.dy, r.g, r.du, rows)
            r.value[rows, :] = gates
            r.dgate[rows, :] = dgate_rows(r.dh[rows, :], made_y)
            r.yf[rows, :] = made_y
            r.made[rows, :] = made_dn
            lax.fori_loop(n * near, (n + 1) * near, arrived, None)
            _, made_y, made_dn = products(r.took2, r.dh2, r.dy2, act2, back2, rows)
            r.dgate2[rows, :] = dgate_rows(r.dh2[rows, :], made_y)
            r.y2[rows, :] = made_y.astype(BF16)
            r.dn2[rows, :] = made_dn.astype(BF16)

        lax.fori_loop(0, 2, half_rows, None)
        exchange_sent(me, r.disp, r.took, r.ns, r.nr, me.cap)
        r.dg_send[...] = jnp.transpose(jnp.broadcast_to(r.dgate2[...], (slots, 128)))[0:8, :]
        dg_move = remote(r.dg_send, r.dg_got, r.dgs, r.dgr, sums.partner)
        dg_move.start()

        def dn_start(n, _):
            k = turned(me, n)
            dn_move(k, slot_rows_of(k)).start()

        lax.fori_loop(0, me.ne, dn_start, None)

        def y_move(part):
            rows = pl.ds(part * half_slots, half_slots)
            return remote(
                r.y2.at[rows], r.y_got.at[rows], r.y2s.at[part], r.y2r.at[part], sums.partner
            )

        y_move(0).start()

        def weight_part(hi):
            place = sums.place(hi)
            r.win[:, place] = (
                dot(r.took[...], r.du[hi], TN) + dot(r.took2[...], back2[hi], TN)
            ).astype(BF16)
            r.wout[place, :] = (
                dot(r.g[hi], r.dy[...], TN) + dot(act2[hi], r.dy2[...], TN)
            ).astype(BF16)

        for step in range(1, sums.count):
            weight_part(sums.turn(step))
            sums.in_move(step).start()
    else:
        sums.tile = sums.size
        lax.fori_loop(0, me.nb, expert_part, None)

    weights = (count_sum.total() - me.mean_load) / me.mean_load
    weight = jnp.sum(jnp.where(iota(weights.shape, 0) == me.e, weights, 0.0), axis=0, keepdims=True)
    weight = weight[:, 0:1]
    if me.paired:
        landed(r.dg_got, r.dgr)
        theirs = jnp.transpose(jnp.broadcast_to(r.dg_got[0:1, :], (128, slots)))[:, 0:1]
        dgate = r.dgate[...] + theirs + weight / me.tokens
        value = r.value[...]
    else:
        r.ysend[...] = r.yf[0:slots, :].astype(BF16)
        dgate = (
            jnp.sum(r.dh[...].astype(F32) * r.ysend[...].astype(F32), axis=1, keepdims=True)
            + weight / me.tokens
        )
    dlogits = jnp.where(lanes == me.e, dgate * value * (1.0 - value), 0.0).astype(BF16)
    if me.paired:
        r.made[0:slots, :] += dot(dlogits, r.router[...])

        def add_theirs(k, rows):
            landed(r.dn_got.at[rows], r.g2r.at[k])
            r.disp[rows, :] = (r.made[rows, :] + r.dn_got[rows, :].astype(F32)).astype(BF16)

        exchange_start(me, r.disp, r.back, r.rs, r.rr, me.cap, ahead=add_theirs)
        weight_part(sums.hi)
    else:
        r.disp[...] = (r.made[0:slots, :] + dot(dlogits, r.router[...])).astype(BF16)
        exchange_start(me, r.disp, r.back, r.rs, r.rr, me.cap)
    r.sums[2 : 2 + me.experts, :] = dot(dlogits, r.took[...], TN)
    r.sums[2 + me.experts : 3 + me.experts, 0 : me.experts] = r.mass[...]
    if not me.paired:
        sums.second_add()
    exchange_wait(me, r.disp, r.back, r.rs, r.rr, me.cap)

    r.made[0 : me.rows, :] = dot(takes, r.back[...], TN)

    def norm_rows(n, _):
        here = split_rows(n * ROWS, ROWS)
        grad = r.made[here, :]
        hat, inverse = normalize(r.h1[here, :])
        r.sums[0:1, :] += jnp.sum(grad * hat, axis=0, keepdims=True)
        r.sums[1:2, :] += jnp.sum(grad, axis=0, keepdims=True)
        total = r.og[here, :].astype(F32) + norm_back(hat, inverse, gain2, grad)
        r.dh1[here, :] = total
        r.mail[here, :] = dot(total.astype(BF16), r.wo[...], NT).astype(BF16)

    def do_moves(s):
        for h in range(2):
            yield (
                r.mail.at[pl.ds(s * me.span, me.span), pl.ds(h * me.half_width, me.half_width)],
                r.do.at[split_rows(me.b * me.span, me.span)],
                r.dos.at[2 * s + h],
                r.dor.at[me.b],
                (me.c * me.seqs + s, me.pair + h),
            )

    steps = me.span // ROWS
    for s in range(me.seqs):
        lax.fori_loop(s * steps, (s + 1) * steps, norm_rows, None)
        for move in do_moves(s):
            push(me, *move)
    sums.second_send()
    early = AllSum(me, r.sums, r.sum_exp, r.sum_blk, (r.es, r.er, r.bs, r.br))
    early.start()
    if me.paired:
        y_move(1).start()
        lax.fori_loop(
            0,
            me.ne,
            lambda k, _: took_move(k, split_rows(exp_peer(me, k, -1) * me.cap, me.cap)).wait_send(),
            None,
        )

    def output_columns(core):
        cols = pl.ds(pl.multiple_of(core * me.half_width, PAIR), me.half_width)
        return dot(r.o[...], r.dh1[:, cols].astype(BF16), TN)

    r.part[0] = output_columns(1 - me.c).astype(BF16)
    o_swap = remote(r.part.at[0], r.ogot, r.ows, r.owr, (me.b, me.sibling))
    o_swap.start()
    own_columns = output_columns(me.c)
    o_swap.wait()
    r.part[3] = (own_columns + r.ogot[...].astype(F32)).astype(BF16)
    pieces = [SharedSum(me, r, p, p in BLK_FIRST) for p in range(4)] if me.sum_here else []

    def advance(point):
        for p, stage in PLAN.get(point, ()) if pieces else ():
            getattr(pieces[p], f"stage{stage}")()

    advance("start")
    if me.paired:
        for part in range(2):
            landed(r.y_got.at[pl.ds(part * half_slots, half_slots)], r.y2r.at[part])
        r.ysend[...] = (r.yf[0:slots, :] + r.y_got[...].astype(F32)).astype(BF16)
    exchange_start(me, r.ysend, r.yback, r.ys, r.yr, me.cap)

    r.made[...] = jnp.zeros_like(r.made)
    for j in range(me.nb):
        landed(r.do.at[pl.ds(j * me.span, me.span)], r.dor.at[j])
    visible = iota((QUERY_ROWS, QUERY_ROWS), 0) <= iota((QUERY_ROWS, QUERY_ROWS), 1)

    def pair_back(n, _):
        lanes = split_rows(n * PAIR, PAIR)
        r.dk_sum[...] = jnp.zeros_like(r.dk_sum)
        r.dv_sum[...] = jnp.zeros_like(r.dv_sum)
        for i in range(blocks):
            here = pl.ds(i * QUERY_ROWS, QUERY_ROWS)
            queries, grads = r.q[here, lanes], r.do[here, lanes]
            parts = [here]
            if i:
                parts.append(pl.ds(0, i * QUERY_ROWS))
            dq_block = jnp.zeros((QUERY_ROWS, PAIR), F32)
            for h, mask in enumerate((first, second)):
                qm, gm = queries * mask, grads * mask
                log_sums = r.lse[pl.ds(2 * n + h, 1), here]
                scores = [dot(r.k[part, lanes], qm, NT) for part in parts]
                powers = [jnp.exp(s - log_sums) for s in scores]
                powers[0] = jnp.where(visible, powers[0], 0.0)
                weighted = [
                    s * dot(r.v[part, lanes], gm, NT) for s, part in zip(powers, parts)
                ]
                delta = sum(jnp.sum(t, axis=0, keepdims=True) for t in weighted)
                for s, t, part in zip(powers, weighted, parts):
                    ds = (t - s * delta).astype(BF16)
                    r.dv_sum[part, :] += dot(s.astype(BF16), gm)
                    r.dk_sum[part, :] += dot(ds, qm)
                    dq_block += dot(ds, r.k[part, lanes] * mask, TN)
            r.dqkv[here, 0:PAIR] = (dq_block * SCALE).astype(BF16)
        r.dqkv[:, PAIR : 2 * PAIR] = r.dk_sum[...].astype(BF16)
        r.dqkv[:, 2 * PAIR : 3 * PAIR] = r.dv_sum[...].astype(BF16)
        r.part[n] = dot(r.a[...], r.dqkv[...], TN).astype(BF16)

        def normed_columns(f, _):
            cols = split_rows(f * model_tile, model_tile)
            r.made[:, cols] += dot(r.dqkv[...], r.w[n, cols, :], NT)

        lax.fori_loop(0, me.width // model_tile, normed_columns, None)
        for done in range(pairs):

            @pl.when(n == done)
            def _(done=done):
                advance(done)

    lax.fori_loop(0, pairs, pair_back, None)
    early.middle()

    for s in range(me.seqs):
        for move in do_moves(s):
            push_done(me, *move)
    for j in range(me.nb):
        theirs = split_rows(j * me.span + (1 - me.c) * half, half)
        r.mail[pl.ds(j * half, half), :] = r.made[theirs, :].astype(BF16)
    swap = remote(r.mail, r.swap, r.ss, r.sr, (me.b, me.sibling))
    swap.start()
    exchange_wait(me, r.ysend, r.yback, r.ys, r.yr, me.cap)
    r.yf[0 : me.rows, :] = dot(takes, r.yback[...], TN)

    def out_rows(n, _):
        here = split_rows(n * ROWS, ROWS)
        r.out[here, :] = (r.h1[here, :] + r.gate[here, :] * r.yf[here, :]).astype(BF16)

    lax.fori_loop(0, me.rows // ROWS, out_rows, None)
    swap.wait()
    def da_move(j):
        return (
            r.mail.at[pl.ds(j * half, half)],
            r.da_in.at[split_rows(lax.rem(me.b, me.seqs) * me.span + me.c * half, half)],
            r.fs.at[j],
            r.fr.at[2 * lax.rem(me.b, me.seqs) + me.c],
            (j, home),
        )

    for j in range(me.nb):
        mine = r.made[split_rows(j * me.span + me.c * half, half), :]
        rows = pl.ds(j * half, half)
        r.mail[rows, :] = (mine + r.swap[rows, :].astype(F32)).astype(BF16)
        push(me, *da_move(j))
    advance("rows sent")
    for s in range(me.seqs):
        for h in range(2):
            landed(r.da_in.at[pl.ds(s * me.span + h * half, half)], r.fr.at[2 * s + h])

    r.late[...] = jnp.zeros_like(r.late)
    tiles = me.width // FF_COLS

    def first_norm_rows(n, _):
        here = split_rows(n * ROWS, ROWS)
        grad = r.da_in[here, :].astype(F32)
        hat, inverse = normalize(r.x[here, :].astype(F32))
        gain_part = jnp.sum(grad * hat, axis=0, keepdims=True)
        bias_part = jnp.sum(grad, axis=0, keepdims=True)
        for j in range(tiles):
            cols = slice(j * FF_COLS, (j + 1) * FF_COLS)
            r.late[j : j + 1, :] += gain_part[:, cols]
            r.late[tiles + j : tiles + j + 1, :] += bias_part[:, cols]
        r.dx[here, :] = (r.dh1[here, :] + norm_back(hat, inverse, gain1, grad)).astype(BF16)

    lax.fori_loop(0, me.rows // ROWS, first_norm_rows, None)
    late = AllSum(me, r.late, r.late_exp, r.late_blk, (r.les, r.ler, r.lbs, r.lbr))
    late.start()
    advance("rows done")
    late.middle()
    advance("late")

    size = sums.size
    sums.total_in(r.made)
    store_in = pltpu.make_async_copy(
        r.made.at[pl.ds(0, me.width), pl.ds(0, size)], r.dwin, r.fsem.at[0]
    )
    store_in.start()
    sums.total_out(r.yf)
    store_out = pltpu.make_async_copy(r.yf.at[pl.ds(0, size)], r.dwout, r.fsem.at[1])
    store_out.start()
    advance("last")
    early_total = early.total()
    late_total = late.total()
    r.small[0 : r.sums.shape[0], :] = early_total
    for j in range(tiles):
        cols = slice(j * FF_COLS, (j + 1) * FF_COLS)
        r.small[me.experts + 4 : me.experts + 5, cols] = late_total[j : j + 1, :]
        r.small[me.experts + 5 : me.experts + 6, cols] = late_total[tiles + j : tiles + j + 1, :]
    own_weight = jnp.transpose(jnp.broadcast_to(weights, (weights.shape[0], 128)))[0:1, :]
    mass = early_total[2 + me.experts : 3 + me.experts, 0 : me.experts]
    r.small[me.experts + 3 : me.experts + 4, 0:1] = (
        jnp.sum(own_weight[:, 0 : me.experts] * mass, axis=1, keepdims=True) / me.tokens
    )
    for each in (count_sum, early, late):
        each.sent()
    exchange_sent(me, r.disp, r.back, r.rs, r.rr, me.cap)
    exchange_sent(me, r.ysend, r.yback, r.ys, r.yr, me.cap)
    for j in range(me.nb):
        push_done(me, *da_move(j))
    sums.sent()
    if me.paired:
        for k in range(me.ne):
            dh_move(k).wait_send()
        dg_move.wait_send()
        for part in range(2):
            y_move(part).wait_send()
        lax.fori_loop(0, me.ne, lambda k, _: dn_move(k, slot_rows_of(k)).wait_send(), None)
    stores = [store_in, store_out]
    for piece in pieces:
        piece.end()
    if pieces:
        targets = [(r.shared.at[j], out) for j, out in enumerate((r.gq, r.gk, r.gv, r.go))]
    else:
        targets = [(r.part, r.own_part)]
    for n, (src, dst) in enumerate(targets):
        store = pltpu.make_async_copy(src, dst, r.fsem.at[2 + n])
        store.start()
        stores.append(store)
    for store in stores:
        store.wait()


def in_vmem(count):
    return [pl.BlockSpec(memory_space=pltpu.VMEM)] * count


def anywhere(count):
    return [pl.BlockSpec(memory_space=pl.ANY)] * count


def finish_kernel(experts, *refs):
    small, *narrow = refs[: len(refs) // 2 - 2]
    balance, router, *rest = refs[len(refs) // 2 - 2 :]
    norms, wide = rest[:4], rest[4:]
    for src, dst in zip(narrow, wide, strict=True):
        dst[...] = src[...].astype(dst.dtype)

    @pl.when(pl.program_id(0) == 0)
    def _():
        balance[...] = small[experts + 3 : experts + 4, 0:128]
        router[...] = small[2 : 2 + experts, :]
        for dst, row in zip(norms, (experts + 4, experts + 5, 0, 1), strict=True):
            dst[...] = small[row, :]


def finish(experts, small, narrow, kinds):
    steps = 4
    width = small.shape[1]

    def rows(array):
        return pl.BlockSpec((array.shape[0] // steps, array.shape[1]), lambda n: (n, 0))

    def whole(*shape):
        return pl.BlockSpec(shape, lambda n: (0,) * len(shape))

    small_shapes = [(1, 128), (experts, width)] + 4 * [(width,)]
    return pl.pallas_call(
        functools.partial(finish_kernel, experts),
        grid=(steps,),
        out_shape=[jax.ShapeDtypeStruct(shape, F32) for shape in small_shapes]
        + [jax.ShapeDtypeStruct(a.shape, kind) for a, kind in zip(narrow, kinds)],
        in_specs=[whole(*small.shape)] + [rows(a) for a in narrow],
        out_specs=[whole(*shape) for shape in small_shapes] + [rows(a) for a in narrow],
        compiler_params=pltpu.CompilerParams(vmem_limit_bytes=VMEM_BYTES),
        cost_estimate=pl.CostEstimate(flops=0, bytes_accessed=24 << 20, transcendentals=0),
        name="finish",
    )(small, *narrow)


def shards(
    tokens,
    output_grad,
    expert_index,
    query_weight,
    key_weight,
    value_weight,
    output_weight,
    router_weight,
    expert_in,
    expert_out,
    norm1_gain,
    norm1_bias,
    norm2_gain,
    norm2_bias,
):
    seqs, span, width = tokens.shape
    rows = seqs * span
    nb, ne = lax.axis_size("blk"), lax.axis_size("exp")
    length = span * nb
    experts = router_weight.shape[1]
    ff = expert_in.shape[2]
    cap = -(-max(2, rows * 5 // (4 * experts)) // 16) * 16
    slots = experts * cap
    token_total = rows * nb * ne
    half_width = width // 2
    cfg = dict(
        seqs=seqs, span=span, width=width, rows=rows, nb=nb, ne=ne, length=length,
        experts=experts, ff=ff, cap=cap, half_width=half_width, tokens=token_total,
        mean_load=token_total / experts,
    )
    dma = pltpu.SemaphoreType.DMA
    vmem = pltpu.VMEM
    hi = nb // 2
    size = ff // nb
    sum_rows = -(-(3 + experts) // 8) * 8
    cfg["sum_here"] = width % (8 * nb * ne) == 0
    paired = cfg["paired"] = cfg["sum_here"] and size == width and hi == 2 and slots <= width
    outer = width // min(nb, ne // 2)
    inner = width // (nb * ne // 2)
    inputs = (
        ("idx", expert_index.reshape(1, rows), True),
        ("router", router_weight.T, True),
        ("gain1", norm1_gain, True),
        ("bias1", norm1_bias, True),
        ("gain2", norm2_gain, True),
        ("bias2", norm2_bias, True),
        ("x_hbm", tokens.reshape(rows, width), False),
        ("og_hbm", output_grad.reshape(rows, width), False),
        ("wo_hbm", output_weight, False),
        ("win_hbm", expert_in.reshape(width, ff), False),
        ("wout_hbm", expert_out.reshape(ff, width), False),
        ("wq_hbm", query_weight, False),
        ("wk_hbm", key_weight, False),
        ("wv_hbm", value_weight, False),
    )
    small_rows = -(-(6 + experts) // 8) * 8
    outputs = [
        ("out", (rows, width), BF16, True),
        ("dx", (rows, width), BF16, True),
        ("small", (small_rows, width), F32, True),
        ("dwin", (width, size), F32, False),
        ("dwout", (size, width), F32, False),
    ]
    if cfg["sum_here"]:
        outputs += [(n, (width, width), BF16, False) for n in ("gq", "gk", "gv", "go")]
    else:
        outputs.append(("own_part", (4, width, half_width), BF16, False))
    scratch = dict(
        win=vmem((width, ff // 2 if paired else ff), BF16),
        wout=vmem((ff // 2 if paired else ff, width), BF16),
        x=vmem((rows, width), BF16),
        og=vmem((rows, width), BF16),
        o=vmem((rows, width), BF16),
        wo=vmem((width, width), BF16),
        dh=vmem((slots, width), BF16),
        idx_col=vmem((rows, 128), F32),
        cnt=vmem((experts, 128), F32),
        cnt_exp=vmem((ne, experts, 128), F32),
        cnt_blk=vmem((nb, experts, 128), F32),
        q=vmem((length, half_width), BF16),
        k=vmem((length, half_width), BF16),
        v=vmem((length, half_width), BF16),
        a=vmem((length, width), BF16),
        lse=vmem((8, length), F32),
        w=vmem((half_width // PAIR, width, 3 * PAIR), BF16),
        h1=vmem((rows, width), F32),
        gate=vmem((rows, 1), F32),
        mass=vmem((1, experts), F32),
        mail=vmem((rows, width), BF16),
        disp=vmem((slots, width), BF16),
        took=vmem((slots, width), BF16),
        g=vmem((hi, slots, width) if paired else (slots, width), BF16),
        du=vmem((hi, slots, width) if paired else (slots, width), BF16),
        yf=vmem((max(slots, size), width), F32),
        made=vmem((length, width), F32),
        back=vmem((slots, width), BF16),
        dh1=vmem((rows, width), F32),
        do=vmem((length, half_width), BF16),
        ogot=vmem((width, half_width), BF16),
        dk_sum=vmem((length, PAIR), F32),
        dv_sum=vmem((length, PAIR), F32),
        dqkv=vmem((length, 3 * PAIR), BF16),
        sums=vmem((sum_rows, width), F32),
        sum_exp=vmem((ne, sum_rows, width), F32),
        sum_blk=vmem((nb, sum_rows, width), F32),
        late=vmem((8, FF_COLS), F32),
        late_exp=vmem((ne, 8, FF_COLS), F32),
        late_blk=vmem((nb, 8, FF_COLS), F32),
        part=vmem((4, width, half_width), BF16),
        lsem=dma((5 + 2 * hi + 3 * (half_width // PAIR),)),
        fsem=dma((6,)),
        xs=dma((2 * seqs,)), xr=dma((nb,)),
        fws=dma((nb,)), fwr=dma((nb,)),
        os=dma((nb,)), osr=dma((2 * seqs,)),
        ds=dma((ne,)), dr=dma((ne,)),
        ces=dma((ne,)), cer=dma((ne,)), cbs=dma((nb,)), cbr=dma((nb,)),
        ns=dma((ne,)), nr=dma((ne,)),
        rs=dma((ne,)), rr=dma((ne,)),
        ys=dma((ne,)), yr=dma((ne,)),
        dos=dma((2 * seqs,)), dor=dma((nb,)),
        ows=dma, owr=dma,
        ss=dma, sr=dma,
        fs=dma((nb,)), fr=dma((2 * seqs,)),
        es=dma((ne,)), er=dma((ne,)), bs=dma((nb,)), br=dma((nb,)),
        les=dma((ne,)), ler=dma((ne,)), lbs=dma((nb,)), lbr=dma((nb,)),
    )
    if cfg["sum_here"]:
        scratch.update(
            shared=vmem((4, width, width), BF16),
            got1=vmem((4, max(nb, ne // 2), outer, half_width), BF16),
            got2=vmem((4, max(nb, ne // 2), inner, half_width), BF16),
            s5=dma((4,)),
            r5=dma((4,)),
        )
        for n in range(1, 5):
            scratch[f"s{n}"] = dma((4, max(nb, ne // 2)))
            scratch[f"r{n}"] = dma((4, max(nb, ne // 2)))
    if paired:
        scratch.update(
            {n: vmem((slots, width), BF16) for n in ("took2", "dh2", "dy", "dy2", "dn2", "dn_got", "y2", "y_got")},
            **{n: vmem((slots, 1), F32) for n in ("value", "dgate", "dgate2")},
            dg_send=vmem((8, slots), F32),
            dg_got=vmem((8, slots), F32),
            in_got=vmem((hi - 1, width, size), BF16),
            out_got=vmem((hi - 1, size, width), BF16),
            ins=dma((hi - 1,)), inr=dma((hi - 1,)),
            outs=dma((hi - 1,)), outr=dma((hi - 1,)),
            t2s=dma((ne,)), t2r=dma((ne,)),
            g2s=dma((ne,)), g2r=dma((ne,)),
            d2s=dma((ne,)), d2r=dma((ne,)),
            **{n: dma for n in ("dgs", "dgr")},
            y2s=dma((2,)), y2r=dma((2,)),
        )
    else:
        scratch.update(
            in1=vmem((hi, width, size), BF16),
            in2=vmem((hi - 1, width, size), BF16),
            out1=vmem((hi - 1, 2, size, width), BF16),
            out2=vmem((size, width), BF16),
            in1s=dma((hi,)), in1r=dma((hi,)),
            in2s=dma((hi - 1,)), in2r=dma((hi - 1,)),
            out1s=dma((hi - 1, 2)), out1r=dma((hi - 1, 2)),
            out2s=dma, out2r=dma,
        )
    names = [n for n, _, _ in inputs] + [n for n, _, _, _ in outputs] + list(scratch)
    out, dx, small, dwin, dwout, *wide = pl.pallas_call(
        functools.partial(layer_kernel, cfg, names),
        out_shape=[jax.ShapeDtypeStruct(shape, kind) for _, shape, kind, _ in outputs],
        in_specs=[(in_vmem if near else anywhere)(1)[0] for _, _, near in inputs],
        out_specs=[(in_vmem if near else anywhere)(1)[0] for _, _, _, near in outputs],
        scratch_shapes=list(scratch.values()),
        compiler_params=pltpu.CompilerParams(
            collective_id=1, has_side_effects=True, vmem_limit_bytes=VMEM_BYTES
        ),
        cost_estimate=pl.CostEstimate(
            flops=30 << 30, bytes_accessed=1 << 25, transcendentals=1 << 23
        ),
        name="layer",
    )(*[value for _, value, _ in inputs])
    if not cfg["sum_here"]:
        own = wide[0]
        own = jnp.concatenate(
            [
                own[:3].reshape(3, width, 3, PAIR).transpose(2, 1, 0, 3).reshape(3, width, half_width),
                own[3:],
            ]
        )
        core, empty = lax.rem(lax.axis_index("exp"), 2), jnp.zeros_like(own)
        wide = lax.psum(
            jnp.concatenate(
                [jnp.where(core == 0, own, empty), jnp.where(core == 0, empty, own)], axis=2
            ),
            ("blk", "exp"),
        )
    arrays = [out, dx, dwin, dwout, *[wide[n] for n in range(4)]]
    balance, router, gain1, bias1, gain2, bias2, out, dx, dwin, dwout, *wide = finish(
        experts, small, arrays, [BF16, BF16] + [F32] * 6
    )
    return (
        out.reshape(seqs, span, width),
        balance[0, 0],
        dx.reshape(seqs, span, width),
        *wide,
        router.T,
        dwin[None],
        dwout[None],
        gain1,
        bias1,
        gain2,
        bias2,
    )


def solution(mesh):
    return jax.shard_map(
        shards,
        mesh=mesh,
        in_specs=(
            P("exp", "blk", None),
            P("exp", "blk", None),
            P("blk", "exp", None, None),
            P(),
            P(),
            P(),
            P(),
            P(),
            P("exp", None, None),
            P("exp", None, None),
            P(),
            P(),
            P(),
            P(),
        ),
        out_specs=(
            P("exp", "blk", None),
            P(),
            P("exp", "blk", None),
            P(),
            P(),
            P(),
            P(),
            P(),
            P("exp", None, "blk"),
            P("exp", "blk", None),
            P(),
            P(),
            P(),
            P(),
        ),
        check_vma=False,
    )
```

```python
import functools

import jax
import jax.numpy as jnp
from jax import lax
from jax.experimental import pallas as pl
from jax.experimental.pallas import tpu as pltpu
from jax.sharding import PartitionSpec as P

HEAD_DIM = 64
PAIR = 2 * HEAD_DIM
EPSILON = 1e-05
SCALE = HEAD_DIM ** (-0.5)
QUERY_ROWS = 256
ROWS = 128
FF_COLS = 256
MESH = pl.DeviceIdType.MESH
BF16, F32 = jnp.bfloat16, jnp.float32
BLK_FIRST = (0, 1, 2)
PLAN = {
    "start": ((3, 1),),
    0: ((0, 1),),
    1: ((1, 1),),
    2: ((2, 1), (0, 2)),
    "rows sent": ((1, 2), (2, 2), (0, 3), (3, 2), (1, 3), (0, 4), (2, 3), (3, 3)),
    "rows done": ((1, 4), (2, 4), (3, 4)),
    "late": ((0, 5), (1, 5)),
    "last": ((2, 5), (3, 5)),
}
VMEM_BYTES = 255 << 18
NT = (((1,), (1,)), ((), ()))
TN = (((0,), (0,)), ((), ()))


def dot(left, right, dims=(((1,), (0,)), ((), ()))):
    return lax.dot_general(left, right, dims, preferred_element_type=F32)


def iota(shape, dim):
    return lax.broadcasted_iota(jnp.int32, shape, dim)


def normalize(values):
    centered = values - jnp.mean(values, axis=-1, keepdims=True)
    variance = jnp.mean(centered * centered, axis=-1, keepdims=True)
    inverse = lax.rsqrt(variance + EPSILON)
    return centered * inverse, inverse


def norm_back(hat, inverse, gain, grad):
    scaled = grad * gain
    return inverse * (
        scaled
        - jnp.mean(scaled, axis=-1, keepdims=True)
        - hat * jnp.mean(scaled * hat, axis=-1, keepdims=True)
    )


def split_rows(base, size):
    return pl.ds(pl.multiple_of(base, size), size)


class Place:
    def __init__(self, cfg):
        self.__dict__.update(cfg)
        self.b = lax.axis_index("blk")
        self.e = lax.axis_index("exp")
        self.c = lax.rem(self.e, 2)
        self.pair = self.e - self.c
        self.sibling = self.pair + 1 - self.c

    def greet(self):
        bar = pltpu.get_barrier_semaphore()

        def exp_peer(k, _):
            pl.semaphore_signal(
                bar, 1, device_id=(self.b, lax.rem(self.e + k, self.ne)), device_id_type=MESH
            )

        def blk_peer(k, _):
            there = lax.rem(self.b + k, self.nb)
            pl.semaphore_signal(bar, 1, device_id=(there, self.e), device_id_type=MESH)
            pl.semaphore_signal(bar, 1, device_id=(there, self.sibling), device_id_type=MESH)

        lax.fori_loop(1, self.ne, exp_peer, None)
        lax.fori_loop(1, self.nb, blk_peer, None)
        pl.semaphore_wait(bar, self.ne - 1 + 2 * (self.nb - 1))

    def is_me(self, there):
        return there[0] * self.ne + there[1] == self.b * self.ne + self.e


def remote(src, dst, send_sem, recv_sem, there):
    return pltpu.make_async_remote_copy(
        src, dst, send_sem, recv_sem, device_id=there, device_id_type=MESH
    )


def push(me, src, dst, send_sem, recv_sem, there):
    mine = me.is_me(there)

    @pl.when(mine)
    def _():
        pltpu.make_async_copy(src, dst, recv_sem).start()

    @pl.when(jnp.logical_not(mine))
    def _():
        remote(src, dst, send_sem, recv_sem, there).start()


def push_done(me, src, dst, send_sem, recv_sem, there):
    @pl.when(jnp.logical_not(me.is_me(there)))
    def _():
        remote(src, dst, send_sem, recv_sem, there).wait_send()


def landed(dst, recv_sem):
    pltpu.make_async_copy(dst, dst, recv_sem).wait()


def exp_peer(me, k, sign):
    near = me.ne // 2
    place = lax.rem(me.e, near)
    base = lax.rem(me.e - place + near * lax.div(k, near), me.ne)
    return base + lax.rem(place + near + sign * lax.rem(k, near), near)


def turned(me, k):
    return lax.rem(k + me.ne // 2, me.ne)


def exchange_move(me, src, dst, send_sem, recv_sem, size, k):
    there = exp_peer(me, k, 1)
    return remote(
        src.at[split_rows(there * size, size)],
        dst.at[split_rows(me.e * size, size)],
        send_sem.at[k],
        recv_sem.at[k],
        (me.b, there),
    )


def exchange_start(me, src, dst, send_sem, recv_sem, size, ahead=None):
    own = split_rows(me.e * size, size)

    def one(k, _):
        if ahead:
            k = turned(me, k)
            ahead(k, split_rows(exp_peer(me, k, 1) * size, size))
        exchange_move(me, src, dst, send_sem, recv_sem, size, k).start()

    if ahead:
        lax.fori_loop(0, me.ne // 2, one, None)
        ahead(0, own)
    pltpu.make_async_copy(src.at[own], dst.at[own], recv_sem.at[0]).start()
    lax.fori_loop(me.ne // 2 + 1 if ahead else 1, me.ne, one, None)


def exchange_wait(me, src, dst, send_sem, recv_sem, size):
    own = split_rows(me.e * size, size)
    landed(dst.at[own], recv_sem.at[0])

    def one(k, _):
        rows = split_rows(exp_peer(me, k, -1) * size, size)
        landed(dst.at[rows], recv_sem.at[k])

    lax.fori_loop(1, me.ne, one, None)


def exchange_sent(me, src, dst, send_sem, recv_sem, size):
    def one(k, _):
        exchange_move(me, src, dst, send_sem, recv_sem, size, k).wait_send()

    lax.fori_loop(1, me.ne, one, None)


def token_slots(me, idx):
    rows = idx.shape[1]
    hot = (iota((128, rows), 0) == idx).astype(F32)
    earlier = (iota((rows, rows), 0) < iota((rows, rows), 1)).astype(F32).astype(BF16)
    ahead = dot(hot.astype(BF16), earlier)
    slot = jnp.sum(ahead * hot, axis=0, keepdims=True).astype(jnp.int32) + idx * me.cap
    return slot, jnp.sum(hot, axis=1, keepdims=True)[0 : me.experts]


def slots_by_token(me, slot):
    shape = (me.experts * me.cap, slot.shape[1])
    return (iota(shape, 0) == slot).astype(F32).astype(BF16)


def head_masks():
    lane = iota((1, PAIR), 1)
    first = (lane < HEAD_DIM).astype(F32).astype(BF16)
    second = (lane >= HEAD_DIM).astype(F32).astype(BF16)
    return first, second


def gelu_parts(u):
    root = 0.7978845608028654
    cubic = 0.044715
    square = u * u
    t = jnp.tanh(root * u * (1.0 + cubic * square))
    value = 0.5 * u * (1.0 + t)
    slope = 0.5 * (1.0 + t) + (0.5 * root) * u * (1.0 - t * t) * (1.0 + 3.0 * cubic * square)
    return value, slope


class Refs:
    def __init__(self, names, refs):
        self.__dict__.update(zip(names, refs, strict=True))


class ExpertSums:
    def __init__(self, me, r):
        self.me, self.r = me, r
        self.hi, self.lo = lax.div(me.b, 2), lax.rem(me.b, 2)
        self.other = 1 - self.lo
        self.count = me.nb // 2
        self.size = me.ff // me.nb

    def turn(self, step):
        return lax.rem(self.hi + step, self.count)

    def span(self, hi, lo):
        return pl.ds(pl.multiple_of((2 * hi + lo) * self.size, 128), self.size)

    def in_first(self, hi):
        r = self.r
        there = (2 * self.hi + self.other, self.me.e)
        return remote(
            r.win.at[:, self.span(hi, self.other)], r.in1.at[hi], r.in1s.at[hi], r.in1r.at[hi], there
        )

    def in_second(self, step):
        r, hi = self.r, self.turn(step)
        return remote(
            r.win.at[:, self.span(hi, self.lo)],
            r.in2.at[step - 1],
            r.in2s.at[step - 1],
            r.in2r.at[step - 1],
            (2 * hi + self.lo, self.me.e),
        )

    def out_first(self, step, lo):
        r, hi = self.r, self.turn(step)
        return remote(
            r.wout.at[self.span(hi, lo)],
            r.out1.at[step - 1, lo],
            r.out1s.at[step - 1, lo],
            r.out1r.at[step - 1, lo],
            (2 * hi + self.lo, self.me.e),
        )

    def out_second(self):
        r = self.r
        return remote(
            r.wout.at[self.span(self.hi, self.other)],
            r.out2,
            r.out2s,
            r.out2r,
            (2 * self.hi + self.other, self.me.e),
        )

    def after_part(self, n):
        step = lax.div(n, 2) + 1
        lo = lax.rem(self.other + n, 2)

        @pl.when(lax.rem(n, 2) == 0)
        def _():
            self.in_first(self.turn(step)).start()

        @pl.when(step < self.count)
        def _():
            self.out_first(step, lo).start()

    def second_add(self):
        r = self.r
        for step in range(1, self.count):
            hi = self.turn(step)
            landed(r.in1.at[hi], r.in1r.at[hi])
            here = self.span(hi, self.lo)

            def in_rows(n, _, hi=hi, here=here):
                rows = split_rows(n * ROWS, ROWS)
                r.win[rows, here] = (
                    r.win[rows, here].astype(F32) + r.in1[hi, rows, :].astype(F32)
                ).astype(BF16)

            lax.fori_loop(0, self.me.width // ROWS, in_rows, None)
        for step in range(1, self.count):
            landed(r.out1.at[step - 1, self.other], r.out1r.at[step - 1, self.other])
        base = (2 * self.hi + self.other) * self.size

        def out_rows(n, _):
            here, rows = split_rows(base + n * ROWS, ROWS), split_rows(n * ROWS, ROWS)
            total = r.wout[here, :].astype(F32)
            for step in range(1, self.count):
                total += r.out1[step - 1, self.other, rows, :].astype(F32)
            r.wout[here, :] = total.astype(BF16)

        lax.fori_loop(0, self.size // ROWS, out_rows, None)

    def second_send(self):
        for step in range(1, self.count):
            self.in_second(step).start()
        self.out_second().start()

    def total_in(self):
        r = self.r
        landed(r.in1.at[self.hi], r.in1r.at[self.hi])
        for step in range(1, self.count):
            landed(r.in2.at[step - 1], r.in2r.at[step - 1])

        def in_rows(n, _):
            rows = split_rows(n * ROWS, ROWS)
            total = r.win[rows, self.span(self.hi, self.lo)].astype(F32)
            total += r.in1[self.hi, rows, :].astype(F32)
            for step in range(1, self.count):
                total += r.in2[step - 1, rows, :].astype(F32)
            r.win[rows, self.span(self.hi, self.lo)] = total.astype(BF16)

        lax.fori_loop(0, self.me.width // ROWS, in_rows, None)
        return r.win.at[:, self.span(self.hi, self.lo)]

    def total_out(self):
        r = self.r
        for step in range(1, self.count):
            landed(r.out1.at[step - 1, self.lo], r.out1r.at[step - 1, self.lo])
        landed(r.out2, r.out2r)
        base = (2 * self.hi + self.lo) * self.size

        def out_rows(n, _):
            rows = split_rows(n * ROWS, ROWS)
            own = split_rows(base + n * ROWS, ROWS)
            total = r.wout[own, :].astype(F32)
            for step in range(1, self.count):
                total += r.out1[step - 1, self.lo, rows, :].astype(F32)
            r.wout[own, :] = (total + r.out2[rows, :].astype(F32)).astype(BF16)

        lax.fori_loop(0, self.size // ROWS, out_rows, None)
        return r.wout.at[self.span(self.hi, self.lo)]

    def sent(self):
        for step in range(1, self.count + 1):
            self.in_first(self.turn(step)).wait_send()
            if step < self.count:
                self.in_second(step).wait_send()
                for lo in range(2):
                    self.out_first(step, lo).wait_send()
        self.out_second().wait_send()


class PairSums:
    def __init__(self, me, r):
        self.me, self.r = me, r
        self.hi, self.lo = lax.div(me.b, 2), lax.rem(me.b, 2)
        self.count = me.nb // 2
        self.size = me.ff // me.nb
        self.partner = (2 * self.hi + 1 - self.lo, me.e)

    def turn(self, step):
        return lax.rem(self.hi + step, self.count)

    def place(self, hi):
        return split_rows(hi * self.size, self.size)

    def owner(self, step):
        return (2 * self.turn(step) + self.lo, self.me.e)

    def in_move(self, step):
        r, k = self.r, step - 1
        src = r.win.at[:, self.place(self.turn(step))]
        return remote(src, r.in_got.at[k], r.ins.at[k], r.inr.at[k], self.owner(step))

    def out_move(self, step):
        r, k = self.r, step - 1
        src = r.wout.at[self.place(self.turn(step))]
        return remote(src, r.out_got.at[k], r.outs.at[k], r.outr.at[k], self.owner(step))

    def second_send(self):
        for step in range(1, self.count):
            self.out_move(step).start()

    def total_in(self):
        r = self.r
        for step in range(1, self.count):
            landed(r.in_got.at[step - 1], r.inr.at[step - 1])

        def in_rows(n, _):
            rows = split_rows(n * ROWS, ROWS)
            total = r.win[rows, self.place(self.hi)].astype(F32)
            for step in range(1, self.count):
                total += r.in_got[step - 1, rows, :].astype(F32)
            r.win[rows, self.place(self.hi)] = total.astype(BF16)

        lax.fori_loop(0, self.me.width // ROWS, in_rows, None)
        return r.win.at[:, self.place(self.hi)]

    def total_out(self):
        r = self.r
        for step in range(1, self.count):
            landed(r.out_got.at[step - 1], r.outr.at[step - 1])

        def out_rows(n, _):
            rows = split_rows(n * ROWS, ROWS)
            own = split_rows(self.hi * self.size + n * ROWS, ROWS)
            total = r.wout[own, :].astype(F32)
            for step in range(1, self.count):
                total += r.out_got[step - 1, rows, :].astype(F32)
            r.wout[own, :] = total.astype(BF16)

        lax.fori_loop(0, self.size // ROWS, out_rows, None)
        return r.wout.at[self.place(self.hi)]

    def sent(self):
        for step in range(1, self.count):
            self.in_move(step).wait_send()
            self.out_move(step).wait_send()


class SharedSum:
    def __init__(self, me, r, p, blk_first):
        self.me, self.r, self.p = me, r, p
        z = lax.div(me.e, 2)
        nz = me.ne // 2
        blk = (me.b, me.nb, lambda t: (t, me.e))
        along_z = (z, nz, lambda t: (me.b, 2 * t + me.c))
        self.first, self.second = (blk, along_z) if blk_first else (along_z, blk)
        self.outer = me.width // self.first[1]
        self.inner = self.outer // self.second[1]

    def outer_rows(self, t):
        return split_rows(t * self.outer, self.outer)

    def inner_rows(self, t, s):
        return split_rows(t * self.outer + s * self.inner, self.inner)

    def view(self, rows, core):
        me, r, p = self.me, self.r, self.p
        if p < 3:
            return r.shared.at[
                pl.ds(0, 3), rows, pl.ds(pl.multiple_of(core * me.half_width + p * PAIR, PAIR), PAIR)
            ]
        return r.shared.at[
            3, rows, pl.ds(pl.multiple_of(core * me.half_width, PAIR), me.half_width)
        ]

    def peer(self, axis, k):
        return lax.rem(axis[0] + k, axis[1])

    def source(self, axis, k):
        return lax.rem(axis[0] + axis[1] - k, axis[1])

    def move1(self, k):
        r, p = self.r, self.p
        t = self.peer(self.first, k)
        return remote(
            r.part.at[p, self.outer_rows(t)],
            r.got1.at[p, k, pl.ds(0, self.outer)],
            r.s1.at[p, k],
            r.r1.at[p, k],
            self.first[2](t),
        )

    def move2(self, k):
        r, p = self.r, self.p
        t = self.peer(self.second, k)
        return remote(
            r.got1.at[p, 0, split_rows(t * self.inner, self.inner)],
            r.got2.at[p, k],
            r.s2.at[p, k],
            r.r2.at[p, k],
            self.second[2](t),
        )

    def move3(self, k):
        r, p = self.r, self.p
        here = self.view(self.inner_rows(self.first[0], self.second[0]), self.me.c)
        return remote(
            here, here, r.s3.at[p, k], r.r3.at[p, k], self.second[2](self.peer(self.second, k))
        )

    def move4(self, k):
        r, p = self.r, self.p
        here = self.view(self.outer_rows(self.first[0]), self.me.c)
        return remote(
            here, here, r.s4.at[p, k], r.r4.at[p, k], self.first[2](self.peer(self.first, k))
        )

    def move5(self):
        r, p = self.r, self.p
        here = self.view(pl.ds(0, self.me.width), self.me.c)
        return remote(here, here, r.s5.at[p], r.r5.at[p], (self.me.b, self.me.sibling))

    def stage1(self):
        for k in range(1, self.first[1]):
            self.move1(k).start()

    def stage2(self):
        r, p = self.r, self.p
        total = r.part[p, self.outer_rows(self.first[0])].astype(F32)
        for k in range(1, self.first[1]):
            here = r.got1.at[p, k, pl.ds(0, self.outer)]
            landed(here, r.r1.at[p, k])
            total += here[...].astype(F32)
        r.got1[p, 0, 0 : self.outer, :] = total.astype(BF16)
        for k in range(1, self.second[1]):
            self.move2(k).start()

    def stage3(self):
        r, p = self.r, self.p
        total = r.got1[p, 0, split_rows(self.second[0] * self.inner, self.inner)].astype(F32)
        for k in range(1, self.second[1]):
            landed(r.got2.at[p, k], r.r2.at[p, k])
            total += r.got2[p, k].astype(F32)
        total = total.astype(BF16)
        here = self.view(self.inner_rows(self.first[0], self.second[0]), self.me.c)
        if p < 3:
            for j in range(3):
                here[j] = total[:, j * PAIR : (j + 1) * PAIR]
        else:
            here[...] = total
        for k in range(1, self.second[1]):
            self.move3(k).start()

    def stage4(self):
        for k in range(1, self.second[1]):
            rows = self.inner_rows(self.first[0], self.source(self.second, k))
            landed(self.view(rows, self.me.c), self.r.r3.at[self.p, k])
        for k in range(1, self.first[1]):
            self.move4(k).start()

    def stage5(self):
        for k in range(1, self.first[1]):
            rows = self.outer_rows(self.source(self.first, k))
            landed(self.view(rows, self.me.c), self.r.r4.at[self.p, k])
        self.move5().start()

    def end(self):
        landed(self.view(pl.ds(0, self.me.width), 1 - self.me.c), self.r.r5.at[self.p])
        for k in range(1, self.first[1]):
            self.move1(k).wait_send()
            self.move4(k).wait_send()
        for k in range(1, self.second[1]):
            self.move2(k).wait_send()
            self.move3(k).wait_send()
        self.move5().wait_send()


class AllSum:
    def __init__(self, me, own, by_exp, by_blk, sems):
        self.me, self.own, self.by_exp, self.by_blk = me, own, by_exp, by_blk
        self.es, self.er, self.bs, self.br = sems

    def exp_move(self, k):
        me = self.me
        there = (me.b, lax.rem(me.e + k, me.ne))
        return remote(self.own, self.by_exp.at[me.e], self.es.at[k], self.er.at[k], there)

    def blk_move(self, k):
        me = self.me
        here = self.by_blk.at[me.b]
        there = (lax.rem(me.b + k, me.nb), me.e)
        return remote(here, here, self.bs.at[k], self.br.at[k], there)

    def start(self):
        lax.fori_loop(1, self.me.ne, lambda k, _: self.exp_move(k).start(), None)
        self.by_exp[self.me.e] = self.own[...]

    def middle(self):
        me = self.me

        def arrived(k, _):
            landed(self.by_exp.at[lax.rem(me.e + me.ne - k, me.ne)], self.er.at[k])

        lax.fori_loop(1, me.ne, arrived, None)
        self.by_blk[me.b] = jnp.sum(self.by_exp[...], axis=0)
        for k in range(1, me.nb):
            self.blk_move(k).start()

    def total(self):
        me = self.me
        for k in range(1, me.nb):
            landed(self.by_blk.at[lax.rem(me.b + me.nb - k, me.nb)], self.br.at[k])
        return jnp.sum(self.by_blk[...], axis=0)

    def sent(self):
        lax.fori_loop(1, self.me.ne, lambda k, _: self.exp_move(k).wait_send(), None)
        for k in range(1, self.me.nb):
            self.blk_move(k).wait_send()


def layer_kernel(cfg, names, *refs):
    me = Place(cfg)
    r = Refs(names, refs)
    half = me.span // 2
    pairs = me.half_width // PAIR
    blocks = me.length // QUERY_ROWS
    slots = me.experts * me.cap
    roomy = slots * me.width <= 1 << 19
    model_tile = me.width if roomy else FF_COLS
    early_g = r.g.at[0] if me.paired else r.g
    r.ysend, r.yback = early_g, r.dh2 if me.paired else r.du
    r.swap, r.da_in = r.took.at[pl.ds(0, me.rows)], r.back.at[pl.ds(0, me.rows)]
    r.xin, r.o_send, r.lse_cols, r.dh_send = r.mail, early_g, r.dk_sum, r.disp
    gain1, bias1, gain2, bias2 = (
        v[...].reshape(1, me.width) for v in (r.gain1, r.bias1, r.gain2, r.bias2)
    )
    loads = {}
    sums = PairSums(me, r) if me.paired else ExpertSums(me, r)
    whole = ("x", "og", "wo") if me.paired else ("x", "og", "wo", "win", "wout")
    for name in whole:
        loads[name] = pltpu.make_async_copy(
            getattr(r, name + "_hbm"), getattr(r, name), r.lsem.at[len(loads)]
        )
    for p in range(pairs):
        for j, matrix in enumerate((r.wq_hbm, r.wk_hbm, r.wv_hbm)):
            src = matrix.at[:, pl.ds(pl.multiple_of(me.c * me.half_width + p * PAIR, PAIR), PAIR)]
            loads["w", p, j] = pltpu.make_async_copy(
                src, r.w.at[p, :, pl.ds(j * PAIR, PAIR)], r.lsem.at[len(loads)]
            )
    for h in range(sums.count) if me.paired else ():
        part = pl.ds(pl.multiple_of((2 * h + sums.lo) * sums.size, 128), sums.size)
        place = pl.ds(h * sums.size, sums.size)
        loads["win", h] = pltpu.make_async_copy(
            r.win_hbm.at[:, part], r.win.at[:, place], r.lsem.at[len(loads)]
        )
        loads["wout", h] = pltpu.make_async_copy(
            r.wout_hbm.at[part], r.wout.at[place], r.lsem.at[len(loads)]
        )
    for load in loads.values():
        load.start()
    me.greet()

    def row_moves():
        for s in range(me.seqs):
            for h in range(2):
                yield (
                    r.x_hbm.at[pl.ds(s * me.span + h * half, half)],
                    r.xin.at[split_rows(me.b * half, half)],
                    r.xs.at[2 * s + h],
                    r.xr.at[me.b],
                    (me.c * me.seqs + s, me.pair + h),
                )

    for move in row_moves():
        push(me, *move)

    slot, counts = token_slots(me, r.idx[...])
    r.cnt[...] = jnp.broadcast_to(counts, r.cnt.shape)
    count_sum = AllSum(me, r.cnt, r.cnt_exp, r.cnt_blk, (r.ces, r.cer, r.cbs, r.cbr))
    count_sum.start()
    r.idx_col[...] = jnp.transpose(
        jnp.broadcast_to(r.idx[...].astype(F32), (128, me.rows))
    )
    loads["og"].wait()
    r.dh_send[...] = dot(slots_by_token(me, slot), r.og[...]).astype(BF16)
    exchange_start(me, r.dh_send, r.dh, r.ds, r.dr, me.cap)

    def forward_move(j):
        rows = split_rows(j * me.span + me.c * half, half)
        return remote(r.a.at[rows], r.a.at[rows], r.fws.at[j], r.fwr.at[j], (me.b, me.sibling))

    for j in range(me.nb):
        landed(r.xin.at[pl.ds(j * half, half)], r.xr.at[j])
        hat, _ = normalize(r.xin[pl.ds(j * half, half), :].astype(F32))
        r.a[split_rows(j * me.span + me.c * half, half), :] = (hat * gain1 + bias1).astype(BF16)
        forward_move(j).start()

    for p in range(pairs):
        for j in range(3):
            loads["w", p, j].wait()
    first, second = head_masks()
    spans = QUERY_ROWS // me.span
    lane = iota((1, PAIR), 1)
    visible = iota((QUERY_ROWS, QUERY_ROWS), 1) <= iota((QUERY_ROWS, QUERY_ROWS), 0)
    home = me.pair + lax.div(me.b, me.seqs)
    columns = pl.ds(pl.multiple_of(me.c * me.half_width, PAIR), me.half_width)

    def o_move(j):
        return (
            r.o_send.at[
                pl.ds(j * me.span % me.rows, me.span),
                pl.ds(j * me.span // me.rows * me.half_width, me.half_width),
            ],
            r.o.at[split_rows(lax.rem(me.b, me.seqs) * me.span, me.span), columns],
            r.os.at[j],
            r.osr.at[2 * lax.rem(me.b, me.seqs) + me.c],
            (j, home),
        )

    def dh_slot(k):
        return split_rows(exp_peer(me, jnp.int32(k), -1) * me.cap, me.cap)

    def dh_move(k):
        rows = dh_slot(k)
        return remote(r.dh.at[rows], r.dh2.at[rows], r.d2s.at[k], r.d2r.at[k], sums.partner)

    def dh_arrived(k):
        landed(r.dh.at[dh_slot(k)], r.dr.at[k])
        if me.paired:
            dh_move(k).start()

    for i in range(blocks):
        for j in range(i * spans, (i + 1) * spans):
            theirs = split_rows(j * me.span + (1 - me.c) * half, half)
            landed(r.a.at[theirs], r.fwr.at[j])
        here = pl.ds(i * QUERY_ROWS, QUERY_ROWS)

        def pair_of_heads(p, _, i=i, here=here):
            lanes = split_rows(p * PAIR, PAIR)
            qkv = dot(r.a[here, :], r.w[p]).astype(BF16)
            queries = qkv[:, 0:PAIR] * jnp.asarray(SCALE, BF16)
            r.q[here, lanes] = queries
            r.k[here, lanes] = qkv[:, PAIR : 2 * PAIR]
            r.v[here, lanes] = qkv[:, 2 * PAIR : 3 * PAIR]
            parts = [pl.ds(i * QUERY_ROWS, QUERY_ROWS)]
            if i:
                parts.append(pl.ds(0, i * QUERY_ROWS))
            done = []
            for h, mask in enumerate((first, second)):
                masked = queries * mask
                scores = [dot(masked, r.k[part, lanes], NT) for part in parts]
                scores[0] = jnp.where(visible, scores[0], -1e30)
                peak = functools.reduce(
                    jnp.maximum, [jnp.max(s, axis=1, keepdims=True) for s in scores]
                )
                powers = [jnp.exp(s - peak) for s in scores]
                total = sum(jnp.sum(s, axis=1, keepdims=True) for s in powers)
                mixed = sum(
                    dot(s.astype(BF16), r.v[part, lanes]) for s, part in zip(powers, parts)
                )
                done.append(mixed / total)
                r.lse_cols[here, :] = jnp.where(
                    lane == 2 * p + h, peak + jnp.log(total), r.lse_cols[here, :]
                )
            base = i * QUERY_ROWS // me.rows * me.half_width
            r.o_send[
                pl.ds(i * QUERY_ROWS % me.rows, QUERY_ROWS),
                pl.ds(pl.multiple_of(base + p * PAIR, PAIR), PAIR),
            ] = jnp.where(lane < HEAD_DIM, done[0], done[1]).astype(BF16)

        lax.fori_loop(0, pairs, pair_of_heads, None)
        for j in range(i * spans, (i + 1) * spans):
            push(me, *o_move(j))
        if i == 0:
            count_sum.middle()
        for k in range(me.ne):
            if (i == blocks - 1) if not me.paired else (max(0, k + 1 - me.ne // 2) == i):
                dh_arrived(k)
    for k in range(me.ne // 2 + blocks - 1, me.ne) if me.paired else ():
        dh_arrived(k)
    r.lse[...] = jnp.transpose(r.lse_cols[...])[0:8, :]
    for j in range(me.nb):
        forward_move(j).wait_send()
        push_done(me, *o_move(j))
    for move in row_moves():
        push_done(me, *move)
    for name in ("x", "wo"):
        loads[name].wait()
    exchange_sent(me, r.dh_send, r.dh, r.ds, r.dr, me.cap)

    expert_lane = iota((ROWS, me.experts), 1)
    r.sums[...] = jnp.zeros_like(r.sums)
    r.mass[...] = jnp.zeros_like(r.mass)
    for s in range(me.seqs):
        for h in range(2):
            landed(
                r.o.at[pl.ds(s * me.span, me.span), pl.ds(h * me.half_width, me.half_width)],
                r.osr.at[2 * s + h],
            )

    def token_rows(n, _):
        here = split_rows(n * ROWS, ROWS)
        hidden = r.x[here, :].astype(F32) + dot(r.o[here, :], r.wo[...])
        r.h1[here, :] = hidden
        hat, _ = normalize(hidden)
        normed = (hat * gain2 + bias2).astype(BF16)
        r.mail[here, :] = normed
        logits = dot(normed, r.router[...], NT)
        hot = r.idx_col[here, 0 : me.experts].astype(jnp.int32) == expert_lane
        value = jax.nn.sigmoid(jnp.sum(jnp.where(hot, logits, 0.0), axis=1, keepdims=True))
        r.gate[here, :] = value
        r.mass[...] += jnp.sum(jnp.where(hot, value, 0.0), axis=0, keepdims=True)

    lax.fori_loop(0, me.rows // ROWS, token_rows, None)
    takes = slots_by_token(me, slot)
    r.disp[...] = dot(takes, r.mail[...]).astype(BF16)
    exchange_start(me, r.disp, r.took, r.ns, r.nr, me.cap)
    for key, load in loads.items():
        if key in ("win", "wout") or key[0] in ("win", "wout"):
            load.wait()

    def took_move(k, rows):
        return remote(r.took.at[rows], r.took2.at[rows], r.t2s.at[k], r.t2r.at[k], sums.partner)

    if not me.paired:
        exchange_wait(me, r.disp, r.took, r.ns, r.nr, me.cap)
        exchange_sent(me, r.disp, r.took, r.ns, r.nr, me.cap)

    lanes = iota((slots, me.experts), 1)

    def gate_of(rows, lanes):
        logits = dot(rows, r.router[...], NT)
        picked = jnp.sum(jnp.where(lanes == me.e, logits, 0.0), axis=1, keepdims=True)
        return jax.nn.sigmoid(picked)

    if not me.paired:
        value = gate_of(r.took[...], lanes)
        r.disp[...] = (value * r.dh[...].astype(F32)).astype(BF16)
        r.yf[0:slots, :] = jnp.zeros((slots, me.width), F32)
        r.made[...] = jnp.zeros_like(r.made)
    slot_rows = slots if roomy else slots // 4

    def expert_part(n, _):
        hi, lo = sums.turn(lax.div(n, 2) + 1), lax.rem(sums.other + n, 2)
        base = (2 * hi + lo) * sums.size

        def hidden_columns(f, _):
            here = pl.ds(pl.multiple_of(base + f * sums.tile, 128), sums.tile)
            there = pl.ds(pl.multiple_of(f * sums.tile, 128), sums.tile)

            def hidden_rows(n, _):
                rows = split_rows(n * slot_rows, slot_rows)
                act, slope = gelu_parts(dot(r.took[rows, :], r.win[:, here]))
                r.g[rows, there] = act.astype(BF16)
                r.du[rows, there] = (dot(r.disp[rows, :], r.wout[here, :], NT) * slope).astype(BF16)

            lax.fori_loop(0, slots // slot_rows, hidden_rows, None)

        lax.fori_loop(0, sums.size // sums.tile, hidden_columns, None)
        part = sums.span(hi, lo)


        def model_columns(f, _):
            here = split_rows(f * model_tile, model_tile)
            r.yf[0:slots, here] += dot(r.g[:, 0 : sums.size], r.wout[part, here])
            r.made[0:slots, here] += dot(r.du[:, 0 : sums.size], r.win[here, part], NT)

        lax.fori_loop(0, me.width // model_tile, model_columns, None)

        def weight_columns(f, _):
            here = pl.ds(pl.multiple_of(base + f * sums.tile, 128), sums.tile)
            there = pl.ds(pl.multiple_of(f * sums.tile, 128), sums.tile)
            r.win[:, here] = dot(r.took[...], r.du[:, there], TN).astype(BF16)
            r.wout[here, :] = dot(r.g[:, there], r.disp[...], TN).astype(BF16)

        lax.fori_loop(0, sums.size // sums.tile, weight_columns, None)
        sums.after_part(n)

    near = me.ne // 2
    half_slots = near * me.cap
    half_lanes = iota((half_slots, me.experts), 1)

    def products(took, dh, dy, act, back, rows):
        gates = gate_of(took[rows, :], half_lanes)
        dy[rows, :] = (gates * dh[rows, :].astype(F32)).astype(BF16)
        for h in range(sums.count):
            place = pl.ds(h * sums.size, sums.size)
            value, slope = gelu_parts(dot(took[rows, :], r.win[:, place]))
            act.at[h][rows, :] = value.astype(BF16)
            back.at[h][rows, :] = (dot(dy[rows, :], r.wout[place, :], NT) * slope).astype(BF16)
        places = [pl.ds(h * sums.size, sums.size) for h in range(sums.count)]
        made_y = sum(dot(act.at[h][rows, :], r.wout[place, :]) for h, place in enumerate(places))
        made_dn = sum(
            dot(back.at[h][rows, :], r.win[:, place], NT) for h, place in enumerate(places)
        )
        return gates, made_y, made_dn

    def dgate_rows(dh, y):
        return jnp.sum(dh.astype(F32) * y, axis=1, keepdims=True)

    def dn_move(k, rows):
        return remote(r.dn2.at[rows], r.dn_got.at[rows], r.g2s.at[k], r.g2r.at[k], sums.partner)

    def slot_rows_of(k):
        return split_rows(exp_peer(me, k, 1) * me.cap, me.cap)

    if me.paired:
        act2 = r.shared.at[pl.ds(0, sums.count), pl.ds(0, slots)]
        back2 = r.shared.at[pl.ds(sums.count, sums.count), pl.ds(0, slots)]

        def half_rows(n, _):
            def pass_on(k, _):
                rows = split_rows(exp_peer(me, k, -1) * me.cap, me.cap)
                landed(r.took.at[rows], r.nr.at[k])
                took_move(k, rows).start()

            def arrived(k, _):
                rows = split_rows(exp_peer(me, k, -1) * me.cap, me.cap)
                landed(r.dh2.at[rows], r.d2r.at[k])
                landed(r.took2.at[rows], r.t2r.at[k])

            lax.fori_loop(n * near, (n + 1) * near, pass_on, None)
            base = lax.rem(me.e - lax.rem(me.e, near) + n * near, me.ne)
            rows = pl.ds(pl.multiple_of(base * me.cap, half_slots), half_slots)
            gates, made_y, made_dn = products(r.took, r.dh, r.dy, r.g, r.du, rows)
            r.value[rows, :] = gates
            r.dgate[rows, :] = dgate_rows(r.dh[rows, :], made_y)
            r.yf[rows, :] = made_y
            r.made[rows, :] = made_dn
            lax.fori_loop(n * near, (n + 1) * near, arrived, None)
            _, made_y, made_dn = products(r.took2, r.dh2, r.dy2, act2, back2, rows)
            r.dgate2[rows, :] = dgate_rows(r.dh2[rows, :], made_y)
            r.y2[rows, :] = made_y.astype(BF16)
            r.dn2[rows, :] = made_dn.astype(BF16)

        lax.fori_loop(0, 2, half_rows, None)
        exchange_sent(me, r.disp, r.took, r.ns, r.nr, me.cap)
        r.dg_send[...] = jnp.transpose(jnp.broadcast_to(r.dgate2[...], (slots, 128)))[0:8, :]
        dg_move = remote(r.dg_send, r.dg_got, r.dgs, r.dgr, sums.partner)
        dg_move.start()

        def dn_start(n, _):
            k = turned(me, n)
            dn_move(k, slot_rows_of(k)).start()

        lax.fori_loop(0, me.ne, dn_start, None)

        def half_of(part):
            base = me.e - lax.rem(me.e, near) + (1 - part) * near
            return pl.ds(pl.multiple_of(lax.rem(base, me.ne) * me.cap, half_slots), half_slots)

        def y_move(part):
            rows = half_of(part)
            return remote(
                r.y2.at[rows], r.y_got.at[rows], r.y2s.at[part], r.y2r.at[part], sums.partner
            )

        y_move(0).start()

        def weight_part(hi):
            place = sums.place(hi)
            r.win[:, place] = (
                dot(r.took[...], r.du[hi], TN) + dot(r.took2[...], back2[hi], TN)
            ).astype(BF16)
            r.wout[place, :] = (
                dot(r.g[hi], r.dy[...], TN) + dot(act2[hi], r.dy2[...], TN)
            ).astype(BF16)

        for step in range(1, sums.count):
            weight_part(sums.turn(step))
            sums.in_move(step).start()
    else:
        sums.tile = sums.size
        lax.fori_loop(0, me.nb, expert_part, None)

    weights = (count_sum.total() - me.mean_load) / me.mean_load
    weight = jnp.sum(jnp.where(iota(weights.shape, 0) == me.e, weights, 0.0), axis=0, keepdims=True)
    weight = weight[:, 0:1]
    if me.paired:
        landed(r.dg_got, r.dgr)
        theirs = jnp.transpose(jnp.broadcast_to(r.dg_got[0:1, :], (128, slots)))[:, 0:1]
        dgate = r.dgate[...] + theirs + weight / me.tokens
        value = r.value[...]
    else:
        r.ysend[...] = r.yf[0:slots, :].astype(BF16)
        dgate = (
            jnp.sum(r.dh[...].astype(F32) * r.ysend[...].astype(F32), axis=1, keepdims=True)
            + weight / me.tokens
        )
    dlogits = jnp.where(lanes == me.e, dgate * value * (1.0 - value), 0.0).astype(BF16)
    if me.paired:
        r.made[0:slots, :] += dot(dlogits, r.router[...])

        def add_theirs(k, rows):
            landed(r.dn_got.at[rows], r.g2r.at[k])
            r.disp[rows, :] = (r.made[rows, :] + r.dn_got[rows, :].astype(F32)).astype(BF16)

        exchange_start(me, r.disp, r.back, r.rs, r.rr, me.cap, ahead=add_theirs)
        weight_part(sums.hi)
    else:
        r.disp[...] = (r.made[0:slots, :] + dot(dlogits, r.router[...])).astype(BF16)
        exchange_start(me, r.disp, r.back, r.rs, r.rr, me.cap)
    r.sums[2 : 2 + me.experts, :] = dot(dlogits, r.took[...], TN)
    r.sums[2 + me.experts : 3 + me.experts, 0 : me.experts] = r.mass[...]
    if not me.paired:
        sums.second_add()
    exchange_wait(me, r.disp, r.back, r.rs, r.rr, me.cap)

    r.made[0 : me.rows, :] = dot(takes, r.back[...], TN)

    def norm_rows(n, _):
        here = split_rows(n * ROWS, ROWS)
        grad = r.made[here, :]
        hat, inverse = normalize(r.h1[here, :])
        r.sums[0:1, :] += jnp.sum(grad * hat, axis=0, keepdims=True)
        r.sums[1:2, :] += jnp.sum(grad, axis=0, keepdims=True)
        total = r.og[here, :].astype(F32) + norm_back(hat, inverse, gain2, grad)
        r.dh1[here, :] = total
        r.mail[here, :] = dot(total.astype(BF16), r.wo[...], NT).astype(BF16)

    def do_moves(s):
        for h in range(2):
            yield (
                r.mail.at[pl.ds(s * me.span, me.span), pl.ds(h * me.half_width, me.half_width)],
                r.do.at[split_rows(me.b * me.span, me.span)],
                r.dos.at[2 * s + h],
                r.dor.at[me.b],
                (me.c * me.seqs + s, me.pair + h),
            )

    steps = me.span // ROWS
    for s in range(me.seqs):
        lax.fori_loop(s * steps, (s + 1) * steps, norm_rows, None)
        for move in do_moves(s):
            push(me, *move)
    sums.second_send()
    early = AllSum(me, r.sums, r.sum_exp, r.sum_blk, (r.es, r.er, r.bs, r.br))
    def y_home(part):
        rows = half_of(part)
        landed(r.y_got.at[rows], r.y2r.at[part])
        r.ysend[rows, :] = (r.yf[rows, :] + r.y_got[rows, :].astype(F32)).astype(BF16)

        def one(k, _):
            exchange_move(me, r.ysend, r.yback, r.ys, r.yr, me.cap, k).start()

        if part:
            own = split_rows(me.e * me.cap, me.cap)
            pltpu.make_async_copy(r.ysend.at[own], r.yback.at[own], r.yr.at[0]).start()
            lax.fori_loop(1, near, one, None)
        else:
            lax.fori_loop(near, me.ne, one, None)

    if me.paired:
        y_move(1).start()
        y_home(0)
        lax.fori_loop(
            0,
            me.ne,
            lambda k, _: took_move(k, split_rows(exp_peer(me, k, -1) * me.cap, me.cap)).wait_send(),
            None,
        )

    def output_columns(core):
        cols = pl.ds(pl.multiple_of(core * me.half_width, PAIR), me.half_width)
        return dot(r.o[...], r.dh1[:, cols].astype(BF16), TN)

    r.part[0] = output_columns(1 - me.c).astype(BF16)
    o_swap = remote(r.part.at[0], r.ogot, r.ows, r.owr, (me.b, me.sibling))
    o_swap.start()
    own_columns = output_columns(me.c)
    o_swap.wait()
    r.part[3] = (own_columns + r.ogot[...].astype(F32)).astype(BF16)
    pieces = [SharedSum(me, r, p, p in BLK_FIRST) for p in range(4)] if me.sum_here else []

    def advance(point):
        for p, stage in PLAN.get(point, ()) if pieces else ():
            getattr(pieces[p], f"stage{stage}")()

    advance("start")
    early.start()
    if not me.paired:
        exchange_start(me, r.ysend, r.yback, r.ys, r.yr, me.cap)

    r.made[...] = jnp.zeros_like(r.made)
    if me.paired:
        store_in = pltpu.make_async_copy(sums.total_in(), r.dwin, r.fsem.at[0])
        store_in.start()
    for j in range(me.nb):
        landed(r.do.at[pl.ds(j * me.span, me.span)], r.dor.at[j])
    visible = iota((QUERY_ROWS, QUERY_ROWS), 0) <= iota((QUERY_ROWS, QUERY_ROWS), 1)

    def pair_back(n, _):
        lanes = split_rows(n * PAIR, PAIR)
        r.dk_sum[...] = jnp.zeros_like(r.dk_sum)
        r.dv_sum[...] = jnp.zeros_like(r.dv_sum)
        for i in range(blocks):
            here = pl.ds(i * QUERY_ROWS, QUERY_ROWS)
            queries, grads = r.q[here, lanes], r.do[here, lanes]
            parts = [here]
            if i:
                parts.append(pl.ds(0, i * QUERY_ROWS))
            dq_block = jnp.zeros((QUERY_ROWS, PAIR), F32)
            for h, mask in enumerate((first, second)):
                qm, gm = queries * mask, grads * mask
                log_sums = r.lse[pl.ds(2 * n + h, 1), here]
                scores = [dot(r.k[part, lanes], qm, NT) for part in parts]
                powers = [jnp.exp(s - log_sums) for s in scores]
                powers[0] = jnp.where(visible, powers[0], 0.0)
                weighted = [
                    s * dot(r.v[part, lanes], gm, NT) for s, part in zip(powers, parts)
                ]
                delta = sum(jnp.sum(t, axis=0, keepdims=True) for t in weighted)
                for s, t, part in zip(powers, weighted, parts):
                    ds = (t - s * delta).astype(BF16)
                    r.dv_sum[part, :] += dot(s.astype(BF16), gm)
                    r.dk_sum[part, :] += dot(ds, qm)
                    dq_block += dot(ds, r.k[part, lanes] * mask, TN)
            r.dqkv[here, 0:PAIR] = (dq_block * SCALE).astype(BF16)
        r.dqkv[:, PAIR : 2 * PAIR] = r.dk_sum[...].astype(BF16)
        r.dqkv[:, 2 * PAIR : 3 * PAIR] = r.dv_sum[...].astype(BF16)
        r.part[n] = dot(r.a[...], r.dqkv[...], TN).astype(BF16)

        def normed_columns(f, _):
            cols = split_rows(f * model_tile, model_tile)
            r.made[:, cols] += dot(r.dqkv[...], r.w[n, cols, :], NT)

        lax.fori_loop(0, me.width // model_tile, normed_columns, None)
        for done in range(pairs):

            @pl.when(n == done)
            def _(done=done):
                if me.paired and done == 1:
                    y_home(1)
                advance(done)

    lax.fori_loop(0, pairs, pair_back, None)
    early.middle()

    for s in range(me.seqs):
        for move in do_moves(s):
            push_done(me, *move)
    for j in range(me.nb):
        theirs = split_rows(j * me.span + (1 - me.c) * half, half)
        r.mail[pl.ds(j * half, half), :] = r.made[theirs, :].astype(BF16)
    swap = remote(r.mail, r.swap, r.ss, r.sr, (me.b, me.sibling))
    swap.start()
    exchange_wait(me, r.ysend, r.yback, r.ys, r.yr, me.cap)
    r.yf[0 : me.rows, :] = dot(takes, r.yback[...], TN)

    def out_rows(n, _):
        here = split_rows(n * ROWS, ROWS)
        r.out[here, :] = (r.h1[here, :] + r.gate[here, :] * r.yf[here, :]).astype(BF16)

    lax.fori_loop(0, me.rows // ROWS, out_rows, None)
    swap.wait()
    def da_move(j):
        return (
            r.mail.at[pl.ds(j * half, half)],
            r.da_in.at[split_rows(lax.rem(me.b, me.seqs) * me.span + me.c * half, half)],
            r.fs.at[j],
            r.fr.at[2 * lax.rem(me.b, me.seqs) + me.c],
            (j, home),
        )

    for j in range(me.nb):
        mine = r.made[split_rows(j * me.span + me.c * half, half), :]
        rows = pl.ds(j * half, half)
        r.mail[rows, :] = (mine + r.swap[rows, :].astype(F32)).astype(BF16)
        push(me, *da_move(j))
    advance("rows sent")
    for s in range(me.seqs):
        for h in range(2):
            landed(r.da_in.at[pl.ds(s * me.span + h * half, half)], r.fr.at[2 * s + h])

    r.late[...] = jnp.zeros_like(r.late)
    tiles = me.width // FF_COLS

    def first_norm_rows(n, _):
        here = split_rows(n * ROWS, ROWS)
        grad = r.da_in[here, :].astype(F32)
        hat, inverse = normalize(r.x[here, :].astype(F32))
        gain_part = jnp.sum(grad * hat, axis=0, keepdims=True)
        bias_part = jnp.sum(grad, axis=0, keepdims=True)
        for j in range(tiles):
            cols = slice(j * FF_COLS, (j + 1) * FF_COLS)
            r.late[j : j + 1, :] += gain_part[:, cols]
            r.late[tiles + j : tiles + j + 1, :] += bias_part[:, cols]
        r.dx[here, :] = (r.dh1[here, :] + norm_back(hat, inverse, gain1, grad)).astype(BF16)

    lax.fori_loop(0, me.rows // ROWS, first_norm_rows, None)
    late = AllSum(me, r.late, r.late_exp, r.late_blk, (r.les, r.ler, r.lbs, r.lbr))
    late.start()
    advance("rows done")
    late.middle()
    advance("late")

    if not me.paired:
        store_in = pltpu.make_async_copy(sums.total_in(), r.dwin, r.fsem.at[0])
        store_in.start()
    store_out = pltpu.make_async_copy(sums.total_out(), r.dwout, r.fsem.at[1])
    store_out.start()
    advance("last")
    early_total = early.total()
    late_total = late.total()
    r.small[0 : r.sums.shape[0], :] = early_total
    for j in range(tiles):
        cols = slice(j * FF_COLS, (j + 1) * FF_COLS)
        r.small[me.experts + 4 : me.experts + 5, cols] = late_total[j : j + 1, :]
        r.small[me.experts + 5 : me.experts + 6, cols] = late_total[tiles + j : tiles + j + 1, :]
    own_weight = jnp.transpose(jnp.broadcast_to(weights, (weights.shape[0], 128)))[0:1, :]
    mass = early_total[2 + me.experts : 3 + me.experts, 0 : me.experts]
    r.small[me.experts + 3 : me.experts + 4, 0:1] = (
        jnp.sum(own_weight[:, 0 : me.experts] * mass, axis=1, keepdims=True) / me.tokens
    )
    for each in (count_sum, early, late):
        each.sent()
    exchange_sent(me, r.disp, r.back, r.rs, r.rr, me.cap)
    exchange_sent(me, r.ysend, r.yback, r.ys, r.yr, me.cap)
    for j in range(me.nb):
        push_done(me, *da_move(j))
    sums.sent()
    if me.paired:
        for k in range(me.ne):
            dh_move(k).wait_send()
        dg_move.wait_send()
        for part in range(2):
            y_move(part).wait_send()
        lax.fori_loop(0, me.ne, lambda k, _: dn_move(k, slot_rows_of(k)).wait_send(), None)
    stores = [store_in, store_out]
    for piece in pieces:
        piece.end()
    if pieces:
        targets = [(r.shared.at[j], out) for j, out in enumerate((r.gq, r.gk, r.gv, r.go))]
    else:
        targets = [(r.part, r.own_part)]
    for n, (src, dst) in enumerate(targets):
        store = pltpu.make_async_copy(src, dst, r.fsem.at[2 + n])
        store.start()
        stores.append(store)
    for store in stores:
        store.wait()


def in_vmem(count):
    return [pl.BlockSpec(memory_space=pltpu.VMEM)] * count


def anywhere(count):
    return [pl.BlockSpec(memory_space=pl.ANY)] * count


def finish_kernel(experts, *refs):
    small, *narrow = refs[: len(refs) // 2 - 2]
    balance, router, *rest = refs[len(refs) // 2 - 2 :]
    norms, wide = rest[:4], rest[4:]
    for src, dst in zip(narrow, wide, strict=True):
        dst[...] = src[...].astype(dst.dtype)

    @pl.when(pl.program_id(0) == 0)
    def _():
        balance[...] = small[experts + 3 : experts + 4, 0:128]
        router[...] = small[2 : 2 + experts, :]
        for dst, row in zip(norms, (experts + 4, experts + 5, 0, 1), strict=True):
            dst[...] = small[row, :]


def finish(experts, small, narrow, kinds):
    steps = 4
    width = small.shape[1]

    def rows(array):
        return pl.BlockSpec((array.shape[0] // steps, array.shape[1]), lambda n: (n, 0))

    def whole(*shape):
        return pl.BlockSpec(shape, lambda n: (0,) * len(shape))

    small_shapes = [(1, 128), (experts, width)] + 4 * [(width,)]
    return pl.pallas_call(
        functools.partial(finish_kernel, experts),
        grid=(steps,),
        out_shape=[jax.ShapeDtypeStruct(shape, F32) for shape in small_shapes]
        + [jax.ShapeDtypeStruct(a.shape, kind) for a, kind in zip(narrow, kinds)],
        in_specs=[whole(*small.shape)] + [rows(a) for a in narrow],
        out_specs=[whole(*shape) for shape in small_shapes] + [rows(a) for a in narrow],
        compiler_params=pltpu.CompilerParams(vmem_limit_bytes=VMEM_BYTES),
        cost_estimate=pl.CostEstimate(flops=0, bytes_accessed=24 << 20, transcendentals=0),
        name="finish",
    )(small, *narrow)


def shards(
    tokens,
    output_grad,
    expert_index,
    query_weight,
    key_weight,
    value_weight,
    output_weight,
    router_weight,
    expert_in,
    expert_out,
    norm1_gain,
    norm1_bias,
    norm2_gain,
    norm2_bias,
):
    seqs, span, width = tokens.shape
    rows = seqs * span
    nb, ne = lax.axis_size("blk"), lax.axis_size("exp")
    length = span * nb
    experts = router_weight.shape[1]
    ff = expert_in.shape[2]
    cap = -(-max(2, rows * 5 // (4 * experts)) // 16) * 16
    slots = experts * cap
    token_total = rows * nb * ne
    half_width = width // 2
    cfg = dict(
        seqs=seqs, span=span, width=width, rows=rows, nb=nb, ne=ne, length=length,
        experts=experts, ff=ff, cap=cap, half_width=half_width, tokens=token_total,
        mean_load=token_total / experts,
    )
    dma = pltpu.SemaphoreType.DMA
    vmem = pltpu.VMEM
    hi = nb // 2
    size = ff // nb
    sum_rows = -(-(3 + experts) // 8) * 8
    cfg["sum_here"] = width % (8 * nb * ne) == 0
    paired = cfg["paired"] = cfg["sum_here"] and size == width and hi == 2 and slots <= width
    outer = width // min(nb, ne // 2)
    inner = width // (nb * ne // 2)
    inputs = (
        ("idx", expert_index.reshape(1, rows), True),
        ("router", router_weight.T, True),
        ("gain1", norm1_gain, True),
        ("bias1", norm1_bias, True),
        ("gain2", norm2_gain, True),
        ("bias2", norm2_bias, True),
        ("x_hbm", tokens.reshape(rows, width), False),
        ("og_hbm", output_grad.reshape(rows, width), False),
        ("wo_hbm", output_weight, False),
        ("win_hbm", expert_in.reshape(width, ff), False),
        ("wout_hbm", expert_out.reshape(ff, width), False),
        ("wq_hbm", query_weight, False),
        ("wk_hbm", key_weight, False),
        ("wv_hbm", value_weight, False),
    )
    small_rows = -(-(6 + experts) // 8) * 8
    outputs = [
        ("out", (rows, width), BF16, True),
        ("dx", (rows, width), BF16, True),
        ("small", (small_rows, width), F32, True),
        ("dwin", (width, size), BF16, False),
        ("dwout", (size, width), BF16, False),
    ]
    if cfg["sum_here"]:
        outputs += [(n, (width, width), BF16, False) for n in ("gq", "gk", "gv", "go")]
    else:
        outputs.append(("own_part", (4, width, half_width), BF16, False))
    scratch = dict(
        win=vmem((width, ff // 2 if paired else ff), BF16),
        wout=vmem((ff // 2 if paired else ff, width), BF16),
        x=vmem((rows, width), BF16),
        og=vmem((rows, width), BF16),
        o=vmem((rows, width), BF16),
        wo=vmem((width, width), BF16),
        dh=vmem((slots, width), BF16),
        idx_col=vmem((rows, 128), F32),
        cnt=vmem((experts, 128), F32),
        cnt_exp=vmem((ne, experts, 128), F32),
        cnt_blk=vmem((nb, experts, 128), F32),
        q=vmem((length, half_width), BF16),
        k=vmem((length, half_width), BF16),
        v=vmem((length, half_width), BF16),
        a=vmem((length, width), BF16),
        lse=vmem((8, length), F32),
        w=vmem((half_width // PAIR, width, 3 * PAIR), BF16),
        h1=vmem((rows, width), F32),
        gate=vmem((rows, 1), F32),
        mass=vmem((1, experts), F32),
        mail=vmem((rows, width), BF16),
        disp=vmem((slots, width), BF16),
        took=vmem((slots, width), BF16),
        g=vmem((hi, slots, width) if paired else (slots, width), BF16),
        du=vmem((hi, slots, width) if paired else (slots, width), BF16),
        yf=vmem((max(slots, size), width), F32),
        made=vmem((length, width), F32),
        back=vmem((slots, width), BF16),
        dh1=vmem((rows, width), F32),
        do=vmem((length, half_width), BF16),
        ogot=vmem((width, half_width), BF16),
        dk_sum=vmem((length, PAIR), F32),
        dv_sum=vmem((length, PAIR), F32),
        dqkv=vmem((length, 3 * PAIR), BF16),
        sums=vmem((sum_rows, width), F32),
        sum_exp=vmem((ne, sum_rows, width), F32),
        sum_blk=vmem((nb, sum_rows, width), F32),
        late=vmem((8, FF_COLS), F32),
        late_exp=vmem((ne, 8, FF_COLS), F32),
        late_blk=vmem((nb, 8, FF_COLS), F32),
        part=vmem((4, width, half_width), BF16),
        lsem=dma((5 + 2 * hi + 3 * (half_width // PAIR),)),
        fsem=dma((6,)),
        xs=dma((2 * seqs,)), xr=dma((nb,)),
        fws=dma((nb,)), fwr=dma((nb,)),
        os=dma((nb,)), osr=dma((2 * seqs,)),
        ds=dma((ne,)), dr=dma((ne,)),
        ces=dma((ne,)), cer=dma((ne,)), cbs=dma((nb,)), cbr=dma((nb,)),
        ns=dma((ne,)), nr=dma((ne,)),
        rs=dma((ne,)), rr=dma((ne,)),
        ys=dma((ne,)), yr=dma((ne,)),
        dos=dma((2 * seqs,)), dor=dma((nb,)),
        ows=dma, owr=dma,
        ss=dma, sr=dma,
        fs=dma((nb,)), fr=dma((2 * seqs,)),
        es=dma((ne,)), er=dma((ne,)), bs=dma((nb,)), br=dma((nb,)),
        les=dma((ne,)), ler=dma((ne,)), lbs=dma((nb,)), lbr=dma((nb,)),
    )
    if cfg["sum_here"]:
        scratch.update(
            shared=vmem((4, width, width), BF16),
            got1=vmem((4, max(nb, ne // 2), outer, half_width), BF16),
            got2=vmem((4, max(nb, ne // 2), inner, half_width), BF16),
            s5=dma((4,)),
            r5=dma((4,)),
        )
        for n in range(1, 5):
            scratch[f"s{n}"] = dma((4, max(nb, ne // 2)))
            scratch[f"r{n}"] = dma((4, max(nb, ne // 2)))
    if paired:
        scratch.update(
            {n: vmem((slots, width), BF16) for n in ("took2", "dh2", "dy", "dy2", "dn2", "dn_got", "y2", "y_got")},
            **{n: vmem((slots, 1), F32) for n in ("value", "dgate", "dgate2")},
            dg_send=vmem((8, slots), F32),
            dg_got=vmem((8, slots), F32),
            in_got=vmem((hi - 1, width, size), BF16),
            out_got=vmem((hi - 1, size, width), BF16),
            ins=dma((hi - 1,)), inr=dma((hi - 1,)),
            outs=dma((hi - 1,)), outr=dma((hi - 1,)),
            t2s=dma((ne,)), t2r=dma((ne,)),
            g2s=dma((ne,)), g2r=dma((ne,)),
            d2s=dma((ne,)), d2r=dma((ne,)),
            **{n: dma for n in ("dgs", "dgr")},
            y2s=dma((2,)), y2r=dma((2,)),
        )
    else:
        scratch.update(
            in1=vmem((hi, width, size), BF16),
            in2=vmem((hi - 1, width, size), BF16),
            out1=vmem((hi - 1, 2, size, width), BF16),
            out2=vmem((size, width), BF16),
            in1s=dma((hi,)), in1r=dma((hi,)),
            in2s=dma((hi - 1,)), in2r=dma((hi - 1,)),
            out1s=dma((hi - 1, 2)), out1r=dma((hi - 1, 2)),
            out2s=dma, out2r=dma,
        )
    names = [n for n, _, _ in inputs] + [n for n, _, _, _ in outputs] + list(scratch)
    out, dx, small, dwin, dwout, *wide = pl.pallas_call(
        functools.partial(layer_kernel, cfg, names),
        out_shape=[jax.ShapeDtypeStruct(shape, kind) for _, shape, kind, _ in outputs],
        in_specs=[(in_vmem if near else anywhere)(1)[0] for _, _, near in inputs],
        out_specs=[(in_vmem if near else anywhere)(1)[0] for _, _, _, near in outputs],
        scratch_shapes=list(scratch.values()),
        compiler_params=pltpu.CompilerParams(
            collective_id=1, has_side_effects=True, vmem_limit_bytes=VMEM_BYTES
        ),
        cost_estimate=pl.CostEstimate(
            flops=30 << 30, bytes_accessed=1 << 25, transcendentals=1 << 23
        ),
        name="layer",
    )(*[value for _, value, _ in inputs])
    if not cfg["sum_here"]:
        own = wide[0]
        own = jnp.concatenate(
            [
                own[:3].reshape(3, width, 3, PAIR).transpose(2, 1, 0, 3).reshape(3, width, half_width),
                own[3:],
            ]
        )
        core, empty = lax.rem(lax.axis_index("exp"), 2), jnp.zeros_like(own)
        wide = lax.psum(
            jnp.concatenate(
                [jnp.where(core == 0, own, empty), jnp.where(core == 0, empty, own)], axis=2
            ),
            ("blk", "exp"),
        )
    arrays = [out, dx, dwin, dwout, *[wide[n] for n in range(4)]]
    balance, router, gain1, bias1, gain2, bias2, out, dx, dwin, dwout, *wide = finish(
        experts, small, arrays, [BF16, BF16] + [F32] * 6
    )
    return (
        out.reshape(seqs, span, width),
        balance[0, 0],
        dx.reshape(seqs, span, width),
        *wide,
        router.T,
        dwin[None],
        dwout[None],
        gain1,
        bias1,
        gain2,
        bias2,
    )


def solution(mesh):
    return jax.shard_map(
        shards,
        mesh=mesh,
        in_specs=(
            P("exp", "blk", None),
            P("exp", "blk", None),
            P("blk", "exp", None, None),
            P(),
            P(),
            P(),
            P(),
            P(),
            P("exp", None, None),
            P("exp", None, None),
            P(),
            P(),
            P(),
            P(),
        ),
        out_specs=(
            P("exp", "blk", None),
            P(),
            P("exp", "blk", None),
            P(),
            P(),
            P(),
            P(),
            P(),
            P("exp", None, "blk"),
            P("exp", "blk", None),
            P(),
            P(),
            P(),
            P(),
        ),
        check_vma=False,
    )
```
